256 devices in a mesh: ja: 16 (over y_hi, x, core), aa: 16 (over y_lo, z).
Axes of the slice: x: 4, y: 4 (y_hi: 2, y_lo: 2; y = y_hi * 2 + y_lo), z: 8, core: 2. Of those that a mesh axis runs over, the one named last changes fastest.
Arguments:
- amplitudes: float32 [2, 64, 1024, 1024], P(None, 'ja', 'aa'), may hold values from -6 to 6
- chol: float32 [2, 1024, 1024], P(None, 'ja'), as said below
- irrep_i: int32 [2], replicated, may hold values from 0 to 7
- irrep_j: int32 [64], replicated, may hold values from 0 to 7
- irrep_v: int32 [1024], replicated, may hold values from 0 to 7
- irrep_l: int32 [2], replicated, may hold values from 0 to 7
Outputs:
- ladder: float32 [2, 64, 1024, 1024], P(None, 'ja', 'aa')
The draws below stay inside these ranges and needn't reach their ends.
Inputs may be any that keep to these rules, and one draw needn't show every extreme that they name: chol[l] is symmetric in its last two indices.
All inputs are finite; a program needn't handle non-finite values.
Results may differ from the reference program's by a relative error of at most 0.0003.
Values sent between devices are 32-bit elements; how exact they have to be, the bound alone decides.
No kernel may reach another device: no remote copies, remote signals or barrier semaphores. Data moves between devices by JAX's collectives and lax.ppermute only.
A program may use at most 128 MiB of HBM per device.

```python
import math
import jax
import jax.numpy as jnp
from jax import lax

V = 1024
J = 64
I = 2
NL = 2


def draw_chol(key, part):
    key = jax.random.fold_in(key, 11)
    base = jax.random.normal(key, (NL, V, V), jnp.float32)
    factor = (16.0 / (NL * V * V)) ** 0.25
    return ((base + jnp.swapaxes(base, 1, 2)) * (factor / math.sqrt(2.0))).astype(jnp.float32)


def draw_irrep_v(key, part):
    key = jax.random.fold_in(key, 23)
    key_main, key_pick, key_rest = jax.random.split(key, 3)
    dominant = jax.random.randint(key_main, (), 0, 8, jnp.int32)
    pick = jax.random.randint(key_pick, (V,), 0, 8, jnp.int32)
    others = jax.random.randint(key_rest, (V,), 0, 8, jnp.int32)
    return jnp.where(pick < 7, dominant, others).astype(jnp.int32)


def set_ends(result, key, smallest, high):
    longest = result.shape.index(max(result.shape))
    spots = []
    for shift in (0, 1):
        where = [jax.random.randint(jax.random.fold_in(key, axis), (), 0, length) for axis, length in enumerate(result.shape)]
        where[longest] = (where[longest] + shift) % result.shape[longest]
        spots.append(tuple(where))
    return result.at[spots[0]].set(smallest).at[spots[1]].set(high)


def block_scale(rng, extent, shards, low, top_value):
    level = 1.0
    for dim, blocks in shards:
        steps = jax.random.uniform(jax.random.fold_in(jax.random.fold_in(rng, 6), dim), (blocks,), jnp.float32, low / len(shards), top_value / len(shards))
        level = level * jnp.repeat(jnp.exp(steps), extent[dim] // blocks).reshape((-1,) + (1,) * (len(extent) - 1 - dim))
    return level


def normal_values(rng, dims, width, most, cuts=(), kind=jnp.bfloat16):
    array = jax.random.normal(rng, dims, jnp.float32) * width
    if len(cuts) > 0:
        array = block_scale(rng, dims, cuts, -0.22, 0.18) * array
    return jnp.clip(array, min=-most, max=most).astype(kind)


def setup_inputs(seed: int = 0) -> dict:
    streams_of = jax.random.split(jax.random.key(seed), 7)
    amplitudes = normal_values(streams_of[0], (I, J, V, V), 1.0, 6.0, ((1, 16), (2, 16)), jnp.float32)
    chol = draw_chol(jax.random.fold_in(streams_of[6], 71), 0)
    irrep_i = jax.random.randint(streams_of[2], (I,), 0, 8).astype(jnp.int32)
    irrep_j = set_ends(jax.random.randint(streams_of[3], (J,), 0, 8), jax.random.fold_in(streams_of[3], 1), 0, 7).astype(jnp.int32)
    irrep_v = draw_irrep_v(jax.random.fold_in(streams_of[6], 71), 0)
    irrep_l = jax.random.randint(streams_of[5], (NL,), 0, 8).astype(jnp.int32)
    return dict(amplitudes=amplitudes, chol=chol, irrep_i=irrep_i, irrep_j=irrep_j, irrep_v=irrep_v, irrep_l=irrep_l)


def reference(amplitudes, chol, irrep_i, irrep_j, irrep_v, irrep_l):
    pair_virt = jnp.bitwise_xor(irrep_v[:, None], irrep_v[None, :])
    panel_keep = pair_virt[None, :, :] == irrep_l[:, None, None]
    panel = jnp.where(panel_keep, chol, jnp.zeros_like(chol))

    def one_slab(item):
        amp_slab, label = item
        pair_occ = jnp.bitwise_xor(label, irrep_j)
        keep_mask = pair_occ[:, None, None] == pair_virt[None, :, :]
        masked = jnp.where(keep_mask, amp_slab, jnp.zeros_like(amp_slab))
        total = jnp.zeros(amp_slab.shape, jnp.float32)
        for vector in range(NL):
            half = jnp.einsum('jcd,bd->jcb', masked, panel[vector], precision=lax.Precision.HIGHEST)
            total = total + jnp.einsum('ac,jcb->jba', panel[vector], half, precision=lax.Precision.HIGHEST)
        return total

    return lax.map(one_slab, (amplitudes, irrep_i))
```

```python
import jax
import jax.numpy as jnp
from jax import lax
from jax.experimental import pallas as pl
from jax.experimental.pallas import tpu as pltpu
from jax.sharding import PartitionSpec as P

F32, BF16, I32 = jnp.float32, jnp.bfloat16, jnp.int32
NN = (((1,), (0,)), ((), ()))
NT = (((1,), (1,)), ((), ()))
SLOTS = 32
RANKS = 16
CLS, NUM, SLOT, SPOT, LAB, RANK, FLAG, BITS = range(8)


def iota(shape, dim):
    return lax.broadcasted_iota(I32, shape, dim)


def parity(x):
    return (x ^ (x >> 1) ^ (x >> 2)) & 1


def one(cond):
    return jnp.where(cond, 1.0, 0.0).astype(F32)


def dot(a, b, dims=NN):
    return lax.dot_general(a, b, dims, preferred_element_type=F32)


def split(x):
    high = x.astype(BF16)
    return high, (x - high.astype(F32)).astype(BF16)


def dot3(a, b, dims=NN):
    (ah, al), (bh, bl) = a, b
    return dot(ah, bh, dims) + dot(ah, bl, dims) + dot(al, bh, dims)


def dot2(a, b, dims=NN):
    return dot(a, b[0], dims) + dot(a, b[1], dims)


def table_kernel(irrep_ref, l_ref, row_ref, col_ref):
    cls = irrep_ref[...]
    width = cls.shape[1]
    chunks = width // 128
    onehot = one(cls == iota((16, width), 0))
    before = one(iota((128, 128), 0) < iota((128, 128), 1))
    count = jnp.zeros((16, 1), F32)
    blocks = jnp.zeros((16, 128), F32)
    slots = []
    for k in range(chunks):
        part = onehot[:, 128 * k : 128 * k + 128]
        ahead = dot(part.astype(BF16), before.astype(BF16)) + count
        slots.append(jnp.sum(part * ahead, axis=0, keepdims=True))
        count = count + jnp.sum(part, axis=1, keepdims=True)
        place = one(iota((128, 128), 1) == 2 * k + (iota((128, 128), 0) >> 6))
        blocks = blocks + dot(part.astype(BF16), place.astype(BF16))
    slot = jnp.concatenate(slots, axis=1).astype(I32)
    lane = iota((16, 128), 1)
    cand = iota((16, 128), 0)
    count_lane = jnp.sum(jnp.where(lane == cand, count, 0.0), axis=0, keepdims=True)
    member = (parity((cand >> 1) & lane) == (cand & 1)) & (lane < 8)
    largest = jnp.max(jnp.where(member, count_lane, 0.0), axis=1, keepdims=True)
    in_block = jnp.zeros((16, 128), F32)
    for g in range(8):
        in_block = in_block + jnp.where(parity((cand >> 1) & g) == (cand & 1), blocks[g : g + 1, :], 0.0)
    fullest = jnp.max(in_block, axis=1, keepdims=True)
    bits_col = cand[:, 0:1] >> 1
    good = (largest <= SLOTS) & (fullest <= RANKS)
    for n in range(l_ref.shape[0]):
        good = good & (parity(bits_col & l_ref[n]) == 1)
    pick = jnp.min(jnp.where(good, cand[:, 0:1].astype(F32), 99.0), axis=0, keepdims=True).astype(I32)
    bits, side = pick >> 1, pick & 1
    small = parity(bits & cls) == side
    group = jnp.zeros_like(cls)
    label = jnp.zeros_like(cls)
    lane_group = iota((1, width), 1) >> 5
    number = jnp.zeros((1, 1), I32)
    for g in range(8):
        is_small = parity(bits & g) == side
        group = group + jnp.where(is_small & (cls > g), 1, 0)
        label = label + jnp.where(is_small & (number == lane_group), g, 0)
        number = number + jnp.where(is_small, 1, 0)
    inner = one((iota((128, 128), 0) < iota((128, 128), 1)) & ((iota((128, 128), 0) >> 6) == (iota((128, 128), 1) >> 6)))
    small16 = jnp.broadcast_to(one(small), (16, width))
    ranks = [
        dot(small16[:, 128 * k : 128 * k + 128].astype(BF16), inner.astype(BF16))[0:1, :] for k in range(chunks)
    ]
    rank = jnp.concatenate(ranks, axis=1).astype(I32)
    none = jnp.full_like(cls, -1)
    table = jnp.concatenate(
        [
            cls,
            jnp.where(small, group * SLOTS + slot, none),
            jnp.where(small, slot, none),
            jnp.where(small, (iota((1, width), 1) >> 6) * RANKS + rank, none),
            label,
            jnp.where(small, rank, none),
            jnp.broadcast_to(jnp.where(pick < 99, 1, 0), cls.shape),
            jnp.broadcast_to(bits, cls.shape),
        ],
        axis=0,
    )
    row_ref[...] = table
    table = table.astype(F32)
    for k in range(chunks):
        tile = jnp.concatenate([table[:, 128 * k : 128 * k + 128], jnp.zeros((120, 128), F32)], axis=0)
        col_ref[128 * k : 128 * k + 128, :] = jnp.transpose(tile).astype(I32)


def own(col_ref, block, field):
    return col_ref[pl.ds(pl.multiple_of(block * 64, 64), 64), field : field + 1]


def panel_kernel(row_ref, col_ref, chol_ref, l_ref, pos_ref, out_ref):
    cls = row_ref[CLS : CLS + 1, :]
    slot = row_ref[SLOT : SLOT + 1, :]
    own_cls = own(col_ref, pos_ref[0], CLS)
    pick = one(slot == iota((SLOTS, slot.shape[1]), 0)).astype(BF16)
    parts = []
    for n in range(2):
        kept = jnp.where((own_cls ^ cls) == l_ref[n], chol_ref[n], 0.0)
        high, low = split(kept)
        parts.append(dot(high, pick, NT) + dot(low, pick, NT))
    both = jnp.concatenate(parts, axis=1)
    packed = jnp.concatenate([both[0:32], both[32:64]], axis=1)
    out_ref[...] = jnp.broadcast_to(packed[None], out_ref.shape)


def unpack(gathered):
    n = gathered.shape[0]
    return jnp.concatenate([gathered, jnp.roll(gathered, 64, axis=2)], axis=1).reshape(n * 64, 128)


def places(row_ref):
    spot = row_ref[SPOT : SPOT + 1, :]
    number = row_ref[NUM : NUM + 1, :]
    width = spot.shape[1]
    spots = one(spot == iota((16 * RANKS, width), 0)).astype(BF16)
    numbers = one(number == iota((4 * SLOTS, width), 0)).astype(BF16)
    return spots, numbers


def half_kernel(row_ref, col_ref, amp_ref, got_ref, i_ref, j_ref, l_ref, pos_ref, out_ref, high_ref, low_ref):
    p, q = pos_ref[0], pos_ref[1]
    cls = row_ref[CLS : CLS + 1, :]
    label = row_ref[LAB : LAB + 1, 0:128]
    own_cls = own(col_ref, q, CLS)
    own_small = own(col_ref, q, NUM) >= 0
    own_rank = own(col_ref, q, RANK)
    xs = [i_ref[n // 4] ^ j_ref[p * 4 + n % 4] for n in range(8)]
    for n in range(8):
        kept = jnp.where((own_cls ^ cls) == xs[n], amp_ref[n // 4, n % 4], 0.0)
        high_ref[64 * n : 64 * n + 64, :], low_ref[64 * n : 64 * n + 64, :] = split(kept)
    panel = unpack(got_ref[...])
    lane = iota(panel.shape, 1)
    slot = col_ref[:, SLOT : SLOT + 1]
    weights = jnp.where(lane < 64, panel, one(slot == lane - 64))
    wh, wl = split(weights)
    first = dot(high_ref[...], jnp.concatenate([wh, wl], axis=1))
    half = first[:, 0:128] + first[:, 128:256] + dot(low_ref[...], wh)
    parts = [half[64 * n : 64 * n + 64] for n in range(8)]
    firsts = [part[:, 64:96] + jnp.where(own_small, part[:, 0:32], 0.0) for part in parts]
    own_panel = unpack(got_ref[pl.ds(q, 1)])
    stacked = jnp.concatenate([own_panel[:, 0:32], own_panel[:, 32:64]], axis=0)
    ranks = jnp.concatenate([jnp.full_like(own_rank, -1), own_rank], axis=0)
    lane = iota((128, 128), 1)
    left = jnp.where(lane < 32, jnp.concatenate([stacked] * 4, axis=1), one(ranks == lane - 32))
    left = jnp.where(lane < 48, left, 0.0)
    left = jnp.transpose(left)
    pair_cls = jnp.concatenate([own_cls ^ l_ref[0], own_cls ^ l_ref[1]], axis=0)
    both = [jnp.concatenate([part[:, 0:32], part[:, 32:64]], axis=0) for part in parts]
    spread = [
        jnp.where(label == (pair_cls ^ xs[n]), jnp.concatenate([both[n]] * 4, axis=1), 0.0) for n in range(8)
    ]
    sums = dot3(split(left[0:32]), split(jnp.concatenate(spread, axis=1)))
    seconds = dot2(left[32:48].astype(BF16), split(jnp.concatenate(both, axis=1)))
    spots, numbers = places(row_ref)
    order = dot(spots, numbers, NT).astype(BF16)
    for i in range(2):
        rows = jnp.concatenate([sums[:, 128 * n : 128 * n + 128] for n in range(4 * i, 4 * i + 4)], axis=0)
        by_spot = dot2(order, split(rows), NT).reshape(16, RANKS, 128)
        out_ref[:, i, 64 : 64 + RANKS, :] = by_spot + seconds[None, :, 128 * i : 128 * i + 128]
        out_ref[:, i, 0:64, :] = jnp.broadcast_to(
            jnp.concatenate(firsts[4 * i : 4 * i + 4], axis=1)[None], (16, 64, 128)
        )


def ladder_kernel(row_ref, col_ref, got_ref, mid_ref, i_ref, j_ref, l_ref, pos_ref, out_ref):
    p, q = pos_ref[0], pos_ref[1]
    cls = row_ref[CLS : CLS + 1, :]
    number = row_ref[NUM : NUM + 1, :]
    label = row_ref[LAB : LAB + 1, 0:128]
    bits = row_ref[BITS : BITS + 1, 0:1]
    label_col = col_ref[0:128, LAB : LAB + 1]
    width = cls.shape[1]
    turned = jnp.transpose(unpack(got_ref[...]))
    full = [
        jnp.where(label_col == (cls ^ l_ref[n]), jnp.concatenate([turned[32 * n : 32 * n + 32]] * 4, axis=0), 0.0)
        for n in range(2)
    ]
    full = split(jnp.concatenate(full + [one(number == iota((128, width), 0))], axis=0))
    mids = [mid_ref[:, i, 0:64, :].reshape(width, 128) for i in range(2)]
    core = dot3(full, split(jnp.concatenate(mids, axis=1)))
    spots, numbers = places(row_ref)
    order = dot(numbers, spots, NT).astype(BF16)
    own_panel = unpack(got_ref[pl.ds(q, 1)])
    own_slot = own(col_ref, q, SLOT)
    own_rank = own(col_ref, q, RANK)
    own_cls = jnp.concatenate([own(col_ref, q, CLS)] * 4, axis=0)
    lane = iota((64, 128), 1)
    first_tile = jnp.concatenate([own_panel[:, 0:32]] * 4, axis=1)
    second_tile = jnp.concatenate([own_panel[:, 32:64]] * 4, axis=1)
    slot_tile = one(own_slot == (lane & 31))
    rank_pick = one(own_rank == lane).astype(BF16)
    lane_row = iota((1, 128), 1) >> 5
    results = []
    for i in range(2):
        xs = [i_ref[i] ^ j_ref[p * 4 + j] for j in range(4)]
        x_lane = jnp.zeros((1, 128), I32)
        x_row = jnp.zeros((256, 1), I32)
        for j in range(4):
            x_lane = jnp.where(lane_row == j, xs[j], x_lane)
            x_row = jnp.where((iota((256, 1), 0) >> 6) == j, xs[j], x_row)
        odd_lane = parity(x_lane & bits) == 1
        odd = [parity(bits & xs[j]) == 1 for j in range(4)]

        def blocks(tiles):
            return split(
                jnp.concatenate([jnp.where((lane >> 5) == j, tiles[j], 0.0) for j in range(4)], axis=0)
            )

        late = mid_ref[:, i, 64 : 64 + RANKS, :]
        total = jnp.where(odd_lane, 0.0, jnp.sum(late, axis=0))
        late = jnp.where(odd_lane, late.reshape(16 * RANKS, 128), 0.0)
        lanes = slice(128 * i, 128 * i + 128)
        pick = core[256:384, lanes]
        pick2 = jnp.where(odd_lane, dot2(order, split(late)), pick)
        t1 = dot3(blocks([jnp.where(odd[j], slot_tile, first_tile) for j in range(4)]), split(pick), NT)
        t2 = dot3(blocks([jnp.where(odd[j], slot_tile, second_tile) for j in range(4)]), split(pick2), NT)
        t3 = dot3(blocks([first_tile] * 4), split(core[0:128, lanes]), NT)
        t3 = t3 + dot3(blocks([second_tile] * 4), split(core[128:256, lanes]), NT)
        total = jnp.concatenate([total, jnp.zeros((128 - RANKS, 128), F32)], axis=0)
        total = dot2(rank_pick, split(total))
        spread = [jnp.concatenate([total[:, 32 * j : 32 * j + 32]] * 4, axis=1) for j in range(4)]
        t3 = t3 + jnp.concatenate(spread, axis=0)
        goal = own_cls ^ x_row
        t1 = jnp.where(label == (goal ^ l_ref[0]), t1, 0.0)
        t2 = jnp.where(label == (goal ^ l_ref[1]), t2, 0.0)
        t3 = jnp.where(label == goal, t3, 0.0)
        results.append(jnp.concatenate([t1, t2, t3], axis=1))
    result = dot3(split(jnp.concatenate(results, axis=0)), full)
    for n in range(8):
        out_ref[n // 4, n % 4] = result[64 * n : 64 * n + 64]


VMEM = pl.BlockSpec(memory_space=pltpu.VMEM)
SMEM = pl.BlockSpec(memory_space=pltpu.SMEM)
PARAMS = pltpu.CompilerParams(vmem_limit_bytes=48 * 1024 * 1024)


def shape(*dims, dtype=F32):
    return jax.ShapeDtypeStruct(dims, dtype)


def compact(row, col, amplitudes, chol, irrep_i, irrep_j, irrep_l, pos):
    panel = pl.pallas_call(
        panel_kernel,
        out_shape=shape(16, 32, 128),
        in_specs=[VMEM, VMEM, VMEM, SMEM, SMEM],
        out_specs=VMEM,
        compiler_params=PARAMS,
        name="panel_slots",
    )(row, col, chol, irrep_l, pos)
    panel = lax.all_to_all(panel, "ja", split_axis=0, concat_axis=0, tiled=True)
    mid = pl.pallas_call(
        half_kernel,
        out_shape=shape(16, 2, 64 + RANKS, 128),
        in_specs=[VMEM] * 4 + [SMEM] * 4,
        out_specs=VMEM,
        scratch_shapes=[pltpu.VMEM((512, 1024), BF16), pltpu.VMEM((512, 1024), BF16)],
        compiler_params=PARAMS,
        name="half_slots",
    )(row, col, amplitudes, panel, irrep_i, irrep_j, irrep_l, pos)
    mid = lax.all_to_all(mid, "aa", split_axis=0, concat_axis=0, tiled=True)
    return pl.pallas_call(
        ladder_kernel,
        out_shape=shape(*amplitudes.shape),
        in_specs=[VMEM] * 4 + [SMEM] * 4,
        out_specs=VMEM,
        compiler_params=PARAMS,
        name="ladder_slots",
    )(row, col, panel, mid, irrep_i, irrep_j, irrep_l, pos)


def dense_half_kernel(row_ref, col_ref, amp_ref, panel_ref, i_ref, j_ref, pos_ref, out_ref, high_ref, low_ref):
    p, q = pos_ref[0], pos_ref[1]

    @pl.when(pl.program_id(0) == 0)
    def _():
        cls = row_ref[CLS : CLS + 1, :]
        own_cls = own(col_ref, q, CLS)
        for n in range(8):
            kept = jnp.where((own_cls ^ cls) == (i_ref[n // 4] ^ j_ref[p * 4 + n % 4]), amp_ref[n // 4, n % 4], 0.0)
            high_ref[64 * n : 64 * n + 64, :], low_ref[64 * n : 64 * n + 64, :] = split(kept)

    block = panel_ref[...]
    left = split(block.reshape(block.shape[0] * block.shape[1], block.shape[2]))
    result = dot3(left, (high_ref[...], low_ref[...]), NT)
    for k in range(out_ref.shape[0]):
        for n in range(2):
            rows = block.shape[1] * n + 64 * k
            out_ref[k, 64 * n : 64 * n + 64, :] = result[rows : rows + 64]


def dense_ladder_kernel(mid_ref, panel_ref, out_ref, high_ref, low_ref):
    k = pl.program_id(0)

    @pl.when(k == 0)
    def _():
        out_ref[...] = jnp.zeros_like(out_ref)

    block = mid_ref[...]
    pieces = []
    for n in range(8):
        sources = []
        for s in range(0, block.shape[0], 2):
            tile = 128 * (n // 2)
            a, b = block[s, :, tile : tile + 128], block[s + 1, :, tile : tile + 128]
            turn = iota((64, 128), 1) < 64
            if n % 2 == 0:
                both = jnp.where(iota((128, 128), 1) < 64, a, jnp.roll(b, 64, axis=1))
            else:
                both = jnp.where(iota((128, 128), 1) < 64, jnp.roll(a, 64, axis=1), b)
            sources.append(both)
        pieces.append(jnp.concatenate(sources, axis=1))
    for l in range(2):
        left = jnp.concatenate([piece[64 * l : 64 * l + 64] for piece in pieces], axis=0)
        result = dot3(split(left), split(panel_ref[l]))
        for n in range(8):
            out_ref[n // 4, n % 4] += result[64 * n : 64 * n + 64]


def dense(row, col, amplitudes, chol, irrep_i, irrep_j, irrep_v, irrep_l, pos):
    height = chol.shape[1]
    own_rows = lax.dynamic_slice_in_dim(irrep_v, pos[0] * height, height)
    keep = (own_rows[:, None] ^ irrep_v[None, :])[None] == irrep_l[:, None, None]
    panel = lax.all_gather(jnp.where(keep, chol, 0.0), "ja", axis=1, tiled=True)
    steps = 4
    whole = pl.BlockSpec(amplitudes.shape, lambda k: (0, 0, 0, 0))
    mid = pl.pallas_call(
        dense_half_kernel,
        out_shape=shape(16, 128, 512),
        grid=(steps,),
        in_specs=[
            pl.BlockSpec(row.shape, lambda k: (0, 0)),
            pl.BlockSpec(col.shape, lambda k: (0, 0)),
            whole,
            pl.BlockSpec((2, 1024 // steps, 1024), lambda k: (0, k, 0)),
            SMEM,
            SMEM,
            SMEM,
        ],
        out_specs=pl.BlockSpec((16 // steps, 128, 512), lambda k: (k, 0, 0)),
        scratch_shapes=[pltpu.VMEM((512, 1024), BF16), pltpu.VMEM((512, 1024), BF16)],
        compiler_params=PARAMS,
        name="half_dense",
    )(row, col, amplitudes, panel, irrep_i, irrep_j, pos)
    mid = lax.all_to_all(mid, "aa", split_axis=0, concat_axis=0, tiled=True)
    return pl.pallas_call(
        dense_ladder_kernel,
        out_shape=shape(*amplitudes.shape),
        grid=(steps,),
        in_specs=[
            pl.BlockSpec((16 // steps, 128, 512), lambda k: (k, 0, 0)),
            pl.BlockSpec((2, 1024 // steps, 1024), lambda k: (0, k, 0)),
        ],
        out_specs=whole,
        scratch_shapes=[pltpu.VMEM((512, 1024), BF16), pltpu.VMEM((512, 1024), BF16)],
        compiler_params=PARAMS,
        name="ladder_dense",
    )(mid, panel)


def local(amplitudes, chol, irrep_i, irrep_j, irrep_v, irrep_l):
    pos = jnp.stack([lax.axis_index("ja"), lax.axis_index("aa")]).astype(I32)
    width = irrep_v.shape[0]
    row, col = pl.pallas_call(
        table_kernel,
        out_shape=(shape(8, width, dtype=I32), shape(width, 128, dtype=I32)),
        in_specs=[VMEM, SMEM],
        out_specs=(VMEM, VMEM),
        compiler_params=PARAMS,
        name="orbital_table",
    )(irrep_v.reshape(1, width), irrep_l)
    return lax.cond(
        row[FLAG, 0] == 1,
        lambda: compact(row, col, amplitudes, chol, irrep_i, irrep_j, irrep_l, pos),
        lambda: dense(row, col, amplitudes, chol, irrep_i, irrep_j, irrep_v, irrep_l, pos),
    )


def solution(mesh):
    in_specs = (P(None, "ja", "aa", None), P(None, "ja", None), P(), P(), P(), P())
    out_specs = P(None, "ja", "aa", None)
    return jax.shard_map(local, mesh=mesh, in_specs=in_specs, out_specs=out_specs, check_vma=False)
```

```python
import jax
import jax.numpy as jnp
from jax import lax
from jax.experimental import pallas as pl
from jax.experimental.pallas import tpu as pltpu
from jax.sharding import PartitionSpec as P

F32, BF16, I32 = jnp.float32, jnp.bfloat16, jnp.int32
NN = (((1,), (0,)), ((), ()))
NT = (((1,), (1,)), ((), ()))
SLOTS = 32
RANKS = 16
CLS, NUM, SLOT, SPOT, LAB, RANK, FLAG, BITS = range(8)


def iota(shape, dim):
    return lax.broadcasted_iota(I32, shape, dim)


def parity(x):
    return (x ^ (x >> 1) ^ (x >> 2)) & 1


def one(cond):
    return jnp.where(cond, 1.0, 0.0).astype(F32)


def dot(a, b, dims=NN):
    return lax.dot_general(a, b, dims, preferred_element_type=F32)


def split(x):
    high = x.astype(BF16)
    return high, (x - high.astype(F32)).astype(BF16)


def dot3(a, b, dims=NN):
    (ah, al), (bh, bl) = a, b
    return dot(ah, bh, dims) + dot(ah, bl, dims) + dot(al, bh, dims)


def dot2(a, b, dims=NN):
    return dot(a, b[0], dims) + dot(a, b[1], dims)


def table_kernel(irrep_ref, l_ref, row_ref, col_ref):
    cls = irrep_ref[...]
    width = cls.shape[1]
    chunks = width // 128
    onehot = one(cls == iota((16, width), 0))
    before = one(iota((128, 128), 0) < iota((128, 128), 1))
    count = jnp.zeros((16, 1), F32)
    blocks = jnp.zeros((16, 128), F32)
    slots = []
    for k in range(chunks):
        part = onehot[:, 128 * k : 128 * k + 128]
        ahead = dot(part.astype(BF16), before.astype(BF16)) + count
        slots.append(jnp.sum(part * ahead, axis=0, keepdims=True))
        count = count + jnp.sum(part, axis=1, keepdims=True)
        place = one(iota((128, 128), 1) == 2 * k + (iota((128, 128), 0) >> 6))
        blocks = blocks + dot(part.astype(BF16), place.astype(BF16))
    slot = jnp.concatenate(slots, axis=1).astype(I32)
    lane = iota((16, 128), 1)
    cand = iota((16, 128), 0)
    count_lane = jnp.sum(jnp.where(lane == cand, count, 0.0), axis=0, keepdims=True)
    member = (parity((cand >> 1) & lane) == (cand & 1)) & (lane < 8)
    largest = jnp.max(jnp.where(member, count_lane, 0.0), axis=1, keepdims=True)
    in_block = jnp.zeros((16, 128), F32)
    for g in range(8):
        in_block = in_block + jnp.where(parity((cand >> 1) & g) == (cand & 1), blocks[g : g + 1, :], 0.0)
    fullest = jnp.max(in_block, axis=1, keepdims=True)
    bits_col = cand[:, 0:1] >> 1
    good = (largest <= SLOTS) & (fullest <= RANKS)
    for n in range(l_ref.shape[0]):
        good = good & (parity(bits_col & l_ref[n]) == 1)
    pick = jnp.min(jnp.where(good, cand[:, 0:1].astype(F32), 99.0), axis=0, keepdims=True).astype(I32)
    bits, side = pick >> 1, pick & 1
    small = parity(bits & cls) == side
    group = jnp.zeros_like(cls)
    label = jnp.zeros_like(cls)
    lane_group = iota((1, width), 1) >> 5
    number = jnp.zeros((1, 1), I32)
    for g in range(8):
        is_small = parity(bits & g) == side
        group = group + jnp.where(is_small & (cls > g), 1, 0)
        label = label + jnp.where(is_small & (number == lane_group), g, 0)
        number = number + jnp.where(is_small, 1, 0)
    inner = one((iota((128, 128), 0) < iota((128, 128), 1)) & ((iota((128, 128), 0) >> 6) == (iota((128, 128), 1) >> 6)))
    small16 = jnp.broadcast_to(one(small), (16, width))
    ranks = [
        dot(small16[:, 128 * k : 128 * k + 128].astype(BF16), inner.astype(BF16))[0:1, :] for k in range(chunks)
    ]
    rank = jnp.concatenate(ranks, axis=1).astype(I32)
    none = jnp.full_like(cls, -1)
    table = jnp.concatenate(
        [
            cls,
            jnp.where(small, group * SLOTS + slot, none),
            jnp.where(small, slot, none),
            jnp.where(small, (iota((1, width), 1) >> 6) * RANKS + rank, none),
            label,
            jnp.where(small, rank, none),
            jnp.broadcast_to(jnp.where(pick < 99, 1, 0), cls.shape),
            jnp.broadcast_to(bits, cls.shape),
        ],
        axis=0,
    )
    row_ref[...] = table
    table = table.astype(F32)
    for k in range(chunks):
        tile = jnp.concatenate([table[:, 128 * k : 128 * k + 128], jnp.zeros((120, 128), F32)], axis=0)
        col_ref[128 * k : 128 * k + 128, :] = jnp.transpose(tile).astype(I32)


def own(col_ref, block, field):
    return col_ref[pl.ds(pl.multiple_of(block * 64, 64), 64), field : field + 1]


def panel_kernel(row_ref, col_ref, chol_ref, l_ref, pos_ref, out_ref):
    cls = row_ref[CLS : CLS + 1, :]
    slot = row_ref[SLOT : SLOT + 1, :]
    own_cls = own(col_ref, pos_ref[0], CLS)
    pick = one(slot == iota((SLOTS, slot.shape[1]), 0)).astype(BF16)
    parts = []
    for n in range(2):
        kept = jnp.where((own_cls ^ cls) == l_ref[n], chol_ref[n], 0.0)
        high, low = split(kept)
        parts.append(dot(high, pick, NT) + dot(low, pick, NT))
    both = jnp.concatenate(parts, axis=1)
    packed = jnp.concatenate([both[0:32], both[32:64]], axis=1)
    out_ref[...] = jnp.broadcast_to(packed[None], out_ref.shape)


def unpack(gathered):
    n = gathered.shape[0]
    return jnp.concatenate([gathered, jnp.roll(gathered, 64, axis=2)], axis=1).reshape(n * 64, 128)


def places(row_ref):
    spot = row_ref[SPOT : SPOT + 1, :]
    number = row_ref[NUM : NUM + 1, :]
    width = spot.shape[1]
    spots = one(spot == iota((16 * RANKS, width), 0)).astype(BF16)
    numbers = one(number == iota((4 * SLOTS, width), 0)).astype(BF16)
    return spots, numbers


def half_kernel(row_ref, col_ref, amp_ref, got_ref, i_ref, j_ref, l_ref, pos_ref, out_ref, high_ref, low_ref):
    p, q = pos_ref[0], pos_ref[1]
    cls = row_ref[CLS : CLS + 1, :]
    label = row_ref[LAB : LAB + 1, 0:128]
    own_cls = own(col_ref, q, CLS)
    own_small = own(col_ref, q, NUM) >= 0
    own_rank = own(col_ref, q, RANK)
    xs = [i_ref[n // 4] ^ j_ref[p * 4 + n % 4] for n in range(8)]
    for n in range(8):
        kept = jnp.where((own_cls ^ cls) == xs[n], amp_ref[n // 4, n % 4], 0.0)
        high_ref[64 * n : 64 * n + 64, :], low_ref[64 * n : 64 * n + 64, :] = split(kept)
    panel = unpack(got_ref[...])
    lane = iota(panel.shape, 1)
    slot = col_ref[:, SLOT : SLOT + 1]
    weights = jnp.where(lane < 64, panel, one(slot == lane - 64))
    wh, wl = split(weights)
    first = dot(high_ref[...], jnp.concatenate([wh, wl], axis=1))
    half = first[:, 0:128] + first[:, 128:256] + dot(low_ref[...], wh)
    parts = [half[64 * n : 64 * n + 64] for n in range(8)]
    firsts = [part[:, 64:96] + jnp.where(own_small, part[:, 0:32], 0.0) for part in parts]
    own_panel = unpack(got_ref[pl.ds(q, 1)])
    stacked = jnp.concatenate([own_panel[:, 0:32], own_panel[:, 32:64]], axis=0)
    ranks = jnp.concatenate([jnp.full_like(own_rank, -1), own_rank], axis=0)
    lane = iota((128, 128), 1)
    left = jnp.where(lane < 32, jnp.concatenate([stacked] * 4, axis=1), one(ranks == lane - 32))
    left = jnp.where(lane < 48, left, 0.0)
    left = jnp.transpose(left)
    pair_cls = jnp.concatenate([own_cls ^ l_ref[0], own_cls ^ l_ref[1]], axis=0)
    both = [jnp.concatenate([part[:, 0:32], part[:, 32:64]], axis=0) for part in parts]
    spread = [
        jnp.where(label == (pair_cls ^ xs[n]), jnp.concatenate([both[n]] * 4, axis=1), 0.0) for n in range(8)
    ]
    sums = dot3(split(left[0:32]), split(jnp.concatenate(spread, axis=1)))
    seconds = dot2(left[32:48].astype(BF16), split(jnp.concatenate(both, axis=1)))
    spots, numbers = places(row_ref)
    order = dot(spots, numbers, NT).astype(BF16)
    for i in range(2):
        rows = jnp.concatenate([sums[:, 128 * n : 128 * n + 128] for n in range(4 * i, 4 * i + 4)], axis=0)
        by_spot = dot2(order, split(rows), NT).reshape(16, RANKS, 128)
        out_ref[:, i, 64 : 64 + RANKS, :] = by_spot + seconds[None, :, 128 * i : 128 * i + 128]
        out_ref[:, i, 0:64, :] = jnp.broadcast_to(
            jnp.concatenate(firsts[4 * i : 4 * i + 4], axis=1)[None], (16, 64, 128)
        )


def ladder_kernel(row_ref, col_ref, got_ref, mid_ref, i_ref, j_ref, l_ref, pos_ref, out_ref):
    p, q = pos_ref[0], pos_ref[1]
    cls = row_ref[CLS : CLS + 1, :]
    number = row_ref[NUM : NUM + 1, :]
    label = row_ref[LAB : LAB + 1, 0:128]
    bits = row_ref[BITS : BITS + 1, 0:1]
    label_col = col_ref[0:128, LAB : LAB + 1]
    width = cls.shape[1]
    turned = jnp.transpose(unpack(got_ref[...]))
    full = [
        jnp.where(label_col == (cls ^ l_ref[n]), jnp.concatenate([turned[32 * n : 32 * n + 32]] * 4, axis=0), 0.0)
        for n in range(2)
    ]
    full = split(jnp.concatenate(full + [one(number == iota((128, width), 0))], axis=0))
    mids = [mid_ref[:, i, 0:64, :].reshape(width, 128) for i in range(2)]
    core = dot3(full, split(jnp.concatenate(mids, axis=1)))
    spots, numbers = places(row_ref)
    order = dot(numbers, spots, NT).astype(BF16)
    own_panel = unpack(got_ref[pl.ds(q, 1)])
    own_slot = own(col_ref, q, SLOT)
    own_rank = own(col_ref, q, RANK)
    own_cls = jnp.concatenate([own(col_ref, q, CLS)] * 4, axis=0)
    lane = iota((64, 128), 1)
    first_tile = jnp.concatenate([own_panel[:, 0:32]] * 4, axis=1)
    second_tile = jnp.concatenate([own_panel[:, 32:64]] * 4, axis=1)
    slot_tile = one(own_slot == (lane & 31))
    rank_pick = one(own_rank == lane).astype(BF16)
    lane_row = iota((1, 128), 1) >> 5
    results = []
    for i in range(2):
        xs = [i_ref[i] ^ j_ref[p * 4 + j] for j in range(4)]
        x_lane = jnp.zeros((1, 128), I32)
        x_row = jnp.zeros((256, 1), I32)
        for j in range(4):
            x_lane = jnp.where(lane_row == j, xs[j], x_lane)
            x_row = jnp.where((iota((256, 1), 0) >> 6) == j, xs[j], x_row)
        odd_lane = parity(x_lane & bits) == 1
        odd = [parity(bits & xs[j]) == 1 for j in range(4)]

        def blocks(tiles):
            return split(
                jnp.concatenate([jnp.where((lane >> 5) == j, tiles[j], 0.0) for j in range(4)], axis=0)
            )

        late = mid_ref[:, i, 64 : 64 + RANKS, :]
        total = jnp.where(odd_lane, 0.0, jnp.sum(late, axis=0))
        late = jnp.where(odd_lane, late.reshape(16 * RANKS, 128), 0.0)
        lanes = slice(128 * i, 128 * i + 128)
        pick = core[256:384, lanes]
        pick2 = jnp.where(odd_lane, dot2(order, split(late)), pick)
        t1 = dot3(blocks([jnp.where(odd[j], slot_tile, first_tile) for j in range(4)]), split(pick), NT)
        t2 = dot3(blocks([jnp.where(odd[j], slot_tile, second_tile) for j in range(4)]), split(pick2), NT)
        t3 = dot3(blocks([first_tile] * 4), split(core[0:128, lanes]), NT)
        t3 = t3 + dot3(blocks([second_tile] * 4), split(core[128:256, lanes]), NT)
        total = jnp.concatenate([total, jnp.zeros((128 - RANKS, 128), F32)], axis=0)
        total = dot2(rank_pick, split(total))
        spread = [jnp.concatenate([total[:, 32 * j : 32 * j + 32]] * 4, axis=1) for j in range(4)]
        t3 = t3 + jnp.concatenate(spread, axis=0)
        goal = own_cls ^ x_row
        t1 = jnp.where(label == (goal ^ l_ref[0]), t1, 0.0)
        t2 = jnp.where(label == (goal ^ l_ref[1]), t2, 0.0)
        t3 = jnp.where(label == goal, t3, 0.0)
        results.append(jnp.concatenate([t1, t2, t3], axis=1))
    result = dot3(split(jnp.concatenate(results, axis=0)), full)
    for n in range(8):
        out_ref[n // 4, n % 4] = result[64 * n : 64 * n + 64]


VMEM = pl.BlockSpec(memory_space=pltpu.VMEM)
SMEM = pl.BlockSpec(memory_space=pltpu.SMEM)
PARAMS = pltpu.CompilerParams(vmem_limit_bytes=48 * 1024 * 1024)


def shape(*dims, dtype=F32):
    return jax.ShapeDtypeStruct(dims, dtype)


def compact(row, col, amplitudes, chol, irrep_i, irrep_j, irrep_l, pos):
    panel = pl.pallas_call(
        panel_kernel,
        out_shape=shape(16, 32, 128),
        in_specs=[VMEM, VMEM, VMEM, SMEM, SMEM],
        out_specs=VMEM,
        compiler_params=PARAMS,
        name="panel_slots",
    )(row, col, chol, irrep_l, pos)
    panel = lax.all_to_all(panel, "ja", split_axis=0, concat_axis=0, tiled=True)
    mid = pl.pallas_call(
        half_kernel,
        out_shape=shape(16, 2, 64 + RANKS, 128),
        in_specs=[VMEM] * 4 + [SMEM] * 4,
        out_specs=VMEM,
        scratch_shapes=[pltpu.VMEM((512, 1024), BF16), pltpu.VMEM((512, 1024), BF16)],
        compiler_params=PARAMS,
        name="half_slots",
    )(row, col, amplitudes, panel, irrep_i, irrep_j, irrep_l, pos)
    mid = lax.all_to_all(mid, "aa", split_axis=0, concat_axis=0, tiled=True)
    return pl.pallas_call(
        ladder_kernel,
        out_shape=shape(*amplitudes.shape),
        in_specs=[VMEM] * 4 + [SMEM] * 4,
        out_specs=VMEM,
        compiler_params=PARAMS,
        name="ladder_slots",
    )(row, col, panel, mid, irrep_i, irrep_j, irrep_l, pos)


def panel_rows(half_ref, other_ref, core, high_ref, low_ref):
    for k in range(half_ref.shape[0]):
        for part, ref in ((core, half_ref), (1 - core, other_ref)):
            rows = pl.ds(pl.multiple_of((2 * k + part) * 64, 64), 64)
            high_ref[rows, :], low_ref[rows, :] = split(ref[k])


def dense_half_kernel(
    row_ref, col_ref, amp_ref, half_ref, other_ref, i_ref, j_ref, pos_ref, out_ref, ph_ref, pl_ref, high_ref, low_ref
):
    p, q = pos_ref[0], pos_ref[1]
    panel_rows(half_ref, other_ref, p & 1, ph_ref, pl_ref)
    cls = row_ref[CLS : CLS + 1, :]
    own_cls = own(col_ref, q, CLS)
    for n in range(8):
        kept = jnp.where((own_cls ^ cls) == (i_ref[n // 4] ^ j_ref[p * 4 + n % 4]), amp_ref[n // 4, n % 4], 0.0)
        high_ref[64 * n : 64 * n + 64, :], low_ref[64 * n : 64 * n + 64, :] = split(kept)
    result = dot3((ph_ref[...], pl_ref[...]), (high_ref[...], low_ref[...]), NT)
    out_ref[...] = result.reshape(out_ref.shape)


def dense_ladder_kernel(
    row_ref, col_ref, mid_ref, half_ref, other_ref, i_ref, j_ref, pos_ref, out_ref, ph_ref, pl_ref, high_ref, low_ref
):
    p, q = pos_ref[0], pos_ref[1]
    panel_rows(half_ref, other_ref, p & 1, ph_ref, pl_ref)
    first = iota((64, 128), 1) < 64
    for n in range(8):
        lanes = slice(128 * (n // 2), 128 * (n // 2) + 128)
        for s in range(0, 16, 2):
            a, b = mid_ref[s, :, lanes], mid_ref[s + 1, :, lanes]
            both = jnp.where(first, a, jnp.roll(b, 64, axis=1)) if n % 2 == 0 else jnp.where(first, jnp.roll(a, 64, axis=1), b)
            place = (slice(64 * n, 64 * n + 64), slice(64 * s, 64 * s + 128))
            high_ref[place], low_ref[place] = split(both)
    result = dot3((high_ref[...], low_ref[...]), (ph_ref[...], pl_ref[...]))
    pair_cls = own(col_ref, q, CLS) ^ row_ref[CLS : CLS + 1, :]
    for n in range(8):
        x = i_ref[n // 4] ^ j_ref[p * 4 + n % 4]
        out_ref[n // 4, n % 4] = jnp.where(pair_cls == x, result[64 * n : 64 * n + 64], 0.0)


CORES = [[2 * k + core for k in range(8)] for core in (0, 1)]


def dense(row, col, amplitudes, panel, irrep_i, irrep_j, pos):
    half = jnp.broadcast_to(panel[None], (8, *panel.shape))
    half = lax.all_to_all(half, "ja", split_axis=0, concat_axis=0, tiled=True, axis_index_groups=CORES)
    other = lax.ppermute(half, "ja", [(n, n ^ 1) for n in range(16)])
    halves = [pltpu.VMEM((1024, 1024), BF16)] * 2 + [pltpu.VMEM((512, 1024), BF16)] * 2
    mid = pl.pallas_call(
        dense_half_kernel,
        out_shape=shape(16, 64, 512),
        in_specs=[VMEM] * 5 + [SMEM] * 3,
        out_specs=VMEM,
        scratch_shapes=halves,
        compiler_params=PARAMS,
        name="half_dense",
    )(row, col, amplitudes, half, other, irrep_i, irrep_j, pos)
    mid = lax.all_to_all(mid, "aa", split_axis=0, concat_axis=0, tiled=True)
    return pl.pallas_call(
        dense_ladder_kernel,
        out_shape=shape(*amplitudes.shape),
        in_specs=[VMEM] * 5 + [SMEM] * 3,
        out_specs=VMEM,
        scratch_shapes=halves,
        compiler_params=PARAMS,
        name="ladder_dense",
    )(row, col, mid, half, other, irrep_i, irrep_j, pos)


def local(amplitudes, chol, irrep_i, irrep_j, irrep_v, irrep_l):
    pos = jnp.stack([lax.axis_index("ja"), lax.axis_index("aa")]).astype(I32)
    width = irrep_v.shape[0]
    row, col = pl.pallas_call(
        table_kernel,
        out_shape=(shape(8, width, dtype=I32), shape(width, 128, dtype=I32)),
        in_specs=[VMEM, SMEM],
        out_specs=(VMEM, VMEM),
        compiler_params=PARAMS,
        name="orbital_table",
    )(irrep_v.reshape(1, width), irrep_l)
    height = chol.shape[1]

    def panels():
        own_rows = lax.dynamic_slice_in_dim(irrep_v, pos[0] * height, height)
        pair = own_rows[:, None] ^ irrep_v[None, :]
        return [jnp.where(pair == irrep_l[n], chol[n], 0.0) for n in range(2)]

    def run(panel):
        return dense(row, col, amplitudes, panel, irrep_i, irrep_j, pos)

    def together():
        first, second = panels()
        return run(first + second)

    def apart():
        first, second = panels()
        return run(first) + run(second)

    return lax.switch(
        jnp.where(row[FLAG, 0] == 1, 0, jnp.where(irrep_l[0] != irrep_l[1], 1, 2)),
        [
            lambda: compact(row, col, amplitudes, chol, irrep_i, irrep_j, irrep_l, pos),
            together,
            apart,
        ],
    )


def solution(mesh):
    in_specs = (P(None, "ja", "aa", None), P(None, "ja", None), P(), P(), P(), P())
    out_specs = P(None, "ja", "aa", None)
    return jax.shard_map(local, mesh=mesh, in_specs=in_specs, out_specs=out_specs, check_vma=False)
```

```python
import jax
import jax.numpy as jnp
from jax import lax
from jax.experimental import pallas as pl
from jax.experimental.pallas import tpu as pltpu
from jax.sharding import PartitionSpec as P

F32, BF16, I32 = jnp.float32, jnp.bfloat16, jnp.int32
NN = (((1,), (0,)), ((), ()))
NT = (((1,), (1,)), ((), ()))
SLOTS = 32
RANKS = 16
CLS, NUM, SLOT, SPOT, LAB, RANK, BRANCH, BITS = range(8)


def iota(shape, dim):
    return lax.broadcasted_iota(I32, shape, dim)


def parity(x):
    return (x ^ (x >> 1) ^ (x >> 2)) & 1


def one(cond):
    return jnp.where(cond, 1.0, 0.0).astype(F32)


def dot(a, b, dims=NN):
    return lax.dot_general(a, b, dims, preferred_element_type=F32)


def split(x):
    high = x.astype(BF16)
    return high, (x - high.astype(F32)).astype(BF16)


def dot3(a, b, dims=NN):
    (ah, al), (bh, bl) = a, b
    return dot(ah, bh, dims) + dot(ah, bl, dims) + dot(al, bh, dims)


def dot2(a, b, dims=NN):
    return dot(a, b[0], dims) + dot(a, b[1], dims)


def table_kernel(irrep_ref, chol_ref, i_ref, l_ref, pos_ref, row_ref, col_ref, out_ref):
    cls = irrep_ref[...]
    width = cls.shape[1]
    chunks = width // 128
    onehot = one(cls == iota((16, width), 0))
    before = one(iota((128, 128), 0) < iota((128, 128), 1))
    count = jnp.zeros((16, 1), F32)
    blocks = jnp.zeros((16, 128), F32)
    slots = []
    for k in range(chunks):
        part = onehot[:, 128 * k : 128 * k + 128]
        ahead = dot(part.astype(BF16), before.astype(BF16)) + count
        slots.append(jnp.sum(part * ahead, axis=0, keepdims=True))
        count = count + jnp.sum(part, axis=1, keepdims=True)
        place = one(iota((128, 128), 1) == 2 * k + (iota((128, 128), 0) >> 6))
        blocks = blocks + dot(part.astype(BF16), place.astype(BF16))
    slot = jnp.concatenate(slots, axis=1).astype(I32)
    lane = iota((16, 128), 1)
    cand = iota((16, 128), 0)
    count_lane = jnp.sum(jnp.where(lane == cand, count, 0.0), axis=0, keepdims=True)
    member = (parity((cand >> 1) & lane) == (cand & 1)) & (lane < 8)
    largest = jnp.max(jnp.where(member, count_lane, 0.0), axis=1, keepdims=True)
    in_block = jnp.zeros((16, 128), F32)
    for g in range(8):
        in_block = in_block + jnp.where(parity((cand >> 1) & g) == (cand & 1), blocks[g : g + 1, :], 0.0)
    fullest = jnp.max(in_block, axis=1, keepdims=True)
    bits_col = cand[:, 0:1] >> 1
    good = (largest <= SLOTS) & (fullest <= RANKS)
    for n in range(l_ref.shape[0]):
        good = good & (parity(bits_col & l_ref[n]) == 1)
    rank = cand[:, 0:1] + jnp.where(parity(bits_col & (i_ref[0] ^ i_ref[1])) == 1, 0, 16)
    pick = jnp.min(jnp.where(good, rank.astype(F32), 99.0), axis=0, keepdims=True).astype(I32)
    dense_branch = jnp.where(l_ref[0] != l_ref[1], 2, 3)
    branch = jnp.where(pick < 16, 0, jnp.where(pick < 32, 1, dense_branch))
    bits, side = (pick & 15) >> 1, pick & 1
    small = parity(bits & cls) == side
    group = jnp.zeros_like(cls)
    label = jnp.zeros_like(cls)
    lane_group = iota((1, width), 1) >> 5
    number = jnp.zeros((1, 1), I32)
    for g in range(8):
        is_small = parity(bits & g) == side
        group = group + jnp.where(is_small & (cls > g), 1, 0)
        label = label + jnp.where(is_small & (number == lane_group), g, 0)
        number = number + jnp.where(is_small, 1, 0)
    inner = one((iota((128, 128), 0) < iota((128, 128), 1)) & ((iota((128, 128), 0) >> 6) == (iota((128, 128), 1) >> 6)))
    small16 = jnp.broadcast_to(one(small), (16, width))
    ranks = [
        dot(small16[:, 128 * k : 128 * k + 128].astype(BF16), inner.astype(BF16))[0:1, :] for k in range(chunks)
    ]
    rank = jnp.concatenate(ranks, axis=1).astype(I32)
    none = jnp.full_like(cls, -1)
    table = jnp.concatenate(
        [
            cls,
            jnp.where(small, group * SLOTS + slot, none),
            jnp.where(small, slot, none),
            jnp.where(small, (iota((1, width), 1) >> 6) * RANKS + rank, none),
            label,
            jnp.where(small, rank, none),
            jnp.broadcast_to(branch, cls.shape),
            jnp.broadcast_to(bits, cls.shape),
        ],
        axis=0,
    )
    row_ref[...] = table
    table = table.astype(F32)
    for k in range(chunks):
        tile = jnp.concatenate([table[:, 128 * k : 128 * k + 128], jnp.zeros((120, 128), F32)], axis=0)
        col_ref[128 * k : 128 * k + 128, :] = jnp.transpose(tile).astype(I32)
    panel_slots(row_ref, col_ref, chol_ref, l_ref, pos_ref, out_ref)


def own(col_ref, block, field):
    return col_ref[pl.ds(pl.multiple_of(block * 64, 64), 64), field : field + 1]


def panel_slots(row_ref, col_ref, chol_ref, l_ref, pos_ref, out_ref):
    cls = row_ref[CLS : CLS + 1, :]
    slot = row_ref[SLOT : SLOT + 1, :]
    own_cls = own(col_ref, pos_ref[0], CLS)
    pick = one(slot == iota((SLOTS, slot.shape[1]), 0)).astype(BF16)
    parts = []
    for n in range(2):
        kept = jnp.where((own_cls ^ cls) == l_ref[n], chol_ref[n], 0.0)
        high, low = split(kept)
        parts.append(dot(high, pick, NT) + dot(low, pick, NT))
    both = jnp.concatenate(parts, axis=1)
    packed = jnp.concatenate([both[0:32], both[32:64]], axis=1)
    out_ref[...] = jnp.broadcast_to(packed[None], out_ref.shape)


def unpack(gathered):
    n = gathered.shape[0]
    return jnp.concatenate([gathered, jnp.roll(gathered, 64, axis=2)], axis=1).reshape(n * 64, 128)


def places(row_ref):
    spot = row_ref[SPOT : SPOT + 1, :]
    number = row_ref[NUM : NUM + 1, :]
    width = spot.shape[1]
    spots = one(spot == iota((16 * RANKS, width), 0)).astype(BF16)
    numbers = one(number == iota((4 * SLOTS, width), 0)).astype(BF16)
    return spots, numbers


def ladder_kernel(row_ref, col_ref, got_ref, mid_ref, i_ref, j_ref, l_ref, pos_ref, out_ref):
    p, q = pos_ref[0], pos_ref[1]
    cls = row_ref[CLS : CLS + 1, :]
    number = row_ref[NUM : NUM + 1, :]
    label = row_ref[LAB : LAB + 1, 0:128]
    bits = row_ref[BITS : BITS + 1, 0:1]
    label_col = col_ref[0:128, LAB : LAB + 1]
    width = cls.shape[1]
    turned = jnp.transpose(unpack(got_ref[...]))
    full = [
        jnp.where(label_col == (cls ^ l_ref[n]), jnp.concatenate([turned[32 * n : 32 * n + 32]] * 4, axis=0), 0.0)
        for n in range(2)
    ]
    full = split(jnp.concatenate(full + [one(number == iota((128, width), 0))], axis=0))
    mids = [mid_ref[:, i, 0:64, :].reshape(width, 128) for i in range(2)]
    core = dot3(full, split(jnp.concatenate(mids, axis=1)))
    spots, numbers = places(row_ref)
    order = dot(numbers, spots, NT).astype(BF16)
    own_panel = unpack(got_ref[pl.ds(q, 1)])
    own_slot = own(col_ref, q, SLOT)
    own_rank = own(col_ref, q, RANK)
    own_cls = jnp.concatenate([own(col_ref, q, CLS)] * 4, axis=0)
    lane = iota((64, 128), 1)
    first_tile = jnp.concatenate([own_panel[:, 0:32]] * 4, axis=1)
    second_tile = jnp.concatenate([own_panel[:, 32:64]] * 4, axis=1)
    slot_tile = one(own_slot == (lane & 31))
    rank_pick = one(own_rank == lane).astype(BF16)
    lane_row = iota((1, 128), 1) >> 5
    results = []
    for i in range(2):
        xs = [i_ref[i] ^ j_ref[p * 4 + j] for j in range(4)]
        x_lane = jnp.zeros((1, 128), I32)
        x_row = jnp.zeros((256, 1), I32)
        for j in range(4):
            x_lane = jnp.where(lane_row == j, xs[j], x_lane)
            x_row = jnp.where((iota((256, 1), 0) >> 6) == j, xs[j], x_row)
        odd_lane = parity(x_lane & bits) == 1
        odd = [parity(bits & xs[j]) == 1 for j in range(4)]

        def blocks(tiles):
            return split(
                jnp.concatenate([jnp.where((lane >> 5) == j, tiles[j], 0.0) for j in range(4)], axis=0)
            )

        late = mid_ref[:, i, 64 : 64 + RANKS, :]
        total = jnp.where(odd_lane, 0.0, jnp.sum(late, axis=0))
        late = jnp.where(odd_lane, late.reshape(16 * RANKS, 128), 0.0)
        lanes = slice(128 * i, 128 * i + 128)
        pick = core[256:384, lanes]
        pick2 = jnp.where(odd_lane, dot2(order, split(late)), pick)
        t1 = dot3(blocks([jnp.where(odd[j], slot_tile, first_tile) for j in range(4)]), split(pick), NT)
        t2 = dot3(blocks([jnp.where(odd[j], slot_tile, second_tile) for j in range(4)]), split(pick2), NT)
        t3 = dot3(blocks([first_tile] * 4), split(core[0:128, lanes]), NT)
        t3 = t3 + dot3(blocks([second_tile] * 4), split(core[128:256, lanes]), NT)
        total = jnp.concatenate([total, jnp.zeros((128 - RANKS, 128), F32)], axis=0)
        total = dot2(rank_pick, split(total))
        spread = [jnp.concatenate([total[:, 32 * j : 32 * j + 32]] * 4, axis=1) for j in range(4)]
        t3 = t3 + jnp.concatenate(spread, axis=0)
        goal = own_cls ^ x_row
        t1 = jnp.where(label == (goal ^ l_ref[0]), t1, 0.0)
        t2 = jnp.where(label == (goal ^ l_ref[1]), t2, 0.0)
        t3 = jnp.where(label == goal, t3, 0.0)
        results.append(jnp.concatenate([t1, t2, t3], axis=1))
    result = dot3(split(jnp.concatenate(results, axis=0)), full)
    for n in range(8):
        out_ref[n // 4, n % 4] = result[64 * n : 64 * n + 64]


def half_products(row_ref, col_ref, amp_ref, got_ref, i_ref, j_ref, pos_ref, high_ref, low_ref):
    p, q = pos_ref[0], pos_ref[1]
    cls = row_ref[CLS : CLS + 1, :]
    own_cls = own(col_ref, q, CLS)
    for n in range(8):
        kept = jnp.where((own_cls ^ cls) == (i_ref[n // 4] ^ j_ref[p * 4 + n % 4]), amp_ref[n // 4, n % 4], 0.0)
        high_ref[64 * n : 64 * n + 64, :], low_ref[64 * n : 64 * n + 64, :] = split(kept)
    panel = unpack(got_ref[...])
    lane = iota(panel.shape, 1)
    slot = col_ref[:, SLOT : SLOT + 1]
    wh, wl = split(jnp.where(lane < 64, panel, one(slot == lane - 64)))
    first = dot(high_ref[...], jnp.concatenate([wh, wl], axis=1))
    half = first[:, 0:128] + first[:, 128:256] + dot(low_ref[...], wh)
    return [half[64 * n : 64 * n + 64] for n in range(8)]


def left_factor(col_ref, got_ref, q):
    own_rank = own(col_ref, q, RANK)
    own_panel = unpack(got_ref[pl.ds(q, 1)])
    stacked = jnp.concatenate([own_panel[:, 0:32], own_panel[:, 32:64]], axis=0)
    ranks = jnp.concatenate([jnp.full_like(own_rank, -1), own_rank], axis=0)
    lane = iota((128, 128), 1)
    left = jnp.where(lane < 32, jnp.concatenate([stacked] * 4, axis=1), one(ranks == lane - 32))
    return jnp.transpose(jnp.where(lane < 48, left, 0.0))


def odd_even(row_ref, i_ref, j_ref, p):
    bits = row_ref[BITS : BITS + 1, 0:1]
    later = [parity(bits & (i_ref[1] ^ j_ref[p * 4 + j])) == 1 for j in range(4)]
    xs = [[jnp.where(later[j], i_ref[i] ^ j_ref[p * 4 + j], i_ref[1 - i] ^ j_ref[p * 4 + j]) for j in range(4)] for i in (1, 0)]
    return later, xs[0], xs[1]


def half_kernel(row_ref, col_ref, amp_ref, got_ref, i_ref, j_ref, l_ref, pos_ref, out_ref, high_ref, low_ref):
    p, q = pos_ref[0], pos_ref[1]
    label = row_ref[LAB : LAB + 1, 0:128]
    own_cls = own(col_ref, q, CLS)
    own_small = own(col_ref, q, NUM) >= 0
    xs = [i_ref[n // 4] ^ j_ref[p * 4 + n % 4] for n in range(8)]
    parts = half_products(row_ref, col_ref, amp_ref, got_ref, i_ref, j_ref, pos_ref, high_ref, low_ref)
    firsts = [part[:, 64:96] + jnp.where(own_small, part[:, 0:32], 0.0) for part in parts]
    left = left_factor(col_ref, got_ref, q)
    pair_cls = jnp.concatenate([own_cls ^ l_ref[0], own_cls ^ l_ref[1]], axis=0)
    both = [jnp.concatenate([part[:, 0:32], part[:, 32:64]], axis=0) for part in parts]
    spread = [
        jnp.where(label == (pair_cls ^ xs[n]), jnp.concatenate([both[n]] * 4, axis=1), 0.0) for n in range(8)
    ]
    sums = dot3(split(left[0:32]), split(jnp.concatenate(spread, axis=1)))
    seconds = dot2(left[32:48].astype(BF16), split(jnp.concatenate(both, axis=1)))
    spots, numbers = places(row_ref)
    order = dot(spots, numbers, NT).astype(BF16)
    for i in range(2):
        rows = jnp.concatenate([sums[:, 128 * n : 128 * n + 128] for n in range(4 * i, 4 * i + 4)], axis=0)
        by_spot = dot2(order, split(rows), NT).reshape(16, RANKS, 128)
        out_ref[:, i, 64 : 64 + RANKS, :] = by_spot + seconds[None, :, 128 * i : 128 * i + 128]
        out_ref[:, i, 0:64, :] = jnp.broadcast_to(
            jnp.concatenate(firsts[4 * i : 4 * i + 4], axis=1)[None], (16, 64, 128)
        )


def half_paired_kernel(row_ref, col_ref, amp_ref, got_ref, i_ref, j_ref, l_ref, pos_ref, out_ref, high_ref, low_ref):
    p, q = pos_ref[0], pos_ref[1]
    label = row_ref[LAB : LAB + 1, 0:128]
    own_cls = own(col_ref, q, CLS)
    own_small = own(col_ref, q, NUM) >= 0
    parts = half_products(row_ref, col_ref, amp_ref, got_ref, i_ref, j_ref, pos_ref, high_ref, low_ref)
    later, _, even_x = odd_even(row_ref, i_ref, j_ref, p)
    odd = [jnp.where(later[j], parts[4 + j], parts[j]) for j in range(4)]
    even = [jnp.where(later[j], parts[j], parts[4 + j]) for j in range(4)]
    rows = jnp.concatenate([part[:, 64:96] + jnp.where(own_small, part[:, 0:32], 0.0) for part in odd], axis=1)
    out_ref[:, 0:64, :] = jnp.broadcast_to(rows[None], (16, 64, 128))
    left = left_factor(col_ref, got_ref, q)
    firsts = jnp.concatenate([part[:, 64:96] for part in even], axis=1)
    seconds = jnp.concatenate([part[:, 32:64] for part in odd], axis=1)
    few = jnp.concatenate([firsts, seconds], axis=1)
    few = dot2(left[32:48].astype(BF16), split(jnp.concatenate([few, few], axis=0)))
    for k in range(2):
        few_rows = few[None, :, 128 * k : 128 * k + 128]
        out_ref[:, 64 + RANKS * k : 64 + RANKS * (k + 1), :] = jnp.broadcast_to(few_rows, (16, RANKS, 128))
    pair_cls = jnp.concatenate([own_cls ^ l_ref[0], own_cls ^ l_ref[1]], axis=0)
    spread = []
    for j in range(4):
        both = jnp.concatenate([even[j][:, 0:32], even[j][:, 32:64]], axis=0)
        spread.append(jnp.where(label == (pair_cls ^ even_x[j]), jnp.concatenate([both] * 4, axis=1), 0.0))
    sums = dot3(split(left[0:32]), split(jnp.concatenate(spread, axis=1)))
    sums = jnp.concatenate([sums[:, 128 * j : 128 * j + 128] for j in range(4)], axis=0)
    spots, numbers = places(row_ref)
    order = dot(spots, numbers, NT).astype(BF16)
    out_ref[:, 64 + 2 * RANKS : 64 + 3 * RANKS, :] = dot2(order, split(sums), NT).reshape(16, RANKS, 128)


def ladder_paired_kernel(row_ref, col_ref, got_ref, mid_ref, i_ref, j_ref, l_ref, pos_ref, out_ref):
    p, q = pos_ref[0], pos_ref[1]
    cls = row_ref[CLS : CLS + 1, :]
    number = row_ref[NUM : NUM + 1, :]
    label = row_ref[LAB : LAB + 1, 0:128]
    label_col = col_ref[0:128, LAB : LAB + 1]
    width = cls.shape[1]
    turned = jnp.transpose(unpack(got_ref[...]))
    full = [
        jnp.where(label_col == (cls ^ l_ref[n]), jnp.concatenate([turned[32 * n : 32 * n + 32]] * 4, axis=0), 0.0)
        for n in range(2)
    ]
    full = split(jnp.concatenate(full + [one(number == iota((128, width), 0))], axis=0))
    core = dot3(full, split(mid_ref[:, 0:64, :].reshape(width, 128)))
    spots, numbers = places(row_ref)
    order = dot(numbers, spots, NT).astype(BF16)
    few = [mid_ref[:, 64 + RANKS * k : 64 + RANKS * (k + 1), :] for k in range(3)]
    small_rows, second_rows = [dot2(order, split(few[k].reshape(16 * RANKS, 128))) for k in range(2)]
    total = jnp.concatenate([jnp.sum(few[2], axis=0), jnp.zeros((128 - RANKS, 128), F32)], axis=0)
    own_panel = unpack(got_ref[pl.ds(q, 1)])
    own_slot = own(col_ref, q, SLOT)
    own_rank = own(col_ref, q, RANK)
    own_cls = own(col_ref, q, CLS)
    lane = iota((64, 128), 1)

    def blocks(tile):
        return split(jnp.concatenate([jnp.where((lane >> 5) == j, tile, 0.0) for j in range(4)], axis=0))

    first = blocks(jnp.concatenate([own_panel[:, 0:32]] * 4, axis=1))
    second = blocks(jnp.concatenate([own_panel[:, 32:64]] * 4, axis=1))
    slots = blocks(one(own_slot == (lane & 31)))[0]
    total = dot2(one(own_rank == lane).astype(BF16), split(total))
    total = [jnp.concatenate([total[:, 32 * j : 32 * j + 32]] * 4, axis=1) for j in range(4)]
    odd = [
        dot2(slots, split(core[256:384]), NT),
        dot2(slots, split(second_rows), NT),
        dot3(first, split(core[0:128]), NT) + dot3(second, split(core[128:256]), NT),
    ]
    small_rows = split(small_rows)
    even = [dot3(first, small_rows, NT), dot3(second, small_rows, NT), jnp.concatenate(total, axis=0)]
    later, odd_x, even_x = odd_even(row_ref, i_ref, j_ref, p)
    rows = [None] * 8
    for j in range(4):
        kinds = []
        for parts, x in ((odd, odd_x[j]), (even, even_x[j])):
            goal = own_cls ^ x
            labels = (goal ^ l_ref[0], goal ^ l_ref[1], goal)
            kinds.append(
                jnp.concatenate(
                    [jnp.where(label == labels[k], parts[k][64 * j : 64 * j + 64], 0.0) for k in range(3)], axis=1
                )
            )
        rows[j] = jnp.where(later[j], kinds[1], kinds[0])
        rows[4 + j] = jnp.where(later[j], kinds[0], kinds[1])
    result = dot3(split(jnp.concatenate(rows, axis=0)), full)
    for n in range(8):
        out_ref[n // 4, n % 4] = result[64 * n : 64 * n + 64]


VMEM = pl.BlockSpec(memory_space=pltpu.VMEM)
SMEM = pl.BlockSpec(memory_space=pltpu.SMEM)
PARAMS = pltpu.CompilerParams(vmem_limit_bytes=48 * 1024 * 1024)


def shape(*dims, dtype=F32):
    return jax.ShapeDtypeStruct(dims, dtype)


def compact(kernels, middle, row, col, panel, amplitudes, irrep_i, irrep_j, irrep_l, pos):
    panel = lax.all_to_all(panel, "ja", split_axis=0, concat_axis=0, tiled=True)
    mid = pl.pallas_call(
        kernels[0],
        out_shape=shape(16, *middle, 128),
        in_specs=[VMEM] * 4 + [SMEM] * 4,
        out_specs=VMEM,
        scratch_shapes=[pltpu.VMEM((512, 1024), BF16), pltpu.VMEM((512, 1024), BF16)],
        compiler_params=PARAMS,
        name="half_slots",
    )(row, col, amplitudes, panel, irrep_i, irrep_j, irrep_l, pos)
    mid = lax.all_to_all(mid, "aa", split_axis=0, concat_axis=0, tiled=True)
    return pl.pallas_call(
        kernels[1],
        out_shape=shape(*amplitudes.shape),
        in_specs=[VMEM] * 4 + [SMEM] * 4,
        out_specs=VMEM,
        compiler_params=PARAMS,
        name="ladder_slots",
    )(row, col, panel, mid, irrep_i, irrep_j, irrep_l, pos)


def panel_rows(half_ref, other_ref, core, high_ref, low_ref):
    for k in range(half_ref.shape[0]):
        for part, ref in ((core, half_ref), (1 - core, other_ref)):
            rows = pl.ds(pl.multiple_of((2 * k + part) * 64, 64), 64)
            high_ref[rows, :], low_ref[rows, :] = split(ref[k])


def dense_half_kernel(
    row_ref, col_ref, amp_ref, half_ref, other_ref, i_ref, j_ref, pos_ref, out_ref, ph_ref, pl_ref, high_ref, low_ref
):
    p, q = pos_ref[0], pos_ref[1]
    panel_rows(half_ref, other_ref, p & 1, ph_ref, pl_ref)
    cls = row_ref[CLS : CLS + 1, :]
    own_cls = own(col_ref, q, CLS)
    for n in range(8):
        kept = jnp.where((own_cls ^ cls) == (i_ref[n // 4] ^ j_ref[p * 4 + n % 4]), amp_ref[n // 4, n % 4], 0.0)
        high_ref[64 * n : 64 * n + 64, :], low_ref[64 * n : 64 * n + 64, :] = split(kept)
    result = dot3((ph_ref[...], pl_ref[...]), (high_ref[...], low_ref[...]), NT)
    out_ref[...] = result.reshape(out_ref.shape)


def dense_ladder_kernel(
    row_ref, col_ref, mid_ref, half_ref, other_ref, i_ref, j_ref, pos_ref, out_ref, ph_ref, pl_ref, high_ref, low_ref
):
    p, q = pos_ref[0], pos_ref[1]
    panel_rows(half_ref, other_ref, p & 1, ph_ref, pl_ref)
    first = iota((64, 128), 1) < 64
    for n in range(8):
        lanes = slice(128 * (n // 2), 128 * (n // 2) + 128)
        for s in range(0, 16, 2):
            a, b = mid_ref[s, :, lanes], mid_ref[s + 1, :, lanes]
            both = jnp.where(first, a, jnp.roll(b, 64, axis=1)) if n % 2 == 0 else jnp.where(first, jnp.roll(a, 64, axis=1), b)
            place = (slice(64 * n, 64 * n + 64), slice(64 * s, 64 * s + 128))
            high_ref[place], low_ref[place] = split(both)
    result = dot3((high_ref[...], low_ref[...]), (ph_ref[...], pl_ref[...]))
    pair_cls = own(col_ref, q, CLS) ^ row_ref[CLS : CLS + 1, :]
    for n in range(8):
        x = i_ref[n // 4] ^ j_ref[p * 4 + n % 4]
        out_ref[n // 4, n % 4] = jnp.where(pair_cls == x, result[64 * n : 64 * n + 64], 0.0)


CORES = [[2 * k + core for k in range(8)] for core in (0, 1)]


def dense(row, col, amplitudes, panel, irrep_i, irrep_j, pos):
    half = jnp.broadcast_to(panel[None], (8, *panel.shape))
    half = lax.all_to_all(half, "ja", split_axis=0, concat_axis=0, tiled=True, axis_index_groups=CORES)
    other = lax.ppermute(half, "ja", [(n, n ^ 1) for n in range(16)])
    halves = [pltpu.VMEM((1024, 1024), BF16)] * 2 + [pltpu.VMEM((512, 1024), BF16)] * 2
    mid = pl.pallas_call(
        dense_half_kernel,
        out_shape=shape(16, 64, 512),
        in_specs=[VMEM] * 5 + [SMEM] * 3,
        out_specs=VMEM,
        scratch_shapes=halves,
        compiler_params=PARAMS,
        name="half_dense",
    )(row, col, amplitudes, half, other, irrep_i, irrep_j, pos)
    mid = lax.all_to_all(mid, "aa", split_axis=0, concat_axis=0, tiled=True)
    return pl.pallas_call(
        dense_ladder_kernel,
        out_shape=shape(*amplitudes.shape),
        in_specs=[VMEM] * 5 + [SMEM] * 3,
        out_specs=VMEM,
        scratch_shapes=halves,
        compiler_params=PARAMS,
        name="ladder_dense",
    )(row, col, mid, half, other, irrep_i, irrep_j, pos)


def local(amplitudes, chol, irrep_i, irrep_j, irrep_v, irrep_l):
    pos = jnp.stack([lax.axis_index("ja"), lax.axis_index("aa")]).astype(I32)
    width = irrep_v.shape[0]
    row, col, slots = pl.pallas_call(
        table_kernel,
        out_shape=(shape(8, width, dtype=I32), shape(width, 128, dtype=I32), shape(16, 32, 128)),
        in_specs=[VMEM, VMEM, SMEM, SMEM, SMEM],
        out_specs=(VMEM, VMEM, VMEM),
        compiler_params=PARAMS,
        name="orbital_table",
    )(irrep_v.reshape(1, width), chol, irrep_i, irrep_l, pos)
    height = chol.shape[1]

    def panels():
        own_rows = lax.dynamic_slice_in_dim(irrep_v, pos[0] * height, height)
        pair = own_rows[:, None] ^ irrep_v[None, :]
        return [jnp.where(pair == irrep_l[n], chol[n], 0.0) for n in range(2)]

    def run(panel):
        return dense(row, col, amplitudes, panel, irrep_i, irrep_j, pos)

    def together():
        first, second = panels()
        return run(first + second)

    def apart():
        first, second = panels()
        return run(first) + run(second)

    few = (row, col, slots, amplitudes, irrep_i, irrep_j, irrep_l, pos)
    return lax.switch(
        row[BRANCH, 0],
        [
            lambda: compact((half_paired_kernel, ladder_paired_kernel), (64 + 3 * RANKS,), *few),
            lambda: compact((half_kernel, ladder_kernel), (2, 64 + RANKS), *few),
            together,
            apart,
        ],
    )


def solution(mesh):
    in_specs = (P(None, "ja", "aa", None), P(None, "ja", None), P(), P(), P(), P())
    out_specs = P(None, "ja", "aa", None)
    return jax.shard_map(local, mesh=mesh, in_specs=in_specs, out_specs=out_specs, check_vma=False)
```

```python
import functools

import jax
import jax.numpy as jnp
from jax import lax
from jax.experimental import pallas as pl
from jax.experimental.pallas import tpu as pltpu
from jax.sharding import PartitionSpec as P

F32, BF16, I32 = jnp.float32, jnp.bfloat16, jnp.int32
NN = (((1,), (0,)), ((), ()))
NT = (((1,), (1,)), ((), ()))
SLOTS = 32
TIGHT = 24
RANKS = 16
CLS, NUM, SLOT, SPOT, LAB, RANK, BRANCH, BITS = range(8)


def iota(shape, dim):
    return lax.broadcasted_iota(I32, shape, dim)


def parity(x):
    return (x ^ (x >> 1) ^ (x >> 2)) & 1


def one(cond):
    return jnp.where(cond, 1.0, 0.0).astype(F32)


def dot(a, b, dims=NN):
    return lax.dot_general(a, b, dims, preferred_element_type=F32)


def split(x):
    high = x.astype(BF16)
    return high, (x - high.astype(F32)).astype(BF16)


def dot3(a, b, dims=NN):
    (ah, al), (bh, bl) = a, b
    return dot(ah, bh, dims) + dot(ah, bl, dims) + dot(al, bh, dims)


def dot2(a, b, dims=NN):
    return dot(a, b[0], dims) + dot(a, b[1], dims)


def table_kernel(irrep_ref, chol_ref, i_ref, l_ref, pos_ref, row_ref, col_ref, order_ref, turn_ref, out_ref):
    cls = irrep_ref[...]
    width = cls.shape[1]
    chunks = width // 128
    onehot = one(cls == iota((16, width), 0))
    before = one(iota((128, 128), 0) < iota((128, 128), 1))
    count = jnp.zeros((16, 1), F32)
    blocks = jnp.zeros((16, 128), F32)
    slots = []
    for k in range(chunks):
        part = onehot[:, 128 * k : 128 * k + 128]
        ahead = dot(part.astype(BF16), before.astype(BF16)) + count
        slots.append(jnp.sum(part * ahead, axis=0, keepdims=True))
        count = count + jnp.sum(part, axis=1, keepdims=True)
        place = one(iota((128, 128), 1) == 2 * k + (iota((128, 128), 0) >> 6))
        blocks = blocks + dot(part.astype(BF16), place.astype(BF16))
    slot = jnp.concatenate(slots, axis=1).astype(I32)
    lane = iota((16, 128), 1)
    cand = iota((16, 128), 0)
    count_lane = jnp.sum(jnp.where(lane == cand, count, 0.0), axis=0, keepdims=True)
    member = (parity((cand >> 1) & lane) == (cand & 1)) & (lane < 8)
    largest = jnp.max(jnp.where(member, count_lane, 0.0), axis=1, keepdims=True)
    in_block = jnp.zeros((16, 128), F32)
    for g in range(8):
        in_block = in_block + jnp.where(parity((cand >> 1) & g) == (cand & 1), blocks[g : g + 1, :], 0.0)
    fullest = jnp.max(in_block, axis=1, keepdims=True)
    bits_col = cand[:, 0:1] >> 1
    good = (largest <= SLOTS) & (fullest <= RANKS)
    for n in range(l_ref.shape[0]):
        good = good & (parity(bits_col & l_ref[n]) == 1)
    rank = cand[:, 0:1] + jnp.where(parity(bits_col & (i_ref[0] ^ i_ref[1])) == 1, 0, 32)
    rank = rank + jnp.where(largest <= TIGHT, 0, 16)
    pick = jnp.min(jnp.where(good, rank.astype(F32), 99.0), axis=0, keepdims=True).astype(I32)
    branch = jnp.where(pick < 64, pick >> 4, jnp.where(l_ref[0] != l_ref[1], 4, 5))
    bits, side = (pick & 15) >> 1, pick & 1
    small = parity(bits & cls) == side
    group = jnp.zeros_like(cls)
    label = jnp.zeros_like(cls)
    lane_group = iota((1, width), 1) >> 5
    number = jnp.zeros((1, 1), I32)
    for g in range(8):
        is_small = parity(bits & g) == side
        group = group + jnp.where(is_small & (cls > g), 1, 0)
        label = label + jnp.where(is_small & (number == lane_group), g, 0)
        number = number + jnp.where(is_small, 1, 0)
    inner = one((iota((128, 128), 0) < iota((128, 128), 1)) & ((iota((128, 128), 0) >> 6) == (iota((128, 128), 1) >> 6)))
    small16 = jnp.broadcast_to(one(small), (16, width))
    ranks = [
        dot(small16[:, 128 * k : 128 * k + 128].astype(BF16), inner.astype(BF16))[0:1, :] for k in range(chunks)
    ]
    rank = jnp.concatenate(ranks, axis=1).astype(I32)
    none = jnp.full_like(cls, -1)
    table = jnp.concatenate(
        [
            cls,
            jnp.where(small, group * SLOTS + slot, none),
            jnp.where(small, slot, none),
            jnp.where(small, (iota((1, width), 1) >> 6) * RANKS + rank, none),
            label,
            jnp.where(small, rank, none),
            jnp.broadcast_to(branch, cls.shape),
            jnp.broadcast_to(bits, cls.shape),
        ],
        axis=0,
    )
    row_ref[...] = table
    table = table.astype(F32)
    for k in range(chunks):
        tile = jnp.concatenate([table[:, 128 * k : 128 * k + 128], jnp.zeros((120, 128), F32)], axis=0)
        col_ref[128 * k : 128 * k + 128, :] = jnp.transpose(tile).astype(I32)
    spots, numbers = places(row_ref)
    order_ref[...] = dot(spots, numbers, NT).astype(BF16)
    turn_ref[...] = dot(numbers, spots, NT).astype(BF16)
    panel_slots(row_ref, col_ref, chol_ref, l_ref, pos_ref, out_ref)


def own(col_ref, block, field):
    return col_ref[pl.ds(pl.multiple_of(block * 64, 64), 64), field : field + 1]


def panel_slots(row_ref, col_ref, chol_ref, l_ref, pos_ref, out_ref):
    cls = row_ref[CLS : CLS + 1, :]
    slot = row_ref[SLOT : SLOT + 1, :]
    own_cls = own(col_ref, pos_ref[0], CLS)
    pick = one(slot == iota((SLOTS, slot.shape[1]), 0)).astype(BF16)
    parts = []
    for n in range(2):
        kept = jnp.where((own_cls ^ cls) == l_ref[n], chol_ref[n], 0.0)
        high, low = split(kept)
        parts.append(dot(high, pick, NT) + dot(low, pick, NT))
    both = jnp.concatenate(parts, axis=1)
    packed = jnp.concatenate([both[0:32], both[32:64]], axis=1)
    out_ref[...] = jnp.broadcast_to(packed[None], out_ref.shape)


def unpack(gathered):
    n = gathered.shape[0]
    return jnp.concatenate([gathered, jnp.roll(gathered, 64, axis=2)], axis=1).reshape(n * 64, 128)


def places(row_ref):
    spot = row_ref[SPOT : SPOT + 1, :]
    number = row_ref[NUM : NUM + 1, :]
    width = spot.shape[1]
    spots = one(spot == iota((16 * RANKS, width), 0)).astype(BF16)
    numbers = one(number == iota((4 * SLOTS, width), 0)).astype(BF16)
    return spots, numbers


def ladder_kernel(count, row_ref, col_ref, order_ref, got_ref, mid_ref, i_ref, j_ref, l_ref, pos_ref, out_ref):
    p, q = pos_ref[0], pos_ref[1]
    cls = row_ref[CLS : CLS + 1, :]
    number = row_ref[NUM : NUM + 1, :]
    label = row_ref[LAB : LAB + 1, 0:128]
    bits = row_ref[BITS : BITS + 1, 0:1]
    label_col = col_ref[0:128, LAB : LAB + 1]
    width = cls.shape[1]
    turned = jnp.transpose(unpack(got_ref[...]))
    full = [
        jnp.where(label_col == (cls ^ l_ref[n]), jnp.concatenate([turned[32 * n : 32 * n + 32]] * 4, axis=0), 0.0)
        for n in range(2)
    ]
    full = split(jnp.concatenate(full + [one(number == iota((128, width), 0))], axis=0))
    rows, lates = receive(mid_ref, 128, 2 * RANKS, count)
    mids = [rows[:, 64 * i : 64 * i + 64].reshape(width, 128) for i in range(2)]
    core = dot3(full, split(jnp.concatenate(mids, axis=1)))
    order = order_ref[...]
    own_panel = unpack(got_ref[pl.ds(q, 1)])
    own_slot = own(col_ref, q, SLOT)
    own_rank = own(col_ref, q, RANK)
    own_cls = jnp.concatenate([own(col_ref, q, CLS)] * 4, axis=0)
    lane = iota((64, 128), 1)
    first_tile = jnp.concatenate([own_panel[:, 0:32]] * 4, axis=1)
    second_tile = jnp.concatenate([own_panel[:, 32:64]] * 4, axis=1)
    slot_tile = one(own_slot == (lane & 31))
    rank_pick = one(own_rank == lane).astype(BF16)
    lane_row = iota((1, 128), 1) >> 5
    results = []
    for i in range(2):
        xs = [i_ref[i] ^ j_ref[p * 4 + j] for j in range(4)]
        x_lane = jnp.zeros((1, 128), I32)
        x_row = jnp.zeros((256, 1), I32)
        for j in range(4):
            x_lane = jnp.where(lane_row == j, xs[j], x_lane)
            x_row = jnp.where((iota((256, 1), 0) >> 6) == j, xs[j], x_row)
        odd_lane = parity(x_lane & bits) == 1
        odd = [parity(bits & xs[j]) == 1 for j in range(4)]

        def blocks(tiles):
            return split(
                jnp.concatenate([jnp.where((lane >> 5) == j, tiles[j], 0.0) for j in range(4)], axis=0)
            )

        late = lates[:, RANKS * i : RANKS * (i + 1)]
        total = jnp.where(odd_lane, 0.0, jnp.sum(late, axis=0))
        late = jnp.where(odd_lane, late.reshape(16 * RANKS, 128), 0.0)
        lanes = slice(128 * i, 128 * i + 128)
        pick = core[256:384, lanes]
        pick2 = jnp.where(odd_lane, dot2(order, split(late)), pick)
        t1 = dot3(blocks([jnp.where(odd[j], slot_tile, first_tile) for j in range(4)]), split(pick), NT)
        t2 = dot3(blocks([jnp.where(odd[j], slot_tile, second_tile) for j in range(4)]), split(pick2), NT)
        t3 = dot3(blocks([first_tile] * 4), split(core[0:128, lanes]), NT)
        t3 = t3 + dot3(blocks([second_tile] * 4), split(core[128:256, lanes]), NT)
        total = jnp.concatenate([total, jnp.zeros((128 - RANKS, 128), F32)], axis=0)
        total = dot2(rank_pick, split(total))
        spread = [jnp.concatenate([total[:, 32 * j : 32 * j + 32]] * 4, axis=1) for j in range(4)]
        t3 = t3 + jnp.concatenate(spread, axis=0)
        goal = own_cls ^ x_row
        t1 = jnp.where(label == (goal ^ l_ref[0]), t1, 0.0)
        t2 = jnp.where(label == (goal ^ l_ref[1]), t2, 0.0)
        t3 = jnp.where(label == goal, t3, 0.0)
        results.append(jnp.concatenate([t1, t2, t3], axis=1))
    result = dot3(split(jnp.concatenate(results, axis=0)), full)
    for n in range(8):
        out_ref[n // 4, n % 4] = result[64 * n : 64 * n + 64]


def sent_rows(same, own_rows, count):
    return same + own_rows if count == SLOTS else -(-(same + own_rows) * count // SLOTS // 8) * 8


def send(out_ref, same, different, count):
    rows, late = same.shape[0], different.shape[1]
    if count == SLOTS:
        out_ref[:, 0:rows, :] = jnp.broadcast_to(same[None], (16, rows, 128))
        out_ref[:, rows : rows + late, :] = different
        return
    total = out_ref.shape[1]
    same = jnp.concatenate([same[:, 32 * j : 32 * j + count] for j in range(4)], axis=1)
    different = jnp.concatenate([different[:, :, 32 * j : 32 * j + count] for j in range(4)], axis=2)
    rest = rows - total
    side = [same[total:, 32 * k : 32 * k + 32] for k in range(3)] + [jnp.zeros((total - 3 * rest, 32), F32)]
    main = jnp.concatenate([same[0:total], jnp.concatenate(side, axis=0)], axis=1)
    out_ref[...] = jnp.broadcast_to(main[None], out_ref.shape)
    for k in range(3):
        start = 3 * rest + late * k
        out_ref[:, start : start + late, 96:128] = different[:, :, 32 * k : 32 * k + 32]


def receive(mid_ref, rows, late, count):
    if count == SLOTS:
        return mid_ref[:, 0:rows, :], mid_ref[:, rows : rows + late, :]
    total = mid_ref.shape[1]
    rest = rows - total

    def side(start, size):
        parts = [mid_ref[:, start + size * k : start + size * (k + 1), 96:128] for k in range(3)]
        return jnp.concatenate(parts, axis=2)

    def widen(x):
        gap = jnp.zeros((*x.shape[:2], 32 - count), F32)
        parts = []
        for j in range(4):
            parts += [x[:, :, count * j : count * j + count], gap]
        return jnp.concatenate(parts, axis=2)

    same = jnp.concatenate([mid_ref[:, :, 0:96], side(0, rest)], axis=1)
    return widen(same), widen(side(3 * rest, late))


def half_products(row_ref, col_ref, amp_ref, got_ref, i_ref, j_ref, pos_ref, high_ref, low_ref):
    p, q = pos_ref[0], pos_ref[1]
    cls = row_ref[CLS : CLS + 1, :]
    own_cls = own(col_ref, q, CLS)
    for n in range(8):
        kept = jnp.where((own_cls ^ cls) == (i_ref[n // 4] ^ j_ref[p * 4 + n % 4]), amp_ref[n // 4, n % 4], 0.0)
        high_ref[64 * n : 64 * n + 64, :], low_ref[64 * n : 64 * n + 64, :] = split(kept)
    panel = unpack(got_ref[...])
    lane = iota(panel.shape, 1)
    slot = col_ref[:, SLOT : SLOT + 1]
    wh, wl = split(jnp.where(lane < 64, panel, one(slot == lane - 64)))
    first = dot(high_ref[...], jnp.concatenate([wh, wl], axis=1))
    half = first[:, 0:128] + first[:, 128:256] + dot(low_ref[...], wh)
    return [half[64 * n : 64 * n + 64] for n in range(8)]


def left_factor(col_ref, got_ref, q):
    own_rank = own(col_ref, q, RANK)
    own_panel = unpack(got_ref[pl.ds(q, 1)])
    stacked = jnp.concatenate([own_panel[:, 0:32], own_panel[:, 32:64]], axis=0)
    ranks = jnp.concatenate([jnp.full_like(own_rank, -1), own_rank], axis=0)
    lane = iota((128, 128), 1)
    left = jnp.where(lane < 32, jnp.concatenate([stacked] * 4, axis=1), one(ranks == lane - 32))
    return jnp.transpose(jnp.where(lane < 48, left, 0.0))


def odd_even(row_ref, i_ref, j_ref, p):
    bits = row_ref[BITS : BITS + 1, 0:1]
    later = [parity(bits & (i_ref[1] ^ j_ref[p * 4 + j])) == 1 for j in range(4)]
    xs = [[jnp.where(later[j], i_ref[i] ^ j_ref[p * 4 + j], i_ref[1 - i] ^ j_ref[p * 4 + j]) for j in range(4)] for i in (1, 0)]
    return later, xs[0], xs[1]


def half_kernel(
    count, row_ref, col_ref, order_ref, amp_ref, got_ref, i_ref, j_ref, l_ref, pos_ref, out_ref, high_ref, low_ref
):
    p, q = pos_ref[0], pos_ref[1]
    label = row_ref[LAB : LAB + 1, 0:128]
    own_cls = own(col_ref, q, CLS)
    own_small = own(col_ref, q, NUM) >= 0
    xs = [i_ref[n // 4] ^ j_ref[p * 4 + n % 4] for n in range(8)]
    parts = half_products(row_ref, col_ref, amp_ref, got_ref, i_ref, j_ref, pos_ref, high_ref, low_ref)
    firsts = [part[:, 64:96] + jnp.where(own_small, part[:, 0:32], 0.0) for part in parts]
    left = left_factor(col_ref, got_ref, q)
    pair_cls = jnp.concatenate([own_cls ^ l_ref[0], own_cls ^ l_ref[1]], axis=0)
    both = [jnp.concatenate([part[:, 0:32], part[:, 32:64]], axis=0) for part in parts]
    spread = [
        jnp.where(label == (pair_cls ^ xs[n]), jnp.concatenate([both[n]] * 4, axis=1), 0.0) for n in range(8)
    ]
    sums = dot3(split(left[0:32]), split(jnp.concatenate(spread, axis=1)))
    seconds = dot2(left[32:48].astype(BF16), split(jnp.concatenate(both, axis=1)))
    order = order_ref[...]
    mains, lates = [], []
    for i in range(2):
        rows = jnp.concatenate([sums[:, 128 * n : 128 * n + 128] for n in range(4 * i, 4 * i + 4)], axis=0)
        by_spot = dot2(order, split(rows), NT).reshape(16, RANKS, 128)
        lates.append(by_spot + seconds[None, :, 128 * i : 128 * i + 128])
        mains.append(jnp.concatenate(firsts[4 * i : 4 * i + 4], axis=1))
    send(out_ref, jnp.concatenate(mains, axis=0), jnp.concatenate(lates, axis=1), count)


def half_paired_kernel(
    count, row_ref, col_ref, order_ref, amp_ref, got_ref, i_ref, j_ref, l_ref, pos_ref, out_ref, high_ref, low_ref
):
    p, q = pos_ref[0], pos_ref[1]
    label = row_ref[LAB : LAB + 1, 0:128]
    own_cls = own(col_ref, q, CLS)
    own_small = own(col_ref, q, NUM) >= 0
    parts = half_products(row_ref, col_ref, amp_ref, got_ref, i_ref, j_ref, pos_ref, high_ref, low_ref)
    later, _, even_x = odd_even(row_ref, i_ref, j_ref, p)
    odd = [jnp.where(later[j], parts[4 + j], parts[j]) for j in range(4)]
    even = [jnp.where(later[j], parts[j], parts[4 + j]) for j in range(4)]
    rows = jnp.concatenate([part[:, 64:96] + jnp.where(own_small, part[:, 0:32], 0.0) for part in odd], axis=1)
    left = left_factor(col_ref, got_ref, q)
    firsts = jnp.concatenate([part[:, 64:96] for part in even], axis=1)
    seconds = jnp.concatenate([part[:, 32:64] for part in odd], axis=1)
    few = jnp.concatenate([firsts, seconds], axis=1)
    few = dot2(left[32:48].astype(BF16), split(jnp.concatenate([few, few], axis=0)))
    pair_cls = jnp.concatenate([own_cls ^ l_ref[0], own_cls ^ l_ref[1]], axis=0)
    spread = []
    for j in range(4):
        both = jnp.concatenate([even[j][:, 0:32], even[j][:, 32:64]], axis=0)
        spread.append(jnp.where(label == (pair_cls ^ even_x[j]), jnp.concatenate([both] * 4, axis=1), 0.0))
    sums = dot3(split(left[0:32]), split(jnp.concatenate(spread, axis=1)))
    sums = jnp.concatenate([sums[:, 128 * j : 128 * j + 128] for j in range(4)], axis=0)
    order = order_ref[...]
    rows = jnp.concatenate([rows, few[:, 0:128], few[:, 128:256]], axis=0)
    send(out_ref, rows, dot2(order, split(sums), NT).reshape(16, RANKS, 128), count)


def ladder_paired_kernel(count, row_ref, col_ref, order_ref, got_ref, mid_ref, i_ref, j_ref, l_ref, pos_ref, out_ref):
    p, q = pos_ref[0], pos_ref[1]
    cls = row_ref[CLS : CLS + 1, :]
    number = row_ref[NUM : NUM + 1, :]
    label = row_ref[LAB : LAB + 1, 0:128]
    label_col = col_ref[0:128, LAB : LAB + 1]
    width = cls.shape[1]
    turned = jnp.transpose(unpack(got_ref[...]))
    full = [
        jnp.where(label_col == (cls ^ l_ref[n]), jnp.concatenate([turned[32 * n : 32 * n + 32]] * 4, axis=0), 0.0)
        for n in range(2)
    ]
    full = split(jnp.concatenate(full + [one(number == iota((128, width), 0))], axis=0))
    rows, sums = receive(mid_ref, 64 + 2 * RANKS, RANKS, count)
    core = dot3(full, split(rows[:, 0:64].reshape(width, 128)))
    order = order_ref[...]
    few = [rows[:, 64 + RANKS * k : 64 + RANKS * (k + 1)].reshape(16 * RANKS, 128) for k in range(2)]
    small_rows, second_rows = [dot2(order, split(few[k])) for k in range(2)]
    total = jnp.concatenate([jnp.sum(sums, axis=0), jnp.zeros((128 - RANKS, 128), F32)], axis=0)
    own_panel = unpack(got_ref[pl.ds(q, 1)])
    own_slot = own(col_ref, q, SLOT)
    own_rank = own(col_ref, q, RANK)
    own_cls = own(col_ref, q, CLS)
    lane = iota((64, 128), 1)

    def blocks(tile):
        return split(jnp.concatenate([jnp.where((lane >> 5) == j, tile, 0.0) for j in range(4)], axis=0))

    first = blocks(jnp.concatenate([own_panel[:, 0:32]] * 4, axis=1))
    second = blocks(jnp.concatenate([own_panel[:, 32:64]] * 4, axis=1))
    slots = blocks(one(own_slot == (lane & 31)))[0]
    total = dot2(one(own_rank == lane).astype(BF16), split(total))
    total = [jnp.concatenate([total[:, 32 * j : 32 * j + 32]] * 4, axis=1) for j in range(4)]
    odd = [
        dot2(slots, split(core[256:384]), NT),
        dot2(slots, split(second_rows), NT),
        dot3(first, split(core[0:128]), NT) + dot3(second, split(core[128:256]), NT),
    ]
    small_rows = split(small_rows)
    even = [dot3(first, small_rows, NT), dot3(second, small_rows, NT), jnp.concatenate(total, axis=0)]
    later, odd_x, even_x = odd_even(row_ref, i_ref, j_ref, p)
    rows = [None] * 8
    for j in range(4):
        kinds = []
        for parts, x in ((odd, odd_x[j]), (even, even_x[j])):
            goal = own_cls ^ x
            labels = (goal ^ l_ref[0], goal ^ l_ref[1], goal)
            kinds.append(
                jnp.concatenate(
                    [jnp.where(label == labels[k], parts[k][64 * j : 64 * j + 64], 0.0) for k in range(3)], axis=1
                )
            )
        rows[j] = jnp.where(later[j], kinds[1], kinds[0])
        rows[4 + j] = jnp.where(later[j], kinds[0], kinds[1])
    result = dot3(split(jnp.concatenate(rows, axis=0)), full)
    for n in range(8):
        out_ref[n // 4, n % 4] = result[64 * n : 64 * n + 64]


VMEM = pl.BlockSpec(memory_space=pltpu.VMEM)
SMEM = pl.BlockSpec(memory_space=pltpu.SMEM)
PARAMS = pltpu.CompilerParams(vmem_limit_bytes=48 * 1024 * 1024)


def shape(*dims, dtype=F32):
    return jax.ShapeDtypeStruct(dims, dtype)


def compact(kernels, same, late, count, row, col, order, turn, panel, amplitudes, irrep_i, irrep_j, irrep_l, pos):
    panel = lax.all_to_all(panel, "ja", split_axis=0, concat_axis=0, tiled=True)
    mid = pl.pallas_call(
        functools.partial(kernels[0], count),
        out_shape=shape(16, sent_rows(same, late, count), 128),
        in_specs=[VMEM] * 5 + [SMEM] * 4,
        out_specs=VMEM,
        scratch_shapes=[pltpu.VMEM((512, 1024), BF16), pltpu.VMEM((512, 1024), BF16)],
        compiler_params=PARAMS,
        name="half_slots",
    )(row, col, order, amplitudes, panel, irrep_i, irrep_j, irrep_l, pos)
    mid = lax.all_to_all(mid, "aa", split_axis=0, concat_axis=0, tiled=True)
    return pl.pallas_call(
        functools.partial(kernels[1], count),
        out_shape=shape(*amplitudes.shape),
        in_specs=[VMEM] * 5 + [SMEM] * 4,
        out_specs=VMEM,
        compiler_params=PARAMS,
        name="ladder_slots",
    )(row, col, turn, panel, mid, irrep_i, irrep_j, irrep_l, pos)


def panel_rows(half_ref, other_ref, core, high_ref, low_ref):
    for k in range(half_ref.shape[0]):
        for part, ref in ((core, half_ref), (1 - core, other_ref)):
            rows = pl.ds(pl.multiple_of((2 * k + part) * 64, 64), 64)
            high_ref[rows, :], low_ref[rows, :] = split(ref[k])


def dense_half_kernel(
    row_ref, col_ref, amp_ref, half_ref, other_ref, i_ref, j_ref, pos_ref, out_ref, ph_ref, pl_ref, high_ref, low_ref
):
    p, q = pos_ref[0], pos_ref[1]
    panel_rows(half_ref, other_ref, p & 1, ph_ref, pl_ref)
    cls = row_ref[CLS : CLS + 1, :]
    own_cls = own(col_ref, q, CLS)
    for n in range(8):
        kept = jnp.where((own_cls ^ cls) == (i_ref[n // 4] ^ j_ref[p * 4 + n % 4]), amp_ref[n // 4, n % 4], 0.0)
        high_ref[64 * n : 64 * n + 64, :], low_ref[64 * n : 64 * n + 64, :] = split(kept)
    result = dot3((ph_ref[...], pl_ref[...]), (high_ref[...], low_ref[...]), NT)
    out_ref[...] = result.reshape(out_ref.shape)


def dense_ladder_kernel(
    row_ref, col_ref, mid_ref, half_ref, other_ref, i_ref, j_ref, pos_ref, out_ref, ph_ref, pl_ref, high_ref, low_ref
):
    p, q = pos_ref[0], pos_ref[1]
    panel_rows(half_ref, other_ref, p & 1, ph_ref, pl_ref)
    first = iota((64, 128), 1) < 64
    for n in range(8):
        lanes = slice(128 * (n // 2), 128 * (n // 2) + 128)
        for s in range(0, 16, 2):
            a, b = mid_ref[s, :, lanes], mid_ref[s + 1, :, lanes]
            both = jnp.where(first, a, jnp.roll(b, 64, axis=1)) if n % 2 == 0 else jnp.where(first, jnp.roll(a, 64, axis=1), b)
            place = (slice(64 * n, 64 * n + 64), slice(64 * s, 64 * s + 128))
            high_ref[place], low_ref[place] = split(both)
    result = dot3((high_ref[...], low_ref[...]), (ph_ref[...], pl_ref[...]))
    pair_cls = own(col_ref, q, CLS) ^ row_ref[CLS : CLS + 1, :]
    for n in range(8):
        x = i_ref[n // 4] ^ j_ref[p * 4 + n % 4]
        out_ref[n // 4, n % 4] = jnp.where(pair_cls == x, result[64 * n : 64 * n + 64], 0.0)


CORES = [[2 * k + core for k in range(8)] for core in (0, 1)]


def dense(row, col, amplitudes, panel, irrep_i, irrep_j, pos):
    half = jnp.broadcast_to(panel[None], (8, *panel.shape))
    half = lax.all_to_all(half, "ja", split_axis=0, concat_axis=0, tiled=True, axis_index_groups=CORES)
    other = lax.ppermute(half, "ja", [(n, n ^ 1) for n in range(16)])
    halves = [pltpu.VMEM((1024, 1024), BF16)] * 2 + [pltpu.VMEM((512, 1024), BF16)] * 2
    mid = pl.pallas_call(
        dense_half_kernel,
        out_shape=shape(16, 64, 512),
        in_specs=[VMEM] * 5 + [SMEM] * 3,
        out_specs=VMEM,
        scratch_shapes=halves,
        compiler_params=PARAMS,
        name="half_dense",
    )(row, col, amplitudes, half, other, irrep_i, irrep_j, pos)
    mid = lax.all_to_all(mid, "aa", split_axis=0, concat_axis=0, tiled=True)
    return pl.pallas_call(
        dense_ladder_kernel,
        out_shape=shape(*amplitudes.shape),
        in_specs=[VMEM] * 5 + [SMEM] * 3,
        out_specs=VMEM,
        scratch_shapes=halves,
        compiler_params=PARAMS,
        name="ladder_dense",
    )(row, col, mid, half, other, irrep_i, irrep_j, pos)


def local(amplitudes, chol, irrep_i, irrep_j, irrep_v, irrep_l):
    pos = jnp.stack([lax.axis_index("ja"), lax.axis_index("aa")]).astype(I32)
    width = irrep_v.shape[0]
    row, col, order, turn, slots = pl.pallas_call(
        table_kernel,
        out_shape=(
            shape(8, width, dtype=I32),
            shape(width, 128, dtype=I32),
            shape(16 * RANKS, 4 * SLOTS, dtype=BF16),
            shape(4 * SLOTS, 16 * RANKS, dtype=BF16),
            shape(16, 32, 128),
        ),
        in_specs=[VMEM, VMEM, SMEM, SMEM, SMEM],
        out_specs=(VMEM,) * 5,
        compiler_params=PARAMS,
        name="orbital_table",
    )(irrep_v.reshape(1, width), chol, irrep_i, irrep_l, pos)
    height = chol.shape[1]

    def panels():
        own_rows = lax.dynamic_slice_in_dim(irrep_v, pos[0] * height, height)
        pair = own_rows[:, None] ^ irrep_v[None, :]
        return [jnp.where(pair == irrep_l[n], chol[n], 0.0) for n in range(2)]

    def run(panel):
        return dense(row, col, amplitudes, panel, irrep_i, irrep_j, pos)

    def together():
        first, second = panels()
        return run(first + second)

    def apart():
        first, second = panels()
        return run(first) + run(second)

    few = (row, col, order, turn, slots, amplitudes, irrep_i, irrep_j, irrep_l, pos)
    paired = ((half_paired_kernel, ladder_paired_kernel), 64 + 2 * RANKS, RANKS)
    general = ((half_kernel, ladder_kernel), 128, 2 * RANKS)
    return lax.switch(
        row[BRANCH, 0],
        [
            lambda: compact(*paired, TIGHT, *few),
            lambda: compact(*paired, SLOTS, *few),
            lambda: compact(*general, TIGHT, *few),
            lambda: compact(*general, SLOTS, *few),
            together,
            apart,
        ],
    )


def solution(mesh):
    in_specs = (P(None, "ja", "aa", None), P(None, "ja", None), P(), P(), P(), P())
    out_specs = P(None, "ja", "aa", None)
    return jax.shard_map(local, mesh=mesh, in_specs=in_specs, out_specs=out_specs, check_vma=False)
```

```python
import functools

import jax
import jax.numpy as jnp
from jax import lax
from jax.experimental import pallas as pl
from jax.experimental.pallas import tpu as pltpu
from jax.sharding import PartitionSpec as P

F32, BF16, I32 = jnp.float32, jnp.bfloat16, jnp.int32
NN = (((1,), (0,)), ((), ()))
NT = (((1,), (1,)), ((), ()))
SLOTS = 32
TIGHT = 24
RANKS = 16
CLS, NUM, SLOT, SPOT, LAB, RANK, BRANCH, BITS = range(8)


def iota(shape, dim):
    return lax.broadcasted_iota(I32, shape, dim)


def parity(x):
    return (x ^ (x >> 1) ^ (x >> 2)) & 1


def one(cond):
    return jnp.where(cond, 1.0, 0.0).astype(F32)


def dot(a, b, dims=NN):
    return lax.dot_general(a, b, dims, preferred_element_type=F32)


def split(x):
    high = x.astype(BF16)
    return high, (x - high.astype(F32)).astype(BF16)


def dot3(a, b, dims=NN):
    (ah, al), (bh, bl) = a, b
    return dot(ah, bh, dims) + dot(ah, bl, dims) + dot(al, bh, dims)


def dot2(a, b, dims=NN):
    return dot(a, b[0], dims) + dot(a, b[1], dims)


def table_kernel(irrep_ref, chol_ref, i_ref, l_ref, pos_ref, row_ref, col_ref, order_ref, turn_ref, out_ref):
    cls = irrep_ref[...]
    width = cls.shape[1]
    chunks = width // 128
    onehot = one(cls == iota((16, width), 0))
    before = one(iota((128, 128), 0) < iota((128, 128), 1))
    count = jnp.zeros((16, 1), F32)
    blocks = jnp.zeros((16, 128), F32)
    slots = []
    for k in range(chunks):
        part = onehot[:, 128 * k : 128 * k + 128]
        ahead = dot(part.astype(BF16), before.astype(BF16)) + count
        slots.append(jnp.sum(part * ahead, axis=0, keepdims=True))
        count = count + jnp.sum(part, axis=1, keepdims=True)
        place = one(iota((128, 128), 1) == 2 * k + (iota((128, 128), 0) >> 6))
        blocks = blocks + dot(part.astype(BF16), place.astype(BF16))
    slot = jnp.concatenate(slots, axis=1).astype(I32)
    lane = iota((16, 128), 1)
    cand = iota((16, 128), 0)
    count_lane = jnp.sum(jnp.where(lane == cand, count, 0.0), axis=0, keepdims=True)
    member = (parity((cand >> 1) & lane) == (cand & 1)) & (lane < 8)
    largest = jnp.max(jnp.where(member, count_lane, 0.0), axis=1, keepdims=True)
    in_block = jnp.zeros((16, 128), F32)
    for g in range(8):
        in_block = in_block + jnp.where(parity((cand >> 1) & g) == (cand & 1), blocks[g : g + 1, :], 0.0)
    fullest = jnp.max(in_block, axis=1, keepdims=True)
    bits_col = cand[:, 0:1] >> 1
    good = (largest <= SLOTS) & (fullest <= RANKS)
    for n in range(l_ref.shape[0]):
        good = good & (parity(bits_col & l_ref[n]) == 1)
    paired = parity(bits_col & (i_ref[0] ^ i_ref[1])) == 1
    rank = cand[:, 0:1] + jnp.where(largest <= TIGHT, jnp.where(paired, 0, 16), 32)
    pick = jnp.min(jnp.where(good, rank.astype(F32), 99.0), axis=0, keepdims=True).astype(I32)
    branch = jnp.where(pick < 48, pick >> 4, 3)
    bits, side = (pick & 15) >> 1, pick & 1
    small = parity(bits & cls) == side
    group = jnp.zeros_like(cls)
    label = jnp.zeros_like(cls)
    lane_group = iota((1, width), 1) >> 5
    number = jnp.zeros((1, 1), I32)
    for g in range(8):
        is_small = parity(bits & g) == side
        group = group + jnp.where(is_small & (cls > g), 1, 0)
        label = label + jnp.where(is_small & (number == lane_group), g, 0)
        number = number + jnp.where(is_small, 1, 0)
    inner = one((iota((128, 128), 0) < iota((128, 128), 1)) & ((iota((128, 128), 0) >> 6) == (iota((128, 128), 1) >> 6)))
    small16 = jnp.broadcast_to(one(small), (16, width))
    ranks = [
        dot(small16[:, 128 * k : 128 * k + 128].astype(BF16), inner.astype(BF16))[0:1, :] for k in range(chunks)
    ]
    rank = jnp.concatenate(ranks, axis=1).astype(I32)
    none = jnp.full_like(cls, -1)
    table = jnp.concatenate(
        [
            cls,
            jnp.where(small, group * SLOTS + slot, none),
            jnp.where(small, slot, none),
            jnp.where(small, (iota((1, width), 1) >> 6) * RANKS + rank, none),
            label,
            jnp.where(small, rank, none),
            jnp.broadcast_to(branch, cls.shape),
            jnp.broadcast_to(bits, cls.shape),
        ],
        axis=0,
    )
    row_ref[...] = table
    table = table.astype(F32)
    for k in range(chunks):
        tile = jnp.concatenate([table[:, 128 * k : 128 * k + 128], jnp.zeros((120, 128), F32)], axis=0)
        col_ref[128 * k : 128 * k + 128, :] = jnp.transpose(tile).astype(I32)
    spots, numbers = places(row_ref)
    order_ref[...] = dot(spots, numbers, NT).astype(BF16)
    turn_ref[...] = dot(numbers, spots, NT).astype(BF16)
    panel_slots(row_ref, col_ref, chol_ref, l_ref, pos_ref, out_ref)


def own(col_ref, block, field):
    return col_ref[pl.ds(pl.multiple_of(block * 64, 64), 64), field : field + 1]


def panel_slots(row_ref, col_ref, chol_ref, l_ref, pos_ref, out_ref):
    cls = row_ref[CLS : CLS + 1, :]
    slot = row_ref[SLOT : SLOT + 1, :]
    own_cls = own(col_ref, pos_ref[0], CLS)
    pick = one(slot == iota((SLOTS, slot.shape[1]), 0)).astype(BF16)
    parts = []
    for n in range(2):
        kept = jnp.where((own_cls ^ cls) == l_ref[n], chol_ref[n], 0.0)
        high, low = split(kept)
        parts.append(dot(high, pick, NT) + dot(low, pick, NT))
    both = jnp.concatenate(parts, axis=1)
    packed = jnp.concatenate([both[0:32], both[32:64]], axis=1)
    out_ref[...] = jnp.broadcast_to(packed[None], out_ref.shape)


def unpack(gathered):
    n = gathered.shape[0]
    return jnp.concatenate([gathered, jnp.roll(gathered, 64, axis=2)], axis=1).reshape(n * 64, 128)


def places(row_ref):
    spot = row_ref[SPOT : SPOT + 1, :]
    number = row_ref[NUM : NUM + 1, :]
    width = spot.shape[1]
    spots = one(spot == iota((16 * RANKS, width), 0)).astype(BF16)
    numbers = one(number == iota((4 * SLOTS, width), 0)).astype(BF16)
    return spots, numbers


def finish(left, full, out_ref, left_ref):
    left_ref[...] = left

    @pl.loop(0, 2)
    def _(i):
        rows = pl.ds(pl.multiple_of(256 * i, 256), 256)
        out_ref[i] = dot3(split(left_ref[rows, :]), full).reshape(4, 64, full[0].shape[1])


def ladder_kernel(
    count, row_ref, col_ref, order_ref, got_ref, mid_ref, i_ref, j_ref, l_ref, pos_ref, out_ref, left_ref
):
    p, q = pos_ref[0], pos_ref[1]
    cls = row_ref[CLS : CLS + 1, :]
    number = row_ref[NUM : NUM + 1, :]
    label = row_ref[LAB : LAB + 1, 0:128]
    bits = row_ref[BITS : BITS + 1, 0:1]
    label_col = col_ref[0:128, LAB : LAB + 1]
    width = cls.shape[1]
    turned = jnp.transpose(unpack(got_ref[...]))
    full = [
        jnp.where(label_col == (cls ^ l_ref[n]), jnp.concatenate([turned[32 * n : 32 * n + 32]] * 4, axis=0), 0.0)
        for n in range(2)
    ]
    full = split(jnp.concatenate(full + [one(number == iota((128, width), 0))], axis=0))
    rows, lates = receive(mid_ref, 128, 2 * RANKS, count)
    mids = [rows[:, 64 * i : 64 * i + 64].reshape(width, 128) for i in range(2)]
    core = dot3(full, split(jnp.concatenate(mids, axis=1)))
    order = order_ref[...]
    own_panel = unpack(got_ref[pl.ds(q, 1)])
    own_slot = own(col_ref, q, SLOT)
    own_rank = own(col_ref, q, RANK)
    own_cls = jnp.concatenate([own(col_ref, q, CLS)] * 4, axis=0)
    lane = iota((64, 128), 1)
    first_tile = jnp.concatenate([own_panel[:, 0:32]] * 4, axis=1)
    second_tile = jnp.concatenate([own_panel[:, 32:64]] * 4, axis=1)
    slot_tile = one(own_slot == (lane & 31))
    rank_pick = one(own_rank == lane).astype(BF16)
    lane_row = iota((1, 128), 1) >> 5
    results = []
    for i in range(2):
        xs = [i_ref[i] ^ j_ref[p * 4 + j] for j in range(4)]
        x_lane = jnp.zeros((1, 128), I32)
        x_row = jnp.zeros((256, 1), I32)
        for j in range(4):
            x_lane = jnp.where(lane_row == j, xs[j], x_lane)
            x_row = jnp.where((iota((256, 1), 0) >> 6) == j, xs[j], x_row)
        odd_lane = parity(x_lane & bits) == 1
        odd = [parity(bits & xs[j]) == 1 for j in range(4)]

        def blocks(tiles):
            return split(
                jnp.concatenate([jnp.where((lane >> 5) == j, tiles[j], 0.0) for j in range(4)], axis=0)
            )

        late = lates[:, RANKS * i : RANKS * (i + 1)]
        total = jnp.where(odd_lane, 0.0, jnp.sum(late, axis=0))
        late = jnp.where(odd_lane, late.reshape(16 * RANKS, 128), 0.0)
        lanes = slice(128 * i, 128 * i + 128)
        pick = core[256:384, lanes]
        pick2 = jnp.where(odd_lane, dot2(order, split(late)), pick)
        t1 = dot3(blocks([jnp.where(odd[j], slot_tile, first_tile) for j in range(4)]), split(pick), NT)
        t2 = dot3(blocks([jnp.where(odd[j], slot_tile, second_tile) for j in range(4)]), split(pick2), NT)
        t3 = dot3(blocks([first_tile] * 4), split(core[0:128, lanes]), NT)
        t3 = t3 + dot3(blocks([second_tile] * 4), split(core[128:256, lanes]), NT)
        total = jnp.concatenate([total, jnp.zeros((128 - RANKS, 128), F32)], axis=0)
        total = dot2(rank_pick, split(total))
        spread = [jnp.concatenate([total[:, 32 * j : 32 * j + 32]] * 4, axis=1) for j in range(4)]
        t3 = t3 + jnp.concatenate(spread, axis=0)
        goal = own_cls ^ x_row
        t1 = jnp.where(label == (goal ^ l_ref[0]), t1, 0.0)
        t2 = jnp.where(label == (goal ^ l_ref[1]), t2, 0.0)
        t3 = jnp.where(label == goal, t3, 0.0)
        results.append(jnp.concatenate([t1, t2, t3], axis=1))
    finish(jnp.concatenate(results, axis=0), full, out_ref, left_ref)


def sent_rows(same, own_rows, count):
    return same + own_rows if count == SLOTS else -(-(same + own_rows) * count // SLOTS // 8) * 8


def send(out_ref, same, different, count):
    rows, late = same.shape[0], different.shape[1]
    if count == SLOTS:
        out_ref[:, 0:rows, :] = jnp.broadcast_to(same[None], (16, rows, 128))
        out_ref[:, rows : rows + late, :] = different
        return
    total = out_ref.shape[1]
    same = jnp.concatenate([same[:, 32 * j : 32 * j + count] for j in range(4)], axis=1)
    different = jnp.concatenate([different[:, :, 32 * j : 32 * j + count] for j in range(4)], axis=2)
    rest = rows - total
    side = [same[total:, 32 * k : 32 * k + 32] for k in range(3)] + [jnp.zeros((total - 3 * rest, 32), F32)]
    main = jnp.concatenate([same[0:total], jnp.concatenate(side, axis=0)], axis=1)
    out_ref[...] = jnp.broadcast_to(main[None], out_ref.shape)
    for k in range(3):
        start = 3 * rest + late * k
        out_ref[:, start : start + late, 96:128] = different[:, :, 32 * k : 32 * k + 32]


def receive(mid_ref, rows, late, count):
    if count == SLOTS:
        return mid_ref[:, 0:rows, :], mid_ref[:, rows : rows + late, :]
    total = mid_ref.shape[1]
    rest = rows - total

    def side(start, size):
        parts = [mid_ref[:, start + size * k : start + size * (k + 1), 96:128] for k in range(3)]
        return jnp.concatenate(parts, axis=2)

    def widen(x):
        gap = jnp.zeros((*x.shape[:2], 32 - count), F32)
        parts = []
        for j in range(4):
            parts += [x[:, :, count * j : count * j + count], gap]
        return jnp.concatenate(parts, axis=2)

    same = jnp.concatenate([mid_ref[:, :, 0:96], side(0, rest)], axis=1)
    return widen(same), widen(side(3 * rest, late))


def half_products(row_ref, col_ref, amp_ref, got_ref, i_ref, j_ref, pos_ref, half_ref):
    p, q = pos_ref[0], pos_ref[1]
    cls = row_ref[CLS : CLS + 1, :]
    own_cls = own(col_ref, q, CLS)
    panel = unpack(got_ref[...])
    lane = iota(panel.shape, 1)
    slot = col_ref[:, SLOT : SLOT + 1]
    wh, wl = split(jnp.where(lane < 64, panel, one(slot == lane - 64)))
    both = jnp.concatenate([wh, wl], axis=1)
    pair_cls = own_cls ^ cls

    @pl.loop(0, 2)
    def _(i):
        kept = [jnp.where(pair_cls == (i_ref[i] ^ j_ref[p * 4 + j]), amp_ref[i, j], 0.0) for j in range(4)]
        high, low = split(jnp.concatenate(kept, axis=0))
        first = dot(high, both)
        rows = pl.ds(pl.multiple_of(256 * i, 256), 256)
        half_ref[rows, :] = first[:, 0:128] + first[:, 128:256] + dot(low, wh)

    return [half_ref[64 * n : 64 * n + 64, :] for n in range(8)]


def left_factor(col_ref, got_ref, q):
    own_rank = own(col_ref, q, RANK)
    own_panel = unpack(got_ref[pl.ds(q, 1)])
    stacked = jnp.concatenate([own_panel[:, 0:32], own_panel[:, 32:64]], axis=0)
    ranks = jnp.concatenate([jnp.full_like(own_rank, -1), own_rank], axis=0)
    lane = iota((128, 128), 1)
    left = jnp.where(lane < 32, jnp.concatenate([stacked] * 4, axis=1), one(ranks == lane - 32))
    return jnp.transpose(jnp.where(lane < 48, left, 0.0))


def odd_even(row_ref, i_ref, j_ref, p):
    bits = row_ref[BITS : BITS + 1, 0:1]
    later = [parity(bits & (i_ref[1] ^ j_ref[p * 4 + j])) == 1 for j in range(4)]
    xs = [[jnp.where(later[j], i_ref[i] ^ j_ref[p * 4 + j], i_ref[1 - i] ^ j_ref[p * 4 + j]) for j in range(4)] for i in (1, 0)]
    return later, xs[0], xs[1]


def half_kernel(
    count, row_ref, col_ref, order_ref, amp_ref, got_ref, i_ref, j_ref, l_ref, pos_ref, out_ref, half_ref
):
    p, q = pos_ref[0], pos_ref[1]
    label = row_ref[LAB : LAB + 1, 0:128]
    own_cls = own(col_ref, q, CLS)
    own_small = own(col_ref, q, NUM) >= 0
    xs = [i_ref[n // 4] ^ j_ref[p * 4 + n % 4] for n in range(8)]
    parts = half_products(row_ref, col_ref, amp_ref, got_ref, i_ref, j_ref, pos_ref, half_ref)
    firsts = [part[:, 64:96] + jnp.where(own_small, part[:, 0:32], 0.0) for part in parts]
    left = left_factor(col_ref, got_ref, q)
    pair_cls = jnp.concatenate([own_cls ^ l_ref[0], own_cls ^ l_ref[1]], axis=0)
    both = [jnp.concatenate([part[:, 0:32], part[:, 32:64]], axis=0) for part in parts]
    spread = [
        jnp.where(label == (pair_cls ^ xs[n]), jnp.concatenate([both[n]] * 4, axis=1), 0.0) for n in range(8)
    ]
    sums = dot3(split(left[0:32]), split(jnp.concatenate(spread, axis=1)))
    seconds = dot2(left[32:48].astype(BF16), split(jnp.concatenate(both, axis=1)))
    order = order_ref[...]
    mains, lates = [], []
    for i in range(2):
        rows = jnp.concatenate([sums[:, 128 * n : 128 * n + 128] for n in range(4 * i, 4 * i + 4)], axis=0)
        by_spot = dot2(order, split(rows), NT).reshape(16, RANKS, 128)
        lates.append(by_spot + seconds[None, :, 128 * i : 128 * i + 128])
        mains.append(jnp.concatenate(firsts[4 * i : 4 * i + 4], axis=1))
    send(out_ref, jnp.concatenate(mains, axis=0), jnp.concatenate(lates, axis=1), count)


def half_paired_kernel(
    count, row_ref, col_ref, order_ref, amp_ref, got_ref, i_ref, j_ref, l_ref, pos_ref, out_ref, half_ref
):
    p, q = pos_ref[0], pos_ref[1]
    label = row_ref[LAB : LAB + 1, 0:128]
    own_cls = own(col_ref, q, CLS)
    own_small = own(col_ref, q, NUM) >= 0
    parts = half_products(row_ref, col_ref, amp_ref, got_ref, i_ref, j_ref, pos_ref, half_ref)
    later, _, even_x = odd_even(row_ref, i_ref, j_ref, p)
    odd = [jnp.where(later[j], parts[4 + j], parts[j]) for j in range(4)]
    even = [jnp.where(later[j], parts[j], parts[4 + j]) for j in range(4)]
    rows = jnp.concatenate([part[:, 64:96] + jnp.where(own_small, part[:, 0:32], 0.0) for part in odd], axis=1)
    left = left_factor(col_ref, got_ref, q)
    firsts = jnp.concatenate([part[:, 64:96] for part in even], axis=1)
    seconds = jnp.concatenate([part[:, 32:64] for part in odd], axis=1)
    few = jnp.concatenate([firsts, seconds], axis=1)
    few = dot2(left[32:48].astype(BF16), split(jnp.concatenate([few, few], axis=0)))
    pair_cls = jnp.concatenate([own_cls ^ l_ref[0], own_cls ^ l_ref[1]], axis=0)
    spread = []
    for j in range(4):
        both = jnp.concatenate([even[j][:, 0:32], even[j][:, 32:64]], axis=0)
        spread.append(jnp.where(label == (pair_cls ^ even_x[j]), jnp.concatenate([both] * 4, axis=1), 0.0))
    sums = dot3(split(left[0:32]), split(jnp.concatenate(spread, axis=1)))
    sums = jnp.concatenate([sums[:, 128 * j : 128 * j + 128] for j in range(4)], axis=0)
    order = order_ref[...]
    rows = jnp.concatenate([rows, few[:, 0:128], few[:, 128:256]], axis=0)
    send(out_ref, rows, dot2(order, split(sums), NT).reshape(16, RANKS, 128), count)


def ladder_paired_kernel(
    count, row_ref, col_ref, order_ref, got_ref, mid_ref, i_ref, j_ref, l_ref, pos_ref, out_ref, left_ref
):
    p, q = pos_ref[0], pos_ref[1]
    cls = row_ref[CLS : CLS + 1, :]
    number = row_ref[NUM : NUM + 1, :]
    label = row_ref[LAB : LAB + 1, 0:128]
    label_col = col_ref[0:128, LAB : LAB + 1]
    width = cls.shape[1]
    turned = jnp.transpose(unpack(got_ref[...]))
    full = [
        jnp.where(label_col == (cls ^ l_ref[n]), jnp.concatenate([turned[32 * n : 32 * n + 32]] * 4, axis=0), 0.0)
        for n in range(2)
    ]
    full = split(jnp.concatenate(full + [one(number == iota((128, width), 0))], axis=0))
    rows, sums = receive(mid_ref, 64 + 2 * RANKS, RANKS, count)
    core = dot3(full, split(rows[:, 0:64].reshape(width, 128)))
    order = order_ref[...]
    few = [rows[:, 64 + RANKS * k : 64 + RANKS * (k + 1)].reshape(16 * RANKS, 128) for k in range(2)]
    small_rows, second_rows = [dot2(order, split(few[k])) for k in range(2)]
    total = jnp.concatenate([jnp.sum(sums, axis=0), jnp.zeros((128 - RANKS, 128), F32)], axis=0)
    own_panel = unpack(got_ref[pl.ds(q, 1)])
    own_slot = own(col_ref, q, SLOT)
    own_rank = own(col_ref, q, RANK)
    own_cls = own(col_ref, q, CLS)
    lane = iota((64, 128), 1)

    def blocks(tile):
        return split(jnp.concatenate([jnp.where((lane >> 5) == j, tile, 0.0) for j in range(4)], axis=0))

    first = blocks(jnp.concatenate([own_panel[:, 0:32]] * 4, axis=1))
    second = blocks(jnp.concatenate([own_panel[:, 32:64]] * 4, axis=1))
    slots = blocks(one(own_slot == (lane & 31)))[0]
    total = dot2(one(own_rank == lane).astype(BF16), split(total))
    total = [jnp.concatenate([total[:, 32 * j : 32 * j + 32]] * 4, axis=1) for j in range(4)]
    odd = [
        dot2(slots, split(core[256:384]), NT),
        dot2(slots, split(second_rows), NT),
        dot3(first, split(core[0:128]), NT) + dot3(second, split(core[128:256]), NT),
    ]
    small_rows = split(small_rows)
    even = [dot3(first, small_rows, NT), dot3(second, small_rows, NT), jnp.concatenate(total, axis=0)]
    later, odd_x, even_x = odd_even(row_ref, i_ref, j_ref, p)
    rows = [None] * 8
    for j in range(4):
        kinds = []
        for parts, x in ((odd, odd_x[j]), (even, even_x[j])):
            goal = own_cls ^ x
            labels = (goal ^ l_ref[0], goal ^ l_ref[1], goal)
            kinds.append(
                jnp.concatenate(
                    [jnp.where(label == labels[k], parts[k][64 * j : 64 * j + 64], 0.0) for k in range(3)], axis=1
                )
            )
        rows[j] = jnp.where(later[j], kinds[1], kinds[0])
        rows[4 + j] = jnp.where(later[j], kinds[0], kinds[1])
    finish(jnp.concatenate(rows, axis=0), full, out_ref, left_ref)


VMEM = pl.BlockSpec(memory_space=pltpu.VMEM)
SMEM = pl.BlockSpec(memory_space=pltpu.SMEM)
PARAMS = pltpu.CompilerParams(vmem_limit_bytes=48 * 1024 * 1024)


def shape(*dims, dtype=F32):
    return jax.ShapeDtypeStruct(dims, dtype)


def compact(kernels, same, late, count, row, col, order, turn, panel, amplitudes, irrep_i, irrep_j, irrep_l, pos):
    panel = lax.all_to_all(panel, "ja", split_axis=0, concat_axis=0, tiled=True)
    mid = pl.pallas_call(
        functools.partial(kernels[0], count),
        out_shape=shape(16, sent_rows(same, late, count), 128),
        in_specs=[VMEM] * 5 + [SMEM] * 4,
        out_specs=VMEM,
        scratch_shapes=[pltpu.VMEM((512, 128), F32)],
        compiler_params=PARAMS,
        name="half_slots",
    )(row, col, order, amplitudes, panel, irrep_i, irrep_j, irrep_l, pos)
    mid = lax.all_to_all(mid, "aa", split_axis=0, concat_axis=0, tiled=True)
    return pl.pallas_call(
        functools.partial(kernels[1], count),
        out_shape=shape(*amplitudes.shape),
        in_specs=[VMEM] * 5 + [SMEM] * 4,
        out_specs=VMEM,
        scratch_shapes=[pltpu.VMEM((512, 12 * SLOTS), F32)],
        compiler_params=PARAMS,
        name="ladder_slots",
    )(row, col, turn, panel, mid, irrep_i, irrep_j, irrep_l, pos)


def panel_rows(half_ref, other_ref, core, high_ref, low_ref):
    @pl.loop(0, half_ref.shape[0])
    def _(k):
        for part, ref in ((core, half_ref), (1 - core, other_ref)):
            rows = pl.ds(pl.multiple_of((2 * k + part) * 64, 64), 64)
            high_ref[rows, :], low_ref[rows, :] = split(ref[k])


def dense_half_kernel(
    row_ref, col_ref, amp_ref, half_ref, other_ref, i_ref, j_ref, pos_ref, out_ref, ph_ref, pl_ref, high_ref, low_ref
):
    p, q = pos_ref[0], pos_ref[1]
    panel_rows(half_ref, other_ref, p & 1, ph_ref, pl_ref)
    pair_cls = own(col_ref, q, CLS) ^ row_ref[CLS : CLS + 1, :]

    @pl.loop(0, 8)
    def _(n):
        i, j = n >> 2, n & 3
        kept = jnp.where(pair_cls == (i_ref[i] ^ j_ref[p * 4 + j]), amp_ref[i, j], 0.0)
        rows = pl.ds(pl.multiple_of(64 * n, 64), 64)
        high_ref[rows, :], low_ref[rows, :] = split(kept)

    @pl.loop(0, 2)
    def _(k):
        rows = pl.ds(pl.multiple_of(512 * k, 512), 512)
        result = dot3((ph_ref[rows, :], pl_ref[rows, :]), (high_ref[...], low_ref[...]), NT)
        out_ref[pl.ds(8 * k, 8)] = result.reshape(8, 64, 512)


def dense_ladder_kernel(
    row_ref, col_ref, acc_ref, mid_ref, half_ref, other_ref, i_ref, j_ref, pos_ref, out_ref, ph_ref, pl_ref, high_ref, low_ref
):
    p, q = pos_ref[0], pos_ref[1]
    panel_rows(half_ref, other_ref, p & 1, ph_ref, pl_ref)
    first = iota((64, 128), 1) < 64

    for s in range(0, 16, 2):

        @pl.loop(0, 4)
        def _(k):
            lanes = pl.ds(pl.multiple_of(128 * k, 128), 128)
            a, b = mid_ref[s, :, lanes], mid_ref[s + 1, :, lanes]
            left = split(jnp.where(first, a, jnp.roll(b, 64, axis=1)))
            right = split(jnp.where(first, jnp.roll(a, 64, axis=1), b))
            for n, pair in ((0, left), (1, right)):
                rows = pl.ds(pl.multiple_of(128 * k + 64 * n, 64), 64)
                high_ref[rows, 64 * s : 64 * s + 128], low_ref[rows, 64 * s : 64 * s + 128] = pair

    pair_cls = own(col_ref, q, CLS) ^ row_ref[CLS : CLS + 1, :]

    @pl.loop(0, 2)
    def _(i):
        rows = pl.ds(pl.multiple_of(256 * i, 256), 256)
        result = dot3((high_ref[rows, :], low_ref[rows, :]), (ph_ref[...], pl_ref[...]))
        for j in range(4):
            x = i_ref[i] ^ j_ref[p * 4 + j]
            out_ref[i, j] = acc_ref[i, j] + jnp.where(pair_cls == x, result[64 * j : 64 * j + 64], 0.0)


CORES = [[2 * k + core for k in range(8)] for core in (0, 1)]


def dense(row, col, acc, amplitudes, panel, irrep_i, irrep_j, pos):
    half = jnp.broadcast_to(panel[None], (8, *panel.shape))
    half = lax.all_to_all(half, "ja", split_axis=0, concat_axis=0, tiled=True, axis_index_groups=CORES)
    other = lax.ppermute(half, "ja", [(n, n ^ 1) for n in range(16)])
    halves = [pltpu.VMEM((1024, 1024), BF16)] * 2 + [pltpu.VMEM((512, 1024), BF16)] * 2
    mid = pl.pallas_call(
        dense_half_kernel,
        out_shape=shape(16, 64, 512),
        in_specs=[VMEM] * 5 + [SMEM] * 3,
        out_specs=VMEM,
        scratch_shapes=halves,
        compiler_params=PARAMS,
        name="half_dense",
    )(row, col, amplitudes, half, other, irrep_i, irrep_j, pos)
    mid = lax.all_to_all(mid, "aa", split_axis=0, concat_axis=0, tiled=True)
    return pl.pallas_call(
        dense_ladder_kernel,
        out_shape=shape(*amplitudes.shape),
        in_specs=[VMEM] * 6 + [SMEM] * 3,
        out_specs=VMEM,
        scratch_shapes=halves,
        input_output_aliases={2: 0},
        compiler_params=PARAMS,
        name="ladder_dense",
    )(row, col, acc, mid, half, other, irrep_i, irrep_j, pos)


def local(amplitudes, chol, irrep_i, irrep_j, irrep_v, irrep_l):
    pos = jnp.stack([lax.axis_index("ja"), lax.axis_index("aa")]).astype(I32)
    width = irrep_v.shape[0]
    row, col, order, turn, slots = pl.pallas_call(
        table_kernel,
        out_shape=(
            shape(8, width, dtype=I32),
            shape(width, 128, dtype=I32),
            shape(16 * RANKS, 4 * SLOTS, dtype=BF16),
            shape(4 * SLOTS, 16 * RANKS, dtype=BF16),
            shape(16, 32, 128),
        ),
        in_specs=[VMEM, VMEM, SMEM, SMEM, SMEM],
        out_specs=(VMEM,) * 5,
        compiler_params=PARAMS,
        name="orbital_table",
    )(irrep_v.reshape(1, width), chol, irrep_i, irrep_l, pos)
    height = chol.shape[1]

    def whole():
        own_rows = lax.dynamic_slice_in_dim(irrep_v, pos[0] * height, height)
        pair = own_rows[:, None] ^ irrep_v[None, :]
        differ = irrep_l[0] != irrep_l[1]

        def step(n, acc):
            first = jnp.where((pair == irrep_l[0]) & (n == 0), chol[0], 0.0)
            second = jnp.where((pair == irrep_l[1]) & (differ | (n == 1)), chol[1], 0.0)
            return dense(row, col, acc, amplitudes, first + second, irrep_i, irrep_j, pos)

        return lax.fori_loop(0, jnp.where(differ, 1, 2), step, jnp.zeros_like(amplitudes))

    few = (row, col, order, turn, slots, amplitudes, irrep_i, irrep_j, irrep_l, pos)
    paired = ((half_paired_kernel, ladder_paired_kernel), 64 + 2 * RANKS, RANKS)
    general = ((half_kernel, ladder_kernel), 128, 2 * RANKS)
    return lax.switch(
        row[BRANCH, 0],
        [
            lambda: compact(*paired, TIGHT, *few),
            lambda: compact(*general, TIGHT, *few),
            lambda: compact(*general, SLOTS, *few),
            whole,
        ],
    )


def solution(mesh):
    in_specs = (P(None, "ja", "aa", None), P(None, "ja", None), P(), P(), P(), P())
    out_specs = P(None, "ja", "aa", None)
    return jax.shard_map(local, mesh=mesh, in_specs=in_specs, out_specs=out_specs, check_vma=False)
```

```python
import functools

import jax
import jax.numpy as jnp
from jax import lax
from jax.experimental import pallas as pl
from jax.experimental.pallas import tpu as pltpu
from jax.sharding import PartitionSpec as P

F32, BF16, I32 = jnp.float32, jnp.bfloat16, jnp.int32
NN = (((1,), (0,)), ((), ()))
NT = (((1,), (1,)), ((), ()))
SLOTS = 32
TIGHT = 24
RANKS = 16
CLS, NUM, SLOT, SPOT, LAB, RANK, BRANCH, BITS = range(8)


def iota(shape, dim):
    return lax.broadcasted_iota(I32, shape, dim)


def parity(x):
    return (x ^ (x >> 1) ^ (x >> 2)) & 1


def one(cond):
    return jnp.where(cond, 1.0, 0.0).astype(F32)


def dot(a, b, dims=NN):
    return lax.dot_general(a, b, dims, preferred_element_type=F32)


def split(x):
    high = x.astype(BF16)
    return high, (x - high.astype(F32)).astype(BF16)


def dot3(a, b, dims=NN):
    (ah, al), (bh, bl) = a, b
    return dot(ah, bh, dims) + dot(ah, bl, dims) + dot(al, bh, dims)


def dot2(a, b, dims=NN):
    return dot(a, b[0], dims) + dot(a, b[1], dims)


def table_kernel(irrep_ref, chol_ref, i_ref, l_ref, pos_ref, row_ref, col_ref, order_ref, turn_ref, out_ref, rows_ref):
    cls = irrep_ref[...]
    width = cls.shape[1]
    chunks = width // 128
    onehot = one(cls == iota((16, width), 0))
    before = one(iota((128, 128), 0) < iota((128, 128), 1))
    count = jnp.zeros((16, 1), F32)
    blocks = jnp.zeros((16, 128), F32)
    slots = []
    for k in range(chunks):
        part = onehot[:, 128 * k : 128 * k + 128]
        ahead = dot(part.astype(BF16), before.astype(BF16)) + count
        slots.append(jnp.sum(part * ahead, axis=0, keepdims=True))
        count = count + jnp.sum(part, axis=1, keepdims=True)
        place = one(iota((128, 128), 1) == 2 * k + (iota((128, 128), 0) >> 6))
        blocks = blocks + dot(part.astype(BF16), place.astype(BF16))
    slot = jnp.concatenate(slots, axis=1).astype(I32)
    lane = iota((16, 128), 1)
    cand = iota((16, 128), 0)
    count_lane = jnp.sum(jnp.where(lane == cand, count, 0.0), axis=0, keepdims=True)
    member = (parity((cand >> 1) & lane) == (cand & 1)) & (lane < 8)
    largest = jnp.max(jnp.where(member, count_lane, 0.0), axis=1, keepdims=True)
    in_block = jnp.zeros((16, 128), F32)
    for g in range(8):
        in_block = in_block + jnp.where(parity((cand >> 1) & g) == (cand & 1), blocks[g : g + 1, :], 0.0)
    fullest = jnp.max(in_block, axis=1, keepdims=True)
    bits_col = cand[:, 0:1] >> 1
    good = (largest <= SLOTS) & (fullest <= RANKS)
    for n in range(l_ref.shape[0]):
        good = good & (parity(bits_col & l_ref[n]) == 1)
    paired = parity(bits_col & (i_ref[0] ^ i_ref[1])) == 1
    rank = cand[:, 0:1] + jnp.where(largest <= TIGHT, jnp.where(paired, 0, 16), 32)
    pick = jnp.min(jnp.where(good, rank.astype(F32), 99.0), axis=0, keepdims=True).astype(I32)
    branch = jnp.where(pick < 48, pick >> 4, jnp.where(l_ref[0] != l_ref[1], 3, 4))
    bits, side = (pick & 15) >> 1, pick & 1
    small = parity(bits & cls) == side
    group = jnp.zeros_like(cls)
    label = jnp.zeros_like(cls)
    lane_group = iota((1, width), 1) >> 5
    number = jnp.zeros((1, 1), I32)
    for g in range(8):
        is_small = parity(bits & g) == side
        group = group + jnp.where(is_small & (cls > g), 1, 0)
        label = label + jnp.where(is_small & (number == lane_group), g, 0)
        number = number + jnp.where(is_small, 1, 0)
    inner = one((iota((128, 128), 0) < iota((128, 128), 1)) & ((iota((128, 128), 0) >> 6) == (iota((128, 128), 1) >> 6)))
    small16 = jnp.broadcast_to(one(small), (16, width))
    ranks = [
        dot(small16[:, 128 * k : 128 * k + 128].astype(BF16), inner.astype(BF16))[0:1, :] for k in range(chunks)
    ]
    rank = jnp.concatenate(ranks, axis=1).astype(I32)
    none = jnp.full_like(cls, -1)
    table = jnp.concatenate(
        [
            cls,
            jnp.where(small, group * SLOTS + slot, none),
            jnp.where(small, slot, none),
            jnp.where(small, (iota((1, width), 1) >> 6) * RANKS + rank, none),
            label,
            jnp.where(small, rank, none),
            jnp.broadcast_to(branch, cls.shape),
            jnp.broadcast_to(bits, cls.shape),
        ],
        axis=0,
    )
    row_ref[...] = table
    table = table.astype(F32)
    for k in range(chunks):
        tile = jnp.concatenate([table[:, 128 * k : 128 * k + 128], jnp.zeros((120, 128), F32)], axis=0)
        col_ref[128 * k : 128 * k + 128, :] = jnp.transpose(tile).astype(I32)
    spots, numbers = places(row_ref)
    order_ref[...] = dot(spots, numbers, NT).astype(BF16)
    turn_ref[...] = dot(numbers, spots, NT).astype(BF16)
    panel_slots(row_ref, col_ref, chol_ref, l_ref, pos_ref, out_ref, rows_ref)


def own(col_ref, block, field):
    return col_ref[pl.ds(pl.multiple_of(block * 64, 64), 64), field : field + 1]


def panel_slots(row_ref, col_ref, chol_ref, l_ref, pos_ref, out_ref, rows_ref):
    cls = row_ref[CLS : CLS + 1, :]
    slot = row_ref[SLOT : SLOT + 1, :]
    own_cls = own(col_ref, pos_ref[0], CLS)
    pick = one(slot == iota((SLOTS, slot.shape[1]), 0)).astype(BF16)
    parts = []
    kept_all = [jnp.where((own_cls ^ cls) == l_ref[n], chol_ref[n], 0.0) for n in range(2)]
    rows_ref[...] = kept_all[0] + kept_all[1]
    for kept in kept_all:
        high, low = split(kept)
        parts.append(dot(high, pick, NT) + dot(low, pick, NT))
    both = jnp.concatenate(parts, axis=1)
    packed = jnp.concatenate([both[0:32], both[32:64]], axis=1)
    out_ref[...] = jnp.broadcast_to(packed[None], out_ref.shape)


def unpack(gathered):
    n = gathered.shape[0]
    return jnp.concatenate([gathered, jnp.roll(gathered, 64, axis=2)], axis=1).reshape(n * 64, 128)


def places(row_ref):
    spot = row_ref[SPOT : SPOT + 1, :]
    number = row_ref[NUM : NUM + 1, :]
    width = spot.shape[1]
    spots = one(spot == iota((16 * RANKS, width), 0)).astype(BF16)
    numbers = one(number == iota((4 * SLOTS, width), 0)).astype(BF16)
    return spots, numbers


def finish(left, full, out_ref, left_ref):
    left_ref[...] = left

    @pl.loop(0, 2)
    def _(i):
        rows = pl.ds(pl.multiple_of(256 * i, 256), 256)
        out_ref[i] = dot3(split(left_ref[rows, :]), full).reshape(4, 64, full[0].shape[1])


def ladder_kernel(
    count, row_ref, col_ref, order_ref, got_ref, mid_ref, i_ref, j_ref, l_ref, pos_ref, out_ref, left_ref
):
    p, q = pos_ref[0], pos_ref[1]
    cls = row_ref[CLS : CLS + 1, :]
    number = row_ref[NUM : NUM + 1, :]
    label = row_ref[LAB : LAB + 1, 0:128]
    bits = row_ref[BITS : BITS + 1, 0:1]
    label_col = col_ref[0:128, LAB : LAB + 1]
    width = cls.shape[1]
    turned = jnp.transpose(unpack(got_ref[...]))
    full = [
        jnp.where(label_col == (cls ^ l_ref[n]), jnp.concatenate([turned[32 * n : 32 * n + 32]] * 4, axis=0), 0.0)
        for n in range(2)
    ]
    full = split(jnp.concatenate(full + [one(number == iota((128, width), 0))], axis=0))
    rows, lates = receive(mid_ref, 128, 2 * RANKS, count)
    mids = [rows[:, 64 * i : 64 * i + 64].reshape(width, 128) for i in range(2)]
    core = dot3(full, split(jnp.concatenate(mids, axis=1)))
    order = order_ref[...]
    own_panel = unpack(got_ref[pl.ds(q, 1)])
    own_slot = own(col_ref, q, SLOT)
    own_rank = own(col_ref, q, RANK)
    own_cls = jnp.concatenate([own(col_ref, q, CLS)] * 4, axis=0)
    lane = iota((64, 128), 1)
    first_tile = jnp.concatenate([own_panel[:, 0:32]] * 4, axis=1)
    second_tile = jnp.concatenate([own_panel[:, 32:64]] * 4, axis=1)
    slot_tile = one(own_slot == (lane & 31))
    rank_pick = one(own_rank == lane).astype(BF16)
    lane_row = iota((1, 128), 1) >> 5
    results = []
    for i in range(2):
        xs = [i_ref[i] ^ j_ref[p * 4 + j] for j in range(4)]
        x_lane = jnp.zeros((1, 128), I32)
        x_row = jnp.zeros((256, 1), I32)
        for j in range(4):
            x_lane = jnp.where(lane_row == j, xs[j], x_lane)
            x_row = jnp.where((iota((256, 1), 0) >> 6) == j, xs[j], x_row)
        odd_lane = parity(x_lane & bits) == 1
        odd = [parity(bits & xs[j]) == 1 for j in range(4)]

        def blocks(tiles):
            return split(
                jnp.concatenate([jnp.where((lane >> 5) == j, tiles[j], 0.0) for j in range(4)], axis=0)
            )

        late = lates[:, RANKS * i : RANKS * (i + 1)]
        total = jnp.where(odd_lane, 0.0, jnp.sum(late, axis=0))
        late = jnp.where(odd_lane, late.reshape(16 * RANKS, 128), 0.0)
        lanes = slice(128 * i, 128 * i + 128)
        pick = core[256:384, lanes]
        pick2 = jnp.where(odd_lane, dot2(order, split(late)), pick)
        t1 = dot3(blocks([jnp.where(odd[j], slot_tile, first_tile) for j in range(4)]), split(pick), NT)
        t2 = dot3(blocks([jnp.where(odd[j], slot_tile, second_tile) for j in range(4)]), split(pick2), NT)
        t3 = dot3(blocks([first_tile] * 4), split(core[0:128, lanes]), NT)
        t3 = t3 + dot3(blocks([second_tile] * 4), split(core[128:256, lanes]), NT)
        total = jnp.concatenate([total, jnp.zeros((128 - RANKS, 128), F32)], axis=0)
        total = dot2(rank_pick, split(total))
        spread = [jnp.concatenate([total[:, 32 * j : 32 * j + 32]] * 4, axis=1) for j in range(4)]
        t3 = t3 + jnp.concatenate(spread, axis=0)
        goal = own_cls ^ x_row
        t1 = jnp.where(label == (goal ^ l_ref[0]), t1, 0.0)
        t2 = jnp.where(label == (goal ^ l_ref[1]), t2, 0.0)
        t3 = jnp.where(label == goal, t3, 0.0)
        results.append(jnp.concatenate([t1, t2, t3], axis=1))
    finish(jnp.concatenate(results, axis=0), full, out_ref, left_ref)


def sent_rows(same, own_rows, count):
    return same + own_rows if count == SLOTS else -(-(same + own_rows) * count // SLOTS // 8) * 8


def send(out_ref, same, different, count):
    rows, late = same.shape[0], different.shape[1]
    if count == SLOTS:
        out_ref[:, 0:rows, :] = jnp.broadcast_to(same[None], (16, rows, 128))
        out_ref[:, rows : rows + late, :] = different
        return
    total = out_ref.shape[1]
    same = jnp.concatenate([same[:, 32 * j : 32 * j + count] for j in range(4)], axis=1)
    different = jnp.concatenate([different[:, :, 32 * j : 32 * j + count] for j in range(4)], axis=2)
    rest = rows - total
    side = [same[total:, 32 * k : 32 * k + 32] for k in range(3)] + [jnp.zeros((total - 3 * rest, 32), F32)]
    main = jnp.concatenate([same[0:total], jnp.concatenate(side, axis=0)], axis=1)
    out_ref[...] = jnp.broadcast_to(main[None], out_ref.shape)
    for k in range(3):
        start = 3 * rest + late * k
        out_ref[:, start : start + late, 96:128] = different[:, :, 32 * k : 32 * k + 32]


def receive(mid_ref, rows, late, count):
    if count == SLOTS:
        return mid_ref[:, 0:rows, :], mid_ref[:, rows : rows + late, :]
    total = mid_ref.shape[1]
    rest = rows - total

    def side(start, size):
        parts = [mid_ref[:, start + size * k : start + size * (k + 1), 96:128] for k in range(3)]
        return jnp.concatenate(parts, axis=2)

    def widen(x):
        gap = jnp.zeros((*x.shape[:2], 32 - count), F32)
        parts = []
        for j in range(4):
            parts += [x[:, :, count * j : count * j + count], gap]
        return jnp.concatenate(parts, axis=2)

    same = jnp.concatenate([mid_ref[:, :, 0:96], side(0, rest)], axis=1)
    return widen(same), widen(side(3 * rest, late))


def half_products(row_ref, col_ref, amp_ref, got_ref, i_ref, j_ref, pos_ref, half_ref):
    p, q = pos_ref[0], pos_ref[1]
    cls = row_ref[CLS : CLS + 1, :]
    own_cls = own(col_ref, q, CLS)
    panel = unpack(got_ref[...])
    lane = iota(panel.shape, 1)
    slot = col_ref[:, SLOT : SLOT + 1]
    wh, wl = split(jnp.where(lane < 64, panel, one(slot == lane - 64)))
    both = jnp.concatenate([wh, wl], axis=1)
    pair_cls = own_cls ^ cls

    @pl.loop(0, 2)
    def _(i):
        kept = [jnp.where(pair_cls == (i_ref[i] ^ j_ref[p * 4 + j]), amp_ref[i, j], 0.0) for j in range(4)]
        high, low = split(jnp.concatenate(kept, axis=0))
        first = dot(high, both)
        rows = pl.ds(pl.multiple_of(256 * i, 256), 256)
        half_ref[rows, :] = first[:, 0:128] + first[:, 128:256] + dot(low, wh)

    return [half_ref[64 * n : 64 * n + 64, :] for n in range(8)]


def left_factor(col_ref, got_ref, q):
    own_rank = own(col_ref, q, RANK)
    own_panel = unpack(got_ref[pl.ds(q, 1)])
    stacked = jnp.concatenate([own_panel[:, 0:32], own_panel[:, 32:64]], axis=0)
    ranks = jnp.concatenate([jnp.full_like(own_rank, -1), own_rank], axis=0)
    lane = iota((128, 128), 1)
    left = jnp.where(lane < 32, jnp.concatenate([stacked] * 4, axis=1), one(ranks == lane - 32))
    return jnp.transpose(jnp.where(lane < 48, left, 0.0))


def odd_even(row_ref, i_ref, j_ref, p):
    bits = row_ref[BITS : BITS + 1, 0:1]
    later = [parity(bits & (i_ref[1] ^ j_ref[p * 4 + j])) == 1 for j in range(4)]
    xs = [[jnp.where(later[j], i_ref[i] ^ j_ref[p * 4 + j], i_ref[1 - i] ^ j_ref[p * 4 + j]) for j in range(4)] for i in (1, 0)]
    return later, xs[0], xs[1]


def half_kernel(
    count, row_ref, col_ref, order_ref, amp_ref, got_ref, i_ref, j_ref, l_ref, pos_ref, out_ref, half_ref
):
    p, q = pos_ref[0], pos_ref[1]
    label = row_ref[LAB : LAB + 1, 0:128]
    own_cls = own(col_ref, q, CLS)
    own_small = own(col_ref, q, NUM) >= 0
    xs = [i_ref[n // 4] ^ j_ref[p * 4 + n % 4] for n in range(8)]
    parts = half_products(row_ref, col_ref, amp_ref, got_ref, i_ref, j_ref, pos_ref, half_ref)
    firsts = [part[:, 64:96] + jnp.where(own_small, part[:, 0:32], 0.0) for part in parts]
    left = left_factor(col_ref, got_ref, q)
    pair_cls = jnp.concatenate([own_cls ^ l_ref[0], own_cls ^ l_ref[1]], axis=0)
    both = [jnp.concatenate([part[:, 0:32], part[:, 32:64]], axis=0) for part in parts]
    spread = [
        jnp.where(label == (pair_cls ^ xs[n]), jnp.concatenate([both[n]] * 4, axis=1), 0.0) for n in range(8)
    ]
    sums = dot3(split(left[0:32]), split(jnp.concatenate(spread, axis=1)))
    seconds = dot2(left[32:48].astype(BF16), split(jnp.concatenate(both, axis=1)))
    order = order_ref[...]
    mains, lates = [], []
    for i in range(2):
        rows = jnp.concatenate([sums[:, 128 * n : 128 * n + 128] for n in range(4 * i, 4 * i + 4)], axis=0)
        by_spot = dot2(order, split(rows), NT).reshape(16, RANKS, 128)
        lates.append(by_spot + seconds[None, :, 128 * i : 128 * i + 128])
        mains.append(jnp.concatenate(firsts[4 * i : 4 * i + 4], axis=1))
    send(out_ref, jnp.concatenate(mains, axis=0), jnp.concatenate(lates, axis=1), count)


def half_paired_kernel(
    count, row_ref, col_ref, order_ref, amp_ref, got_ref, i_ref, j_ref, l_ref, pos_ref, out_ref, half_ref
):
    p, q = pos_ref[0], pos_ref[1]
    label = row_ref[LAB : LAB + 1, 0:128]
    own_cls = own(col_ref, q, CLS)
    own_small = own(col_ref, q, NUM) >= 0
    parts = half_products(row_ref, col_ref, amp_ref, got_ref, i_ref, j_ref, pos_ref, half_ref)
    later, _, even_x = odd_even(row_ref, i_ref, j_ref, p)
    odd = [jnp.where(later[j], parts[4 + j], parts[j]) for j in range(4)]
    even = [jnp.where(later[j], parts[j], parts[4 + j]) for j in range(4)]
    rows = jnp.concatenate([part[:, 64:96] + jnp.where(own_small, part[:, 0:32], 0.0) for part in odd], axis=1)
    left = left_factor(col_ref, got_ref, q)
    firsts = jnp.concatenate([part[:, 64:96] for part in even], axis=1)
    seconds = jnp.concatenate([part[:, 32:64] for part in odd], axis=1)
    few = jnp.concatenate([firsts, seconds], axis=1)
    few = dot2(left[32:48].astype(BF16), split(jnp.concatenate([few, few], axis=0)))
    pair_cls = jnp.concatenate([own_cls ^ l_ref[0], own_cls ^ l_ref[1]], axis=0)
    spread = []
    for j in range(4):
        both = jnp.concatenate([even[j][:, 0:32], even[j][:, 32:64]], axis=0)
        spread.append(jnp.where(label == (pair_cls ^ even_x[j]), jnp.concatenate([both] * 4, axis=1), 0.0))
    sums = dot3(split(left[0:32]), split(jnp.concatenate(spread, axis=1)))
    sums = jnp.concatenate([sums[:, 128 * j : 128 * j + 128] for j in range(4)], axis=0)
    order = order_ref[...]
    rows = jnp.concatenate([rows, few[:, 0:128], few[:, 128:256]], axis=0)
    send(out_ref, rows, dot2(order, split(sums), NT).reshape(16, RANKS, 128), count)


def ladder_paired_kernel(
    count, row_ref, col_ref, order_ref, got_ref, mid_ref, i_ref, j_ref, l_ref, pos_ref, out_ref, left_ref
):
    p, q = pos_ref[0], pos_ref[1]
    cls = row_ref[CLS : CLS + 1, :]
    number = row_ref[NUM : NUM + 1, :]
    label = row_ref[LAB : LAB + 1, 0:128]
    label_col = col_ref[0:128, LAB : LAB + 1]
    width = cls.shape[1]
    turned = jnp.transpose(unpack(got_ref[...]))
    full = [
        jnp.where(label_col == (cls ^ l_ref[n]), jnp.concatenate([turned[32 * n : 32 * n + 32]] * 4, axis=0), 0.0)
        for n in range(2)
    ]
    full = split(jnp.concatenate(full + [one(number == iota((128, width), 0))], axis=0))
    rows, sums = receive(mid_ref, 64 + 2 * RANKS, RANKS, count)
    core = dot3(full, split(rows[:, 0:64].reshape(width, 128)))
    order = order_ref[...]
    few = [rows[:, 64 + RANKS * k : 64 + RANKS * (k + 1)].reshape(16 * RANKS, 128) for k in range(2)]
    small_rows, second_rows = [dot2(order, split(few[k])) for k in range(2)]
    total = jnp.concatenate([jnp.sum(sums, axis=0), jnp.zeros((128 - RANKS, 128), F32)], axis=0)
    own_panel = unpack(got_ref[pl.ds(q, 1)])
    own_slot = own(col_ref, q, SLOT)
    own_rank = own(col_ref, q, RANK)
    own_cls = own(col_ref, q, CLS)
    lane = iota((64, 128), 1)

    def blocks(tile):
        return split(jnp.concatenate([jnp.where((lane >> 5) == j, tile, 0.0) for j in range(4)], axis=0))

    first = blocks(jnp.concatenate([own_panel[:, 0:32]] * 4, axis=1))
    second = blocks(jnp.concatenate([own_panel[:, 32:64]] * 4, axis=1))
    slots = blocks(one(own_slot == (lane & 31)))[0]
    total = dot2(one(own_rank == lane).astype(BF16), split(total))
    total = [jnp.concatenate([total[:, 32 * j : 32 * j + 32]] * 4, axis=1) for j in range(4)]
    odd = [
        dot2(slots, split(core[256:384]), NT),
        dot2(slots, split(second_rows), NT),
        dot3(first, split(core[0:128]), NT) + dot3(second, split(core[128:256]), NT),
    ]
    small_rows = split(small_rows)
    even = [dot3(first, small_rows, NT), dot3(second, small_rows, NT), jnp.concatenate(total, axis=0)]
    later, odd_x, even_x = odd_even(row_ref, i_ref, j_ref, p)
    rows = [None] * 8
    for j in range(4):
        kinds = []
        for parts, x in ((odd, odd_x[j]), (even, even_x[j])):
            goal = own_cls ^ x
            labels = (goal ^ l_ref[0], goal ^ l_ref[1], goal)
            kinds.append(
                jnp.concatenate(
                    [jnp.where(label == labels[k], parts[k][64 * j : 64 * j + 64], 0.0) for k in range(3)], axis=1
                )
            )
        rows[j] = jnp.where(later[j], kinds[1], kinds[0])
        rows[4 + j] = jnp.where(later[j], kinds[0], kinds[1])
    finish(jnp.concatenate(rows, axis=0), full, out_ref, left_ref)


VMEM = pl.BlockSpec(memory_space=pltpu.VMEM)
SMEM = pl.BlockSpec(memory_space=pltpu.SMEM)
PARAMS = pltpu.CompilerParams(vmem_limit_bytes=48 * 1024 * 1024)


def shape(*dims, dtype=F32):
    return jax.ShapeDtypeStruct(dims, dtype)


def compact(kernels, same, late, count, row, col, order, turn, panel, amplitudes, irrep_i, irrep_j, irrep_l, pos):
    panel = lax.all_to_all(panel, "ja", split_axis=0, concat_axis=0, tiled=True)
    mid = pl.pallas_call(
        functools.partial(kernels[0], count),
        out_shape=shape(16, sent_rows(same, late, count), 128),
        in_specs=[VMEM] * 5 + [SMEM] * 4,
        out_specs=VMEM,
        scratch_shapes=[pltpu.VMEM((512, 128), F32)],
        compiler_params=PARAMS,
        name="half_slots",
    )(row, col, order, amplitudes, panel, irrep_i, irrep_j, irrep_l, pos)
    mid = lax.all_to_all(mid, "aa", split_axis=0, concat_axis=0, tiled=True)
    return pl.pallas_call(
        functools.partial(kernels[1], count),
        out_shape=shape(*amplitudes.shape),
        in_specs=[VMEM] * 5 + [SMEM] * 4,
        out_specs=VMEM,
        scratch_shapes=[pltpu.VMEM((512, 12 * SLOTS), F32)],
        compiler_params=PARAMS,
        name="ladder_slots",
    )(row, col, turn, panel, mid, irrep_i, irrep_j, irrep_l, pos)


def panel_rows(half_ref, other_ref, core, high_ref, low_ref):
    @pl.loop(0, half_ref.shape[0])
    def _(k):
        for part, ref in ((core, half_ref), (1 - core, other_ref)):
            rows = pl.ds(pl.multiple_of((2 * k + part) * 64, 64), 64)
            high_ref[rows, :], low_ref[rows, :] = split(ref[k])


def dense_half_kernel(
    row_ref, col_ref, amp_ref, half_ref, other_ref, i_ref, j_ref, pos_ref, out_ref, ph_ref, pl_ref, high_ref, low_ref
):
    p, q = pos_ref[0], pos_ref[1]
    panel_rows(half_ref, other_ref, p & 1, ph_ref, pl_ref)
    pair_cls = own(col_ref, q, CLS) ^ row_ref[CLS : CLS + 1, :]

    @pl.loop(0, 8)
    def _(n):
        i, j = n >> 2, n & 3
        kept = jnp.where(pair_cls == (i_ref[i] ^ j_ref[p * 4 + j]), amp_ref[i, j], 0.0)
        rows = pl.ds(pl.multiple_of(64 * n, 64), 64)
        high_ref[rows, :], low_ref[rows, :] = split(kept)

    @pl.loop(0, 2)
    def _(k):
        rows = pl.ds(pl.multiple_of(512 * k, 512), 512)
        result = dot3((ph_ref[rows, :], pl_ref[rows, :]), (high_ref[...], low_ref[...]), NT)
        out_ref[pl.ds(8 * k, 8)] = result.reshape(8, 64, 512)


def dense_ladder_kernel(row_ref, col_ref, mid_ref, half_ref, other_ref, i_ref, j_ref, pos_ref, *refs):
    p, q = pos_ref[0], pos_ref[1]
    acc_ref = refs[0] if len(refs) == 6 else None
    out_ref, ph_ref, pl_ref, high_ref, low_ref = refs[-5:]
    panel_rows(half_ref, other_ref, p & 1, ph_ref, pl_ref)
    first = iota((64, 128), 1) < 64

    @pl.loop(0, 4)
    def _(k):
        lanes = pl.ds(pl.multiple_of(128 * k, 128), 128)
        pairs = [(mid_ref[s, :, lanes], mid_ref[s + 1, :, lanes]) for s in range(0, 16, 2)]
        left = [jnp.where(first, a, jnp.roll(b, 64, axis=1)) for a, b in pairs]
        right = [jnp.where(first, jnp.roll(a, 64, axis=1), b) for a, b in pairs]
        rows = pl.ds(pl.multiple_of(128 * k, 128), 128)
        whole = jnp.concatenate([jnp.concatenate(left, axis=1), jnp.concatenate(right, axis=1)], axis=0)
        high_ref[rows, :], low_ref[rows, :] = split(whole)

    pair_cls = own(col_ref, q, CLS) ^ row_ref[CLS : CLS + 1, :]

    @pl.loop(0, 2)
    def _(i):
        rows = pl.ds(pl.multiple_of(256 * i, 256), 256)
        result = dot3((high_ref[rows, :], low_ref[rows, :]), (ph_ref[...], pl_ref[...]))
        for j in range(4):
            x = i_ref[i] ^ j_ref[p * 4 + j]
            kept = jnp.where(pair_cls == x, result[64 * j : 64 * j + 64], 0.0)
            out_ref[i, j] = kept if acc_ref is None else acc_ref[i, j] + kept


CORES = [[2 * k + core for k in range(8)] for core in (0, 1)]


def dense(row, col, acc, amplitudes, panel, irrep_i, irrep_j, pos):
    half = jnp.broadcast_to(panel[None], (8, *panel.shape))
    half = lax.all_to_all(half, "ja", split_axis=0, concat_axis=0, tiled=True, axis_index_groups=CORES)
    other = lax.ppermute(half, "ja", [(n, n ^ 1) for n in range(16)])
    halves = [pltpu.VMEM((1024, 1024), BF16)] * 2 + [pltpu.VMEM((512, 1024), BF16)] * 2
    mid = pl.pallas_call(
        dense_half_kernel,
        out_shape=shape(16, 64, 512),
        in_specs=[VMEM] * 5 + [SMEM] * 3,
        out_specs=VMEM,
        scratch_shapes=halves,
        compiler_params=PARAMS,
        name="half_dense",
    )(row, col, amplitudes, half, other, irrep_i, irrep_j, pos)
    mid = lax.all_to_all(mid, "aa", split_axis=0, concat_axis=0, tiled=True)
    so_far = [] if acc is None else [acc]
    return pl.pallas_call(
        dense_ladder_kernel,
        out_shape=shape(*amplitudes.shape),
        in_specs=[VMEM] * 5 + [SMEM] * 3 + [VMEM] * len(so_far),
        out_specs=VMEM,
        scratch_shapes=halves,
        input_output_aliases={8: 0} if so_far else {},
        compiler_params=PARAMS,
        name="ladder_dense",
    )(row, col, mid, half, other, irrep_i, irrep_j, pos, *so_far)


def local(amplitudes, chol, irrep_i, irrep_j, irrep_v, irrep_l):
    pos = jnp.stack([lax.axis_index("ja"), lax.axis_index("aa")]).astype(I32)
    width = irrep_v.shape[0]
    row, col, order, turn, slots, rows = pl.pallas_call(
        table_kernel,
        out_shape=(
            shape(8, width, dtype=I32),
            shape(width, 128, dtype=I32),
            shape(16 * RANKS, 4 * SLOTS, dtype=BF16),
            shape(4 * SLOTS, 16 * RANKS, dtype=BF16),
            shape(16, 32, 128),
            shape(chol.shape[1], width),
        ),
        in_specs=[VMEM, VMEM, SMEM, SMEM, SMEM],
        out_specs=(VMEM,) * 6,
        compiler_params=PARAMS,
        name="orbital_table",
    )(irrep_v.reshape(1, width), chol, irrep_i, irrep_l, pos)
    height = chol.shape[1]

    def together():
        return dense(row, col, None, amplitudes, rows, irrep_i, irrep_j, pos)

    def apart():
        own_rows = lax.dynamic_slice_in_dim(irrep_v, pos[0] * height, height)
        keep = (own_rows[:, None] ^ irrep_v[None, :]) == irrep_l[0]

        def step(n, acc):
            panel = jnp.where(keep, jnp.where(n == 0, chol[0], chol[1]), 0.0)
            return dense(row, col, acc, amplitudes, panel, irrep_i, irrep_j, pos)

        return lax.fori_loop(0, 2, step, jnp.zeros_like(amplitudes))

    few = (row, col, order, turn, slots, amplitudes, irrep_i, irrep_j, irrep_l, pos)
    paired = ((half_paired_kernel, ladder_paired_kernel), 64 + 2 * RANKS, RANKS)
    general = ((half_kernel, ladder_kernel), 128, 2 * RANKS)
    return lax.switch(
        row[BRANCH, 0],
        [
            lambda: compact(*paired, TIGHT, *few),
            lambda: compact(*general, TIGHT, *few),
            lambda: compact(*general, SLOTS, *few),
            together,
            apart,
        ],
    )


def solution(mesh):
    in_specs = (P(None, "ja", "aa", None), P(None, "ja", None), P(), P(), P(), P())
    out_specs = P(None, "ja", "aa", None)
    return jax.shard_map(local, mesh=mesh, in_specs=in_specs, out_specs=out_specs, check_vma=False)
```

```python
import functools

import jax
import jax.numpy as jnp
from jax import lax
from jax.experimental import pallas as pl
from jax.experimental.pallas import tpu as pltpu
from jax.sharding import PartitionSpec as P

F32, BF16, I32 = jnp.float32, jnp.bfloat16, jnp.int32
NN = (((1,), (0,)), ((), ()))
NT = (((1,), (1,)), ((), ()))
SLOTS = 32
TIGHT = 24
RANKS = 16
CLS, NUM, SLOT, SPOT, LAB, RANK, BRANCH, BITS = range(8)


def iota(shape, dim):
    return lax.broadcasted_iota(I32, shape, dim)


def parity(x):
    return (x ^ (x >> 1) ^ (x >> 2)) & 1


def one(cond):
    return jnp.where(cond, 1.0, 0.0).astype(F32)


def dot(a, b, dims=NN):
    return lax.dot_general(a, b, dims, preferred_element_type=F32)


def split(x):
    high = x.astype(BF16)
    return high, (x - high.astype(F32)).astype(BF16)


def dot3(a, b, dims=NN):
    (ah, al), (bh, bl) = a, b
    return dot(ah, bh, dims) + dot(ah, bl, dims) + dot(al, bh, dims)


def dot2(a, b, dims=NN):
    return dot(a, b[0], dims) + dot(a, b[1], dims)


def table_kernel(irrep_ref, chol_ref, i_ref, l_ref, pos_ref, row_ref, col_ref, order_ref, turn_ref, out_ref, rows_ref, branch_ref):
    cls = irrep_ref[...]
    width = cls.shape[1]
    chunks = width // 128
    onehot = one(cls == iota((16, width), 0))
    before = one(iota((128, 128), 0) < iota((128, 128), 1))
    count = jnp.zeros((16, 1), F32)
    blocks = jnp.zeros((16, 128), F32)
    slots = []
    for k in range(chunks):
        part = onehot[:, 128 * k : 128 * k + 128]
        ahead = dot(part.astype(BF16), before.astype(BF16)) + count
        slots.append(jnp.sum(part * ahead, axis=0, keepdims=True))
        count = count + jnp.sum(part, axis=1, keepdims=True)
        place = one(iota((128, 128), 1) == 2 * k + (iota((128, 128), 0) >> 6))
        blocks = blocks + dot(part.astype(BF16), place.astype(BF16))
    slot = jnp.concatenate(slots, axis=1).astype(I32)
    lane = iota((16, 128), 1)
    cand = iota((16, 128), 0)
    count_lane = jnp.sum(jnp.where(lane == cand, count, 0.0), axis=0, keepdims=True)
    member = (parity((cand >> 1) & lane) == (cand & 1)) & (lane < 8)
    largest = jnp.max(jnp.where(member, count_lane, 0.0), axis=1, keepdims=True)
    in_block = jnp.zeros((16, 128), F32)
    for g in range(8):
        in_block = in_block + jnp.where(parity((cand >> 1) & g) == (cand & 1), blocks[g : g + 1, :], 0.0)
    fullest = jnp.max(in_block, axis=1, keepdims=True)
    bits_col = cand[:, 0:1] >> 1
    good = (largest <= SLOTS) & (fullest <= RANKS)
    for n in range(l_ref.shape[0]):
        good = good & (parity(bits_col & l_ref[n]) == 1)
    paired = parity(bits_col & (i_ref[0] ^ i_ref[1])) == 1
    rank = cand[:, 0:1] + jnp.where(largest <= TIGHT, jnp.where(paired, 0, 16), 32)
    pick = jnp.min(jnp.where(good, rank.astype(F32), 99.0), axis=0, keepdims=True).astype(I32)
    branch = jnp.where(pick < 48, pick >> 4, jnp.where(l_ref[0] != l_ref[1], 3, 4))
    bits, side = (pick & 15) >> 1, pick & 1
    small = parity(bits & cls) == side
    group = jnp.zeros_like(cls)
    label = jnp.zeros_like(cls)
    lane_group = iota((1, width), 1) >> 5
    number = jnp.zeros((1, 1), I32)
    for g in range(8):
        is_small = parity(bits & g) == side
        group = group + jnp.where(is_small & (cls > g), 1, 0)
        label = label + jnp.where(is_small & (number == lane_group), g, 0)
        number = number + jnp.where(is_small, 1, 0)
    inner = one((iota((128, 128), 0) < iota((128, 128), 1)) & ((iota((128, 128), 0) >> 6) == (iota((128, 128), 1) >> 6)))
    small16 = jnp.broadcast_to(one(small), (16, width))
    ranks = [
        dot(small16[:, 128 * k : 128 * k + 128].astype(BF16), inner.astype(BF16))[0:1, :] for k in range(chunks)
    ]
    rank = jnp.concatenate(ranks, axis=1).astype(I32)
    none = jnp.full_like(cls, -1)
    table = jnp.concatenate(
        [
            cls,
            jnp.where(small, group * SLOTS + slot, none),
            jnp.where(small, slot, none),
            jnp.where(small, (iota((1, width), 1) >> 6) * RANKS + rank, none),
            label,
            jnp.where(small, rank, none),
            jnp.broadcast_to(branch, cls.shape),
            jnp.broadcast_to(bits, cls.shape),
        ],
        axis=0,
    )
    row_ref[...] = table
    branch_ref[0] = jnp.max(branch.astype(F32)).astype(I32)
    table = table.astype(F32)
    for k in range(chunks):
        tile = jnp.concatenate([table[:, 128 * k : 128 * k + 128], jnp.zeros((120, 128), F32)], axis=0)
        col_ref[128 * k : 128 * k + 128, :] = jnp.transpose(tile).astype(I32)
    spots, numbers = places(row_ref)
    order_ref[...] = dot(spots, numbers, NT).astype(BF16)
    turn_ref[...] = dot(numbers, spots, NT).astype(BF16)
    panel_slots(row_ref, col_ref, chol_ref, l_ref, pos_ref, out_ref, rows_ref)


def own(col_ref, block, field):
    return col_ref[pl.ds(pl.multiple_of(block * 64, 64), 64), field : field + 1]


def panel_slots(row_ref, col_ref, chol_ref, l_ref, pos_ref, out_ref, rows_ref):
    cls = row_ref[CLS : CLS + 1, :]
    slot = row_ref[SLOT : SLOT + 1, :]
    own_cls = own(col_ref, pos_ref[0], CLS)
    pick = one(slot == iota((SLOTS, slot.shape[1]), 0)).astype(BF16)
    parts = []
    kept_all = [jnp.where((own_cls ^ cls) == l_ref[n], chol_ref[n], 0.0) for n in range(2)]
    rows_ref[...] = kept_all[0] + kept_all[1]
    for kept in kept_all:
        high, low = split(kept)
        parts.append(dot(high, pick, NT) + dot(low, pick, NT))
    both = jnp.concatenate(parts, axis=1)
    packed = jnp.concatenate([both[0:32], both[32:64]], axis=1)
    out_ref[...] = jnp.broadcast_to(packed[None], out_ref.shape)


def unpack(gathered):
    n = gathered.shape[0]
    return jnp.concatenate([gathered, jnp.roll(gathered, 64, axis=2)], axis=1).reshape(n * 64, 128)


def places(row_ref):
    spot = row_ref[SPOT : SPOT + 1, :]
    number = row_ref[NUM : NUM + 1, :]
    width = spot.shape[1]
    spots = one(spot == iota((16 * RANKS, width), 0)).astype(BF16)
    numbers = one(number == iota((4 * SLOTS, width), 0)).astype(BF16)
    return spots, numbers


def finish(left, full, out_ref, left_ref):
    left_ref[...] = left

    @pl.loop(0, 2)
    def _(i):
        rows = pl.ds(pl.multiple_of(256 * i, 256), 256)
        picks = 8 * SLOTS
        high, low = split(left_ref[rows, :])
        result = dot(high, full[0]) + dot(high[:, 0:picks], full[1][0:picks]) + dot(low, full[0])
        out_ref[i] = result.reshape(4, 64, full[0].shape[1])


def ladder_kernel(
    count, row_ref, col_ref, order_ref, got_ref, mid_ref, i_ref, j_ref, l_ref, pos_ref, out_ref, left_ref
):
    p, q = pos_ref[0], pos_ref[1]
    cls = row_ref[CLS : CLS + 1, :]
    number = row_ref[NUM : NUM + 1, :]
    label = row_ref[LAB : LAB + 1, 0:128]
    bits = row_ref[BITS : BITS + 1, 0:1]
    label_col = col_ref[0:128, LAB : LAB + 1]
    width = cls.shape[1]
    turned = jnp.transpose(unpack(got_ref[...]))
    full = [
        jnp.where(label_col == (cls ^ l_ref[n]), jnp.concatenate([turned[32 * n : 32 * n + 32]] * 4, axis=0), 0.0)
        for n in range(2)
    ]
    full = split(jnp.concatenate(full + [one(number == iota((128, width), 0))], axis=0))
    rows, lates = receive(mid_ref, 128, 2 * RANKS, count)
    mids = [rows[:, 64 * i : 64 * i + 64].reshape(width, 128) for i in range(2)]
    core = dot3(full, split(jnp.concatenate(mids, axis=1)))
    order = order_ref[...]
    own_panel = unpack(got_ref[pl.ds(q, 1)])
    own_slot = own(col_ref, q, SLOT)
    own_rank = own(col_ref, q, RANK)
    own_cls = jnp.concatenate([own(col_ref, q, CLS)] * 4, axis=0)
    lane = iota((64, 128), 1)
    first_tile = jnp.concatenate([own_panel[:, 0:32]] * 4, axis=1)
    second_tile = jnp.concatenate([own_panel[:, 32:64]] * 4, axis=1)
    slot_tile = one(own_slot == (lane & 31))
    rank_pick = one(own_rank == lane).astype(BF16)
    lane_row = iota((1, 128), 1) >> 5
    results = []
    for i in range(2):
        xs = [i_ref[i] ^ j_ref[p * 4 + j] for j in range(4)]
        x_lane = jnp.zeros((1, 128), I32)
        x_row = jnp.zeros((256, 1), I32)
        for j in range(4):
            x_lane = jnp.where(lane_row == j, xs[j], x_lane)
            x_row = jnp.where((iota((256, 1), 0) >> 6) == j, xs[j], x_row)
        odd_lane = parity(x_lane & bits) == 1
        odd = [parity(bits & xs[j]) == 1 for j in range(4)]

        def blocks(tiles):
            return split(
                jnp.concatenate([jnp.where((lane >> 5) == j, tiles[j], 0.0) for j in range(4)], axis=0)
            )

        late = lates[:, RANKS * i : RANKS * (i + 1)]
        total = jnp.where(odd_lane, 0.0, jnp.sum(late, axis=0))
        late = jnp.where(odd_lane, late.reshape(16 * RANKS, 128), 0.0)
        lanes = slice(128 * i, 128 * i + 128)
        pick = core[256:384, lanes]
        pick2 = jnp.where(odd_lane, dot2(order, split(late)), pick)
        t1 = dot3(blocks([jnp.where(odd[j], slot_tile, first_tile) for j in range(4)]), split(pick), NT)
        t2 = dot3(blocks([jnp.where(odd[j], slot_tile, second_tile) for j in range(4)]), split(pick2), NT)
        t3 = dot3(blocks([first_tile] * 4), split(core[0:128, lanes]), NT)
        t3 = t3 + dot3(blocks([second_tile] * 4), split(core[128:256, lanes]), NT)
        total = jnp.concatenate([total, jnp.zeros((128 - RANKS, 128), F32)], axis=0)
        total = dot2(rank_pick, split(total))
        spread = [jnp.concatenate([total[:, 32 * j : 32 * j + 32]] * 4, axis=1) for j in range(4)]
        t3 = t3 + jnp.concatenate(spread, axis=0)
        goal = own_cls ^ x_row
        t1 = jnp.where(label == (goal ^ l_ref[0]), t1, 0.0)
        t2 = jnp.where(label == (goal ^ l_ref[1]), t2, 0.0)
        t3 = jnp.where(label == goal, t3, 0.0)
        results.append(jnp.concatenate([t1, t2, t3], axis=1))
    finish(jnp.concatenate(results, axis=0), full, out_ref, left_ref)


def sent_rows(same, own_rows, count):
    return same + own_rows if count == SLOTS else -(-(same + own_rows) * count // SLOTS // 8) * 8


def send(out_ref, same, different, count):
    rows, late = same.shape[0], different.shape[1]
    if count == SLOTS:
        out_ref[:, 0:rows, :] = jnp.broadcast_to(same[None], (16, rows, 128))
        out_ref[:, rows : rows + late, :] = different
        return
    total = out_ref.shape[1]
    same = jnp.concatenate([same[:, 32 * j : 32 * j + count] for j in range(4)], axis=1)
    different = jnp.concatenate([different[:, :, 32 * j : 32 * j + count] for j in range(4)], axis=2)
    rest = rows - total
    side = [same[total:, 32 * k : 32 * k + 32] for k in range(3)] + [jnp.zeros((total - 3 * rest, 32), F32)]
    main = jnp.concatenate([same[0:total], jnp.concatenate(side, axis=0)], axis=1)
    out_ref[...] = jnp.broadcast_to(main[None], out_ref.shape)
    for k in range(3):
        start = 3 * rest + late * k
        out_ref[:, start : start + late, 96:128] = different[:, :, 32 * k : 32 * k + 32]


def receive(mid_ref, rows, late, count):
    if count == SLOTS:
        return mid_ref[:, 0:rows, :], mid_ref[:, rows : rows + late, :]
    total = mid_ref.shape[1]
    rest = rows - total

    def side(start, size):
        parts = [mid_ref[:, start + size * k : start + size * (k + 1), 96:128] for k in range(3)]
        return jnp.concatenate(parts, axis=2)

    def widen(x):
        gap = jnp.zeros((*x.shape[:2], 32 - count), F32)
        parts = []
        for j in range(4):
            parts += [x[:, :, count * j : count * j + count], gap]
        return jnp.concatenate(parts, axis=2)

    same = jnp.concatenate([mid_ref[:, :, 0:96], side(0, rest)], axis=1)
    return widen(same), widen(side(3 * rest, late))


def half_products(unroll, row_ref, col_ref, amp_ref, got_ref, i_ref, j_ref, pos_ref, half_ref):
    p, q = pos_ref[0], pos_ref[1]
    cls = row_ref[CLS : CLS + 1, :]
    own_cls = own(col_ref, q, CLS)
    panel = unpack(got_ref[...])
    lane = iota(panel.shape, 1)
    slot = col_ref[:, SLOT : SLOT + 1]
    wh, wl = split(jnp.where(lane < 64, panel, one(slot == lane - 64)))
    both = jnp.concatenate([wh, wl], axis=1)
    pair_cls = own_cls ^ cls

    @pl.loop(0, 2, unroll=unroll)
    def _(i):
        kept = [jnp.where(pair_cls == (i_ref[i] ^ j_ref[p * 4 + j]), amp_ref[i, j], 0.0) for j in range(4)]
        high, low = split(jnp.concatenate(kept, axis=0))
        first = dot(high, both)
        rows = pl.ds(pl.multiple_of(256 * i, 256), 256)
        half_ref[rows, :] = first[:, 0:128] + first[:, 128:256] + dot(low, wh)

    return [half_ref[64 * n : 64 * n + 64, :] for n in range(8)]


def left_factor(col_ref, got_ref, q):
    own_rank = own(col_ref, q, RANK)
    own_panel = unpack(got_ref[pl.ds(q, 1)])
    stacked = jnp.concatenate([own_panel[:, 0:32], own_panel[:, 32:64]], axis=0)
    ranks = jnp.concatenate([jnp.full_like(own_rank, -1), own_rank], axis=0)
    lane = iota((128, 128), 1)
    left = jnp.where(lane < 32, jnp.concatenate([stacked] * 4, axis=1), one(ranks == lane - 32))
    return jnp.transpose(jnp.where(lane < 48, left, 0.0))


def odd_even(row_ref, i_ref, j_ref, p):
    bits = row_ref[BITS : BITS + 1, 0:1]
    later = [parity(bits & (i_ref[1] ^ j_ref[p * 4 + j])) == 1 for j in range(4)]
    xs = [[jnp.where(later[j], i_ref[i] ^ j_ref[p * 4 + j], i_ref[1 - i] ^ j_ref[p * 4 + j]) for j in range(4)] for i in (1, 0)]
    return later, xs[0], xs[1]


def half_kernel(
    count, row_ref, col_ref, order_ref, amp_ref, got_ref, i_ref, j_ref, l_ref, pos_ref, out_ref, half_ref
):
    p, q = pos_ref[0], pos_ref[1]
    label = row_ref[LAB : LAB + 1, 0:128]
    own_cls = own(col_ref, q, CLS)
    own_small = own(col_ref, q, NUM) >= 0
    xs = [i_ref[n // 4] ^ j_ref[p * 4 + n % 4] for n in range(8)]
    parts = half_products(False, row_ref, col_ref, amp_ref, got_ref, i_ref, j_ref, pos_ref, half_ref)
    firsts = [part[:, 64:96] + jnp.where(own_small, part[:, 0:32], 0.0) for part in parts]
    left = left_factor(col_ref, got_ref, q)
    pair_cls = jnp.concatenate([own_cls ^ l_ref[0], own_cls ^ l_ref[1]], axis=0)
    both = [jnp.concatenate([part[:, 0:32], part[:, 32:64]], axis=0) for part in parts]
    spread = [
        jnp.where(label == (pair_cls ^ xs[n]), jnp.concatenate([both[n]] * 4, axis=1), 0.0) for n in range(8)
    ]
    sums = dot3(split(left[0:32]), split(jnp.concatenate(spread, axis=1)))
    seconds = dot2(left[32:48].astype(BF16), split(jnp.concatenate(both, axis=1)))
    order = order_ref[...]
    mains, lates = [], []
    for i in range(2):
        rows = jnp.concatenate([sums[:, 128 * n : 128 * n + 128] for n in range(4 * i, 4 * i + 4)], axis=0)
        by_spot = dot2(order, split(rows), NT).reshape(16, RANKS, 128)
        lates.append(by_spot + seconds[None, :, 128 * i : 128 * i + 128])
        mains.append(jnp.concatenate(firsts[4 * i : 4 * i + 4], axis=1))
    send(out_ref, jnp.concatenate(mains, axis=0), jnp.concatenate(lates, axis=1), count)


def half_paired_kernel(
    count, row_ref, col_ref, order_ref, amp_ref, got_ref, i_ref, j_ref, l_ref, pos_ref, out_ref, half_ref
):
    p, q = pos_ref[0], pos_ref[1]
    label = row_ref[LAB : LAB + 1, 0:128]
    own_cls = own(col_ref, q, CLS)
    own_small = own(col_ref, q, NUM) >= 0
    parts = half_products(True, row_ref, col_ref, amp_ref, got_ref, i_ref, j_ref, pos_ref, half_ref)
    later, _, even_x = odd_even(row_ref, i_ref, j_ref, p)
    odd = [jnp.where(later[j], parts[4 + j], parts[j]) for j in range(4)]
    even = [jnp.where(later[j], parts[j], parts[4 + j]) for j in range(4)]
    rows = jnp.concatenate([part[:, 64:96] + jnp.where(own_small, part[:, 0:32], 0.0) for part in odd], axis=1)
    left = left_factor(col_ref, got_ref, q)
    firsts = jnp.concatenate([part[:, 64:96] for part in even], axis=1)
    seconds = jnp.concatenate([part[:, 32:64] for part in odd], axis=1)
    few = jnp.concatenate([firsts, seconds], axis=1)
    few = dot2(left[32:48].astype(BF16), split(jnp.concatenate([few, few], axis=0)))
    pair_cls = jnp.concatenate([own_cls ^ l_ref[0], own_cls ^ l_ref[1]], axis=0)
    spread = []
    for j in range(4):
        both = jnp.concatenate([even[j][:, 0:32], even[j][:, 32:64]], axis=0)
        spread.append(jnp.where(label == (pair_cls ^ even_x[j]), jnp.concatenate([both] * 4, axis=1), 0.0))
    sums = dot3(split(left[0:32]), split(jnp.concatenate(spread, axis=1)))
    sums = jnp.concatenate([sums[:, 128 * j : 128 * j + 128] for j in range(4)], axis=0)
    order = order_ref[...]
    rows = jnp.concatenate([rows, few[:, 0:128], few[:, 128:256]], axis=0)
    send(out_ref, rows, dot2(order, split(sums), NT).reshape(16, RANKS, 128), count)


def ladder_paired_kernel(
    count, row_ref, col_ref, order_ref, got_ref, mid_ref, i_ref, j_ref, l_ref, pos_ref, out_ref, left_ref
):
    p, q = pos_ref[0], pos_ref[1]
    cls = row_ref[CLS : CLS + 1, :]
    number = row_ref[NUM : NUM + 1, :]
    label = row_ref[LAB : LAB + 1, 0:128]
    label_col = col_ref[0:128, LAB : LAB + 1]
    width = cls.shape[1]
    turned = jnp.transpose(unpack(got_ref[...]))
    full = [
        jnp.where(label_col == (cls ^ l_ref[n]), jnp.concatenate([turned[32 * n : 32 * n + 32]] * 4, axis=0), 0.0)
        for n in range(2)
    ]
    full = split(jnp.concatenate(full + [one(number == iota((128, width), 0))], axis=0))
    rows, sums = receive(mid_ref, 64 + 2 * RANKS, RANKS, count)
    core = dot3(full, split(rows[:, 0:64].reshape(width, 128)))
    order = order_ref[...]
    few = [rows[:, 64 + RANKS * k : 64 + RANKS * (k + 1)].reshape(16 * RANKS, 128) for k in range(2)]
    small_rows, second_rows = [dot2(order, split(few[k])) for k in range(2)]
    total = jnp.concatenate([jnp.sum(sums, axis=0), jnp.zeros((128 - RANKS, 128), F32)], axis=0)
    own_panel = unpack(got_ref[pl.ds(q, 1)])
    own_slot = own(col_ref, q, SLOT)
    own_rank = own(col_ref, q, RANK)
    own_cls = own(col_ref, q, CLS)
    lane = iota((64, 128), 1)

    def blocks(tile):
        return split(jnp.concatenate([jnp.where((lane >> 5) == j, tile, 0.0) for j in range(4)], axis=0))

    first = blocks(jnp.concatenate([own_panel[:, 0:32]] * 4, axis=1))
    second = blocks(jnp.concatenate([own_panel[:, 32:64]] * 4, axis=1))
    slots = blocks(one(own_slot == (lane & 31)))[0]
    total = dot2(one(own_rank == lane).astype(BF16), split(total))
    total = [jnp.concatenate([total[:, 32 * j : 32 * j + 32]] * 4, axis=1) for j in range(4)]
    odd = [
        dot2(slots, split(core[256:384]), NT),
        dot2(slots, split(second_rows), NT),
        dot3(first, split(core[0:128]), NT) + dot3(second, split(core[128:256]), NT),
    ]
    small_rows = split(small_rows)
    even = [dot3(first, small_rows, NT), dot3(second, small_rows, NT), jnp.concatenate(total, axis=0)]
    later, odd_x, even_x = odd_even(row_ref, i_ref, j_ref, p)
    rows = [None] * 8
    for j in range(4):
        kinds = []
        for parts, x in ((odd, odd_x[j]), (even, even_x[j])):
            goal = own_cls ^ x
            labels = (goal ^ l_ref[0], goal ^ l_ref[1], goal)
            kinds.append(
                jnp.concatenate(
                    [jnp.where(label == labels[k], parts[k][64 * j : 64 * j + 64], 0.0) for k in range(3)], axis=1
                )
            )
        rows[j] = jnp.where(later[j], kinds[1], kinds[0])
        rows[4 + j] = jnp.where(later[j], kinds[0], kinds[1])
    finish(jnp.concatenate(rows, axis=0), full, out_ref, left_ref)


VMEM = pl.BlockSpec(memory_space=pltpu.VMEM)
SMEM = pl.BlockSpec(memory_space=pltpu.SMEM)
PARAMS = pltpu.CompilerParams(vmem_limit_bytes=48 * 1024 * 1024)


def shape(*dims, dtype=F32):
    return jax.ShapeDtypeStruct(dims, dtype)


def compact(kernels, same, late, count, row, col, order, turn, panel, amplitudes, irrep_i, irrep_j, irrep_l, pos):
    panel = lax.all_to_all(panel, "ja", split_axis=0, concat_axis=0, tiled=True)
    mid = pl.pallas_call(
        functools.partial(kernels[0], count),
        out_shape=shape(16, sent_rows(same, late, count), 128),
        in_specs=[VMEM] * 5 + [SMEM] * 4,
        out_specs=VMEM,
        scratch_shapes=[pltpu.VMEM((512, 128), F32)],
        compiler_params=PARAMS,
        name="half_slots",
    )(row, col, order, amplitudes, panel, irrep_i, irrep_j, irrep_l, pos)
    mid = lax.all_to_all(mid, "aa", split_axis=0, concat_axis=0, tiled=True)
    return pl.pallas_call(
        functools.partial(kernels[1], count),
        out_shape=shape(*amplitudes.shape),
        in_specs=[VMEM] * 5 + [SMEM] * 4,
        out_specs=VMEM,
        scratch_shapes=[pltpu.VMEM((512, 12 * SLOTS), F32)],
        compiler_params=PARAMS,
        name="ladder_slots",
    )(row, col, turn, panel, mid, irrep_i, irrep_j, irrep_l, pos)


def panel_rows(half_ref, other_ref, core, high_ref, low_ref):
    @pl.loop(0, half_ref.shape[0])
    def _(k):
        for part, ref in ((core, half_ref), (1 - core, other_ref)):
            rows = pl.ds(pl.multiple_of((2 * k + part) * 64, 64), 64)
            high_ref[rows, :], low_ref[rows, :] = split(ref[k])


def dense_half_kernel(
    row_ref, col_ref, amp_ref, half_ref, other_ref, i_ref, j_ref, pos_ref, out_ref, ph_ref, pl_ref, high_ref, low_ref
):
    p, q = pos_ref[0], pos_ref[1]
    panel_rows(half_ref, other_ref, p & 1, ph_ref, pl_ref)
    pair_cls = own(col_ref, q, CLS) ^ row_ref[CLS : CLS + 1, :]

    @pl.loop(0, 8)
    def _(n):
        i, j = n >> 2, n & 3
        kept = jnp.where(pair_cls == (i_ref[i] ^ j_ref[p * 4 + j]), amp_ref[i, j], 0.0)
        rows = pl.ds(pl.multiple_of(64 * n, 64), 64)
        high_ref[rows, :], low_ref[rows, :] = split(kept)

    @pl.loop(0, 2)
    def _(k):
        rows = pl.ds(pl.multiple_of(512 * k, 512), 512)
        result = dot3((ph_ref[rows, :], pl_ref[rows, :]), (high_ref[...], low_ref[...]), NT)
        out_ref[pl.ds(8 * k, 8)] = result.reshape(8, 64, 512)


def dense_ladder_kernel(row_ref, col_ref, mid_ref, half_ref, other_ref, i_ref, j_ref, pos_ref, *refs):
    p, q = pos_ref[0], pos_ref[1]
    acc_ref = refs[0] if len(refs) == 6 else None
    out_ref, ph_ref, pl_ref, high_ref, low_ref = refs[-5:]
    panel_rows(half_ref, other_ref, p & 1, ph_ref, pl_ref)
    first = iota((64, 128), 1) < 64

    @pl.loop(0, 4)
    def _(k):
        lanes = pl.ds(pl.multiple_of(128 * k, 128), 128)
        pairs = [(mid_ref[s, :, lanes], mid_ref[s + 1, :, lanes]) for s in range(0, 16, 2)]
        left = [jnp.where(first, a, jnp.roll(b, 64, axis=1)) for a, b in pairs]
        right = [jnp.where(first, jnp.roll(a, 64, axis=1), b) for a, b in pairs]
        rows = pl.ds(pl.multiple_of(128 * k, 128), 128)
        whole = jnp.concatenate([jnp.concatenate(left, axis=1), jnp.concatenate(right, axis=1)], axis=0)
        high_ref[rows, :], low_ref[rows, :] = split(whole)

    pair_cls = own(col_ref, q, CLS) ^ row_ref[CLS : CLS + 1, :]

    @pl.loop(0, 2)
    def _(i):
        rows = pl.ds(pl.multiple_of(256 * i, 256), 256)
        result = dot3((high_ref[rows, :], low_ref[rows, :]), (ph_ref[...], pl_ref[...]))
        for j in range(4):
            x = i_ref[i] ^ j_ref[p * 4 + j]
            kept = jnp.where(pair_cls == x, result[64 * j : 64 * j + 64], 0.0)
            out_ref[i, j] = kept if acc_ref is None else acc_ref[i, j] + kept


CORES = [[2 * k + core for k in range(8)] for core in (0, 1)]


def dense(row, col, acc, amplitudes, panel, irrep_i, irrep_j, pos):
    half = jnp.broadcast_to(panel[None], (8, *panel.shape))
    half = lax.all_to_all(half, "ja", split_axis=0, concat_axis=0, tiled=True, axis_index_groups=CORES)
    other = lax.ppermute(half, "ja", [(n, n ^ 1) for n in range(16)])
    halves = [pltpu.VMEM((1024, 1024), BF16)] * 2 + [pltpu.VMEM((512, 1024), BF16)] * 2
    mid = pl.pallas_call(
        dense_half_kernel,
        out_shape=shape(16, 64, 512),
        in_specs=[VMEM] * 5 + [SMEM] * 3,
        out_specs=VMEM,
        scratch_shapes=halves,
        compiler_params=PARAMS,
        name="half_dense",
    )(row, col, amplitudes, half, other, irrep_i, irrep_j, pos)
    mid = lax.all_to_all(mid, "aa", split_axis=0, concat_axis=0, tiled=True)
    so_far = [] if acc is None else [acc]
    return pl.pallas_call(
        dense_ladder_kernel,
        out_shape=shape(*amplitudes.shape),
        in_specs=[VMEM] * 5 + [SMEM] * 3 + [VMEM] * len(so_far),
        out_specs=VMEM,
        scratch_shapes=halves,
        input_output_aliases={8: 0} if so_far else {},
        compiler_params=PARAMS,
        name="ladder_dense",
    )(row, col, mid, half, other, irrep_i, irrep_j, pos, *so_far)


def local(amplitudes, chol, irrep_i, irrep_j, irrep_v, irrep_l):
    pos = jnp.stack([lax.axis_index("ja"), lax.axis_index("aa")]).astype(I32)
    width = irrep_v.shape[0]
    row, col, order, turn, slots, rows, branch = pl.pallas_call(
        table_kernel,
        out_shape=(
            shape(8, width, dtype=I32),
            shape(width, 128, dtype=I32),
            shape(16 * RANKS, 4 * SLOTS, dtype=BF16),
            shape(4 * SLOTS, 16 * RANKS, dtype=BF16),
            shape(16, 32, 128),
            shape(chol.shape[1], width),
            shape(1, dtype=I32),
        ),
        in_specs=[VMEM, VMEM, SMEM, SMEM, SMEM],
        out_specs=(VMEM,) * 6 + (SMEM,),
        compiler_params=PARAMS,
        name="orbital_table",
    )(irrep_v.reshape(1, width), chol, irrep_i, irrep_l, pos)
    height = chol.shape[1]

    def together():
        return dense(row, col, None, amplitudes, rows, irrep_i, irrep_j, pos)

    def apart():
        own_rows = lax.dynamic_slice_in_dim(irrep_v, pos[0] * height, height)
        keep = (own_rows[:, None] ^ irrep_v[None, :]) == irrep_l[0]

        def step(n, acc):
            panel = jnp.where(keep, jnp.where(n == 0, chol[0], chol[1]), 0.0)
            return dense(row, col, acc, amplitudes, panel, irrep_i, irrep_j, pos)

        return lax.fori_loop(0, 2, step, jnp.zeros_like(amplitudes))

    few = (row, col, order, turn, slots, amplitudes, irrep_i, irrep_j, irrep_l, pos)
    paired = ((half_paired_kernel, ladder_paired_kernel), 64 + 2 * RANKS, RANKS)
    general = ((half_kernel, ladder_kernel), 128, 2 * RANKS)
    return lax.switch(
        branch[0],
        [
            lambda: compact(*paired, TIGHT, *few),
            lambda: compact(*general, TIGHT, *few),
            lambda: compact(*general, SLOTS, *few),
            together,
            apart,
        ],
    )


def solution(mesh):
    in_specs = (P(None, "ja", "aa", None), P(None, "ja", None), P(), P(), P(), P())
    out_specs = P(None, "ja", "aa", None)
    return jax.shard_map(local, mesh=mesh, in_specs=in_specs, out_specs=out_specs, check_vma=False)
```

```python
import functools

import jax
import jax.numpy as jnp
from jax import lax
from jax.experimental import pallas as pl
from jax.experimental.pallas import tpu as pltpu
from jax.sharding import PartitionSpec as P

F32, BF16, I32 = jnp.float32, jnp.bfloat16, jnp.int32
NN = (((1,), (0,)), ((), ()))
NT = (((1,), (1,)), ((), ()))
SLOTS = 32
TIGHT = 24
RANKS = 16
CLS, NUM, SLOT, SPOT, LAB, RANK, BRANCH, BITS = range(8)


def iota(shape, dim):
    return lax.broadcasted_iota(I32, shape, dim)


def parity(x):
    return (x ^ (x >> 1) ^ (x >> 2)) & 1


def one(cond):
    return jnp.where(cond, 1.0, 0.0).astype(F32)


def dot(a, b, dims=NN):
    return lax.dot_general(a, b, dims, preferred_element_type=F32)


def split(x):
    high = x.astype(BF16)
    return high, (x - high.astype(F32)).astype(BF16)


def dot3(a, b, dims=NN):
    (ah, al), (bh, bl) = a, b
    return dot(ah, bh, dims) + dot(ah, bl, dims) + dot(al, bh, dims)


def dot2(a, b, dims=NN):
    return dot(a, b[0], dims) + dot(a, b[1], dims)


def table_kernel(irrep_ref, chol_ref, i_ref, l_ref, pos_ref, row_ref, col_ref, order_ref, turn_ref, out_ref, rows_ref, branch_ref):
    cls = irrep_ref[...]
    width = cls.shape[1]
    chunks = width // 128
    onehot = one(cls == iota((16, width), 0))
    before = one(iota((128, 128), 0) < iota((128, 128), 1))
    count = jnp.zeros((16, 1), F32)
    blocks = jnp.zeros((16, 128), F32)
    slots = []
    for k in range(chunks):
        part = onehot[:, 128 * k : 128 * k + 128]
        ahead = dot(part.astype(BF16), before.astype(BF16)) + count
        slots.append(jnp.sum(part * ahead, axis=0, keepdims=True))
        count = count + jnp.sum(part, axis=1, keepdims=True)
        place = one(iota((128, 128), 1) == 2 * k + (iota((128, 128), 0) >> 6))
        blocks = blocks + dot(part.astype(BF16), place.astype(BF16))
    slot = jnp.concatenate(slots, axis=1).astype(I32)
    lane = iota((16, 128), 1)
    cand = iota((16, 128), 0)
    count_lane = jnp.sum(jnp.where(lane == cand, count, 0.0), axis=0, keepdims=True)
    member = (parity((cand >> 1) & lane) == (cand & 1)) & (lane < 8)
    largest = jnp.max(jnp.where(member, count_lane, 0.0), axis=1, keepdims=True)
    in_block = jnp.zeros((16, 128), F32)
    for g in range(8):
        in_block = in_block + jnp.where(parity((cand >> 1) & g) == (cand & 1), blocks[g : g + 1, :], 0.0)
    fullest = jnp.max(in_block, axis=1, keepdims=True)
    bits_col = cand[:, 0:1] >> 1
    good = (largest <= SLOTS) & (fullest <= RANKS)
    for n in range(l_ref.shape[0]):
        good = good & (parity(bits_col & l_ref[n]) == 1)
    paired = parity(bits_col & (i_ref[0] ^ i_ref[1])) == 1
    rank = cand[:, 0:1] + jnp.where(largest <= TIGHT, jnp.where(paired, 0, 16), 32)
    pick = jnp.min(jnp.where(good, rank.astype(F32), 99.0), axis=0, keepdims=True).astype(I32)
    branch = jnp.where(pick < 48, pick >> 4, jnp.where(l_ref[0] != l_ref[1], 3, 4))
    bits, side = (pick & 15) >> 1, pick & 1
    small = parity(bits & cls) == side
    group = jnp.zeros_like(cls)
    label = jnp.zeros_like(cls)
    lane_group = iota((1, width), 1) >> 5
    number = jnp.zeros((1, 1), I32)
    for g in range(8):
        is_small = parity(bits & g) == side
        group = group + jnp.where(is_small & (cls > g), 1, 0)
        label = label + jnp.where(is_small & (number == lane_group), g, 0)
        number = number + jnp.where(is_small, 1, 0)
    inner = one((iota((128, 128), 0) < iota((128, 128), 1)) & ((iota((128, 128), 0) >> 6) == (iota((128, 128), 1) >> 6)))
    small16 = jnp.broadcast_to(one(small), (16, width))
    ranks = [
        dot(small16[:, 128 * k : 128 * k + 128].astype(BF16), inner.astype(BF16))[0:1, :] for k in range(chunks)
    ]
    rank = jnp.concatenate(ranks, axis=1).astype(I32)
    none = jnp.full_like(cls, -1)
    table = jnp.concatenate(
        [
            cls,
            jnp.where(small, group * SLOTS + slot, none),
            jnp.where(small, slot, none),
            jnp.where(small, (iota((1, width), 1) >> 6) * RANKS + rank, none),
            label,
            jnp.where(small, rank, none),
            jnp.broadcast_to(branch, cls.shape),
            jnp.broadcast_to(bits, cls.shape),
        ],
        axis=0,
    )
    row_ref[...] = table
    branch_ref[0] = jnp.max(branch.astype(F32)).astype(I32)
    table = table.astype(F32)
    for k in range(chunks):
        tile = jnp.concatenate([table[:, 128 * k : 128 * k + 128], jnp.zeros((120, 128), F32)], axis=0)
        col_ref[128 * k : 128 * k + 128, :] = jnp.transpose(tile).astype(I32)
    spots, numbers = places(row_ref)
    order_ref[...] = dot(spots, numbers, NT).astype(BF16)
    turn_ref[...] = dot(numbers, spots, NT).astype(BF16)
    panel_slots(row_ref, col_ref, chol_ref, l_ref, pos_ref, out_ref, rows_ref)


def own(col_ref, block, field):
    return col_ref[pl.ds(pl.multiple_of(block * 64, 64), 64), field : field + 1]


def panel_slots(row_ref, col_ref, chol_ref, l_ref, pos_ref, out_ref, rows_ref):
    cls = row_ref[CLS : CLS + 1, :]
    slot = row_ref[SLOT : SLOT + 1, :]
    own_cls = own(col_ref, pos_ref[0], CLS)
    pick = one(slot == iota((SLOTS, slot.shape[1]), 0)).astype(BF16)
    parts = []
    kept_all = [jnp.where((own_cls ^ cls) == l_ref[n], chol_ref[n], 0.0) for n in range(2)]
    rows_ref[...] = kept_all[0] + kept_all[1]
    for kept in kept_all:
        high, low = split(kept)
        parts.append(dot(high, pick, NT) + dot(low, pick, NT))
    both = jnp.concatenate(parts, axis=1)
    packed = jnp.concatenate([both[0:32], both[32:64]], axis=1)
    out_ref[...] = jnp.broadcast_to(packed[None], out_ref.shape)


def unpack(gathered):
    n = gathered.shape[0]
    return jnp.concatenate([gathered, jnp.roll(gathered, 64, axis=2)], axis=1).reshape(n * 64, 128)


def places(row_ref):
    spot = row_ref[SPOT : SPOT + 1, :]
    number = row_ref[NUM : NUM + 1, :]
    width = spot.shape[1]
    spots = one(spot == iota((16 * RANKS, width), 0)).astype(BF16)
    numbers = one(number == iota((4 * SLOTS, width), 0)).astype(BF16)
    return spots, numbers


def finish(left, full, out_ref, left_ref):
    left_ref[...] = left

    @pl.loop(0, 2)
    def _(i):
        rows = pl.ds(pl.multiple_of(256 * i, 256), 256)
        picks = 8 * SLOTS
        high, low = split(left_ref[rows, :])
        result = dot(high, full[0]) + dot(high[:, 0:picks], full[1][0:picks]) + dot(low, full[0])
        out_ref[i] = result.reshape(4, 64, full[0].shape[1])


def ladder_kernel(
    count, row_ref, col_ref, order_ref, got_ref, mid_ref, i_ref, j_ref, l_ref, pos_ref, out_ref, left_ref
):
    p, q = pos_ref[0], pos_ref[1]
    cls = row_ref[CLS : CLS + 1, :]
    number = row_ref[NUM : NUM + 1, :]
    label = row_ref[LAB : LAB + 1, 0:128]
    bits = row_ref[BITS : BITS + 1, 0:1]
    label_col = col_ref[0:128, LAB : LAB + 1]
    width = cls.shape[1]
    turned = jnp.transpose(unpack(got_ref[...]))
    full = [
        jnp.where(label_col == (cls ^ l_ref[n]), jnp.concatenate([turned[32 * n : 32 * n + 32]] * 4, axis=0), 0.0)
        for n in range(2)
    ]
    full = split(jnp.concatenate(full + [one(number == iota((128, width), 0))], axis=0))
    rows, lates = receive(mid_ref, 128, 2 * RANKS, count)
    mids = [rows[:, 64 * i : 64 * i + 64].reshape(width, 128) for i in range(2)]
    core = dot3(full, split(jnp.concatenate(mids, axis=1)))
    order = order_ref[...]
    own_panel = unpack(got_ref[pl.ds(q, 1)])
    own_slot = own(col_ref, q, SLOT)
    own_rank = own(col_ref, q, RANK)
    own_cls = jnp.concatenate([own(col_ref, q, CLS)] * 4, axis=0)
    lane = iota((64, 128), 1)
    first_tile = jnp.concatenate([own_panel[:, 0:32]] * 4, axis=1)
    second_tile = jnp.concatenate([own_panel[:, 32:64]] * 4, axis=1)
    slot_tile = one(own_slot == (lane & 31))
    rank_pick = one(own_rank == lane).astype(BF16)
    lane_row = iota((1, 128), 1) >> 5
    results = []
    for i in range(2):
        xs = [i_ref[i] ^ j_ref[p * 4 + j] for j in range(4)]
        x_lane = jnp.zeros((1, 128), I32)
        x_row = jnp.zeros((256, 1), I32)
        for j in range(4):
            x_lane = jnp.where(lane_row == j, xs[j], x_lane)
            x_row = jnp.where((iota((256, 1), 0) >> 6) == j, xs[j], x_row)
        odd_lane = parity(x_lane & bits) == 1
        odd = [parity(bits & xs[j]) == 1 for j in range(4)]

        def blocks(tiles):
            return split(
                jnp.concatenate([jnp.where((lane >> 5) == j, tiles[j], 0.0) for j in range(4)], axis=0)
            )

        late = lates[:, RANKS * i : RANKS * (i + 1)]
        total = jnp.where(odd_lane, 0.0, jnp.sum(late, axis=0))
        late = jnp.where(odd_lane, late.reshape(16 * RANKS, 128), 0.0)
        lanes = slice(128 * i, 128 * i + 128)
        pick = core[256:384, lanes]
        pick2 = jnp.where(odd_lane, dot2(order, split(late)), pick)
        t1 = dot3(blocks([jnp.where(odd[j], slot_tile, first_tile) for j in range(4)]), split(pick), NT)
        t2 = dot3(blocks([jnp.where(odd[j], slot_tile, second_tile) for j in range(4)]), split(pick2), NT)
        t3 = dot3(blocks([first_tile] * 4), split(core[0:128, lanes]), NT)
        t3 = t3 + dot3(blocks([second_tile] * 4), split(core[128:256, lanes]), NT)
        total = jnp.concatenate([total, jnp.zeros((128 - RANKS, 128), F32)], axis=0)
        total = dot2(rank_pick, split(total))
        spread = [jnp.concatenate([total[:, 32 * j : 32 * j + 32]] * 4, axis=1) for j in range(4)]
        t3 = t3 + jnp.concatenate(spread, axis=0)
        goal = own_cls ^ x_row
        t1 = jnp.where(label == (goal ^ l_ref[0]), t1, 0.0)
        t2 = jnp.where(label == (goal ^ l_ref[1]), t2, 0.0)
        t3 = jnp.where(label == goal, t3, 0.0)
        results.append(jnp.concatenate([t1, t2, t3], axis=1))
    finish(jnp.concatenate(results, axis=0), full, out_ref, left_ref)


def sent_rows(same, own_rows, count):
    return same + own_rows if count == SLOTS else -(-(same + own_rows) * count // SLOTS // 8) * 8


def send(out_ref, same, different, count):
    rows, late = same.shape[0], different.shape[1]
    if count == SLOTS:
        out_ref[:, 0:rows, :] = jnp.broadcast_to(same[None], (16, rows, 128))
        out_ref[:, rows : rows + late, :] = different
        return
    total = out_ref.shape[1]
    same = jnp.concatenate([same[:, 32 * j : 32 * j + count] for j in range(4)], axis=1)
    different = jnp.concatenate([different[:, :, 32 * j : 32 * j + count] for j in range(4)], axis=2)
    rest = rows - total
    side = [same[total:, 32 * k : 32 * k + 32] for k in range(3)] + [jnp.zeros((total - 3 * rest, 32), F32)]
    main = jnp.concatenate([same[0:total], jnp.concatenate(side, axis=0)], axis=1)
    out_ref[...] = jnp.broadcast_to(main[None], out_ref.shape)
    for k in range(3):
        start = 3 * rest + late * k
        out_ref[:, start : start + late, 96:128] = different[:, :, 32 * k : 32 * k + 32]


def receive(mid_ref, rows, late, count):
    if count == SLOTS:
        return mid_ref[:, 0:rows, :], mid_ref[:, rows : rows + late, :]
    total = mid_ref.shape[1]
    rest = rows - total

    def side(start, size):
        parts = [mid_ref[:, start + size * k : start + size * (k + 1), 96:128] for k in range(3)]
        return jnp.concatenate(parts, axis=2)

    def widen(x):
        gap = jnp.zeros((*x.shape[:2], 32 - count), F32)
        parts = []
        for j in range(4):
            parts += [x[:, :, count * j : count * j + count], gap]
        return jnp.concatenate(parts, axis=2)

    same = jnp.concatenate([mid_ref[:, :, 0:96], side(0, rest)], axis=1)
    return widen(same), widen(side(3 * rest, late))


def half_products(row_ref, col_ref, amp_ref, got_ref, i_ref, j_ref, pos_ref, half_ref):
    p, q = pos_ref[0], pos_ref[1]
    cls = row_ref[CLS : CLS + 1, :]
    own_cls = own(col_ref, q, CLS)
    panel = unpack(got_ref[...])
    lane = iota(panel.shape, 1)
    slot = col_ref[:, SLOT : SLOT + 1]
    wh, wl = split(jnp.where(lane < 64, panel, one(slot == lane - 64)))
    both = jnp.concatenate([wh, wl], axis=1)
    pair_cls = own_cls ^ cls

    @pl.loop(0, 2, unroll=True)
    def _(i):
        kept = [jnp.where(pair_cls == (i_ref[i] ^ j_ref[p * 4 + j]), amp_ref[i, j], 0.0) for j in range(4)]
        high, low = split(jnp.concatenate(kept, axis=0))
        first = dot(high, both)
        rows = pl.ds(pl.multiple_of(256 * i, 256), 256)
        half_ref[rows, :] = first[:, 0:128] + first[:, 128:256] + dot(low, wh)

    return [half_ref[64 * n : 64 * n + 64, :] for n in range(8)]


def left_factor(col_ref, got_ref, q):
    own_rank = own(col_ref, q, RANK)
    own_panel = unpack(got_ref[pl.ds(q, 1)])
    stacked = jnp.concatenate([own_panel[:, 0:32], own_panel[:, 32:64]], axis=0)
    ranks = jnp.concatenate([jnp.full_like(own_rank, -1), own_rank], axis=0)
    lane = iota((128, 128), 1)
    left = jnp.where(lane < 32, jnp.concatenate([stacked] * 4, axis=1), one(ranks == lane - 32))
    return jnp.transpose(jnp.where(lane < 48, left, 0.0))


def odd_even(row_ref, i_ref, j_ref, p):
    bits = row_ref[BITS : BITS + 1, 0:1]
    later = [parity(bits & (i_ref[1] ^ j_ref[p * 4 + j])) == 1 for j in range(4)]
    xs = [[jnp.where(later[j], i_ref[i] ^ j_ref[p * 4 + j], i_ref[1 - i] ^ j_ref[p * 4 + j]) for j in range(4)] for i in (1, 0)]
    return later, xs[0], xs[1]


def half_kernel(
    count, row_ref, col_ref, order_ref, amp_ref, got_ref, i_ref, j_ref, l_ref, pos_ref, out_ref, half_ref
):
    p, q = pos_ref[0], pos_ref[1]
    label = row_ref[LAB : LAB + 1, 0:128]
    own_cls = own(col_ref, q, CLS)
    own_small = own(col_ref, q, NUM) >= 0
    xs = [i_ref[n // 4] ^ j_ref[p * 4 + n % 4] for n in range(8)]
    parts = half_products(row_ref, col_ref, amp_ref, got_ref, i_ref, j_ref, pos_ref, half_ref)
    firsts = [part[:, 64:96] + jnp.where(own_small, part[:, 0:32], 0.0) for part in parts]
    left = left_factor(col_ref, got_ref, q)
    pair_cls = jnp.concatenate([own_cls ^ l_ref[0], own_cls ^ l_ref[1]], axis=0)
    both = [jnp.concatenate([part[:, 0:32], part[:, 32:64]], axis=0) for part in parts]
    spread = [
        jnp.where(label == (pair_cls ^ xs[n]), jnp.concatenate([both[n]] * 4, axis=1), 0.0) for n in range(8)
    ]
    sums = dot3(split(left[0:32]), split(jnp.concatenate(spread, axis=1)))
    seconds = dot2(left[32:48].astype(BF16), split(jnp.concatenate(both, axis=1)))
    order = order_ref[...]
    mains, lates = [], []
    for i in range(2):
        rows = jnp.concatenate([sums[:, 128 * n : 128 * n + 128] for n in range(4 * i, 4 * i + 4)], axis=0)
        by_spot = dot2(order, split(rows), NT).reshape(16, RANKS, 128)
        lates.append(by_spot + seconds[None, :, 128 * i : 128 * i + 128])
        mains.append(jnp.concatenate(firsts[4 * i : 4 * i + 4], axis=1))
    send(out_ref, jnp.concatenate(mains, axis=0), jnp.concatenate(lates, axis=1), count)


def half_paired_kernel(
    count, row_ref, col_ref, order_ref, amp_ref, got_ref, i_ref, j_ref, l_ref, pos_ref, out_ref, half_ref
):
    p, q = pos_ref[0], pos_ref[1]
    label = row_ref[LAB : LAB + 1, 0:128]
    own_cls = own(col_ref, q, CLS)
    own_small = own(col_ref, q, NUM) >= 0
    parts = half_products(row_ref, col_ref, amp_ref, got_ref, i_ref, j_ref, pos_ref, half_ref)
    later, _, even_x = odd_even(row_ref, i_ref, j_ref, p)
    odd = [jnp.where(later[j], parts[4 + j], parts[j]) for j in range(4)]
    even = [jnp.where(later[j], parts[j], parts[4 + j]) for j in range(4)]
    rows = jnp.concatenate([part[:, 64:96] + jnp.where(own_small, part[:, 0:32], 0.0) for part in odd], axis=1)
    left = left_factor(col_ref, got_ref, q)
    firsts = jnp.concatenate([part[:, 64:96] for part in even], axis=1)
    seconds = jnp.concatenate([part[:, 32:64] for part in odd], axis=1)
    few = jnp.concatenate([firsts, seconds], axis=1)
    few = dot2(left[32:48].astype(BF16), split(jnp.concatenate([few, few], axis=0)))
    pair_cls = jnp.concatenate([own_cls ^ l_ref[0], own_cls ^ l_ref[1]], axis=0)
    spread = []
    for j in range(4):
        both = jnp.concatenate([even[j][:, 0:32], even[j][:, 32:64]], axis=0)
        spread.append(jnp.where(label == (pair_cls ^ even_x[j]), jnp.concatenate([both] * 4, axis=1), 0.0))
    sums = dot3(split(left[0:32]), split(jnp.concatenate(spread, axis=1)))
    sums = jnp.concatenate([sums[:, 128 * j : 128 * j + 128] for j in range(4)], axis=0)
    order = order_ref[...]
    rows = jnp.concatenate([rows, few[:, 0:128], few[:, 128:256]], axis=0)
    send(out_ref, rows, dot2(order, split(sums), NT).reshape(16, RANKS, 128), count)


def ladder_paired_kernel(
    count, row_ref, col_ref, order_ref, got_ref, mid_ref, i_ref, j_ref, l_ref, pos_ref, out_ref, left_ref
):
    p, q = pos_ref[0], pos_ref[1]
    cls = row_ref[CLS : CLS + 1, :]
    number = row_ref[NUM : NUM + 1, :]
    label = row_ref[LAB : LAB + 1, 0:128]
    label_col = col_ref[0:128, LAB : LAB + 1]
    width = cls.shape[1]
    turned = jnp.transpose(unpack(got_ref[...]))
    full = [
        jnp.where(label_col == (cls ^ l_ref[n]), jnp.concatenate([turned[32 * n : 32 * n + 32]] * 4, axis=0), 0.0)
        for n in range(2)
    ]
    full = split(jnp.concatenate(full + [one(number == iota((128, width), 0))], axis=0))
    rows, sums = receive(mid_ref, 64 + 2 * RANKS, RANKS, count)
    core = dot3(full, split(rows[:, 0:64].reshape(width, 128)))
    order = order_ref[...]
    few = [rows[:, 64 + RANKS * k : 64 + RANKS * (k + 1)].reshape(16 * RANKS, 128) for k in range(2)]
    small_rows, second_rows = [dot2(order, split(few[k])) for k in range(2)]
    total = jnp.concatenate([jnp.sum(sums, axis=0), jnp.zeros((128 - RANKS, 128), F32)], axis=0)
    own_panel = unpack(got_ref[pl.ds(q, 1)])
    own_slot = own(col_ref, q, SLOT)
    own_rank = own(col_ref, q, RANK)
    own_cls = own(col_ref, q, CLS)
    lane = iota((64, 128), 1)

    def blocks(tile):
        return split(jnp.concatenate([jnp.where((lane >> 5) == j, tile, 0.0) for j in range(4)], axis=0))

    first = blocks(jnp.concatenate([own_panel[:, 0:32]] * 4, axis=1))
    second = blocks(jnp.concatenate([own_panel[:, 32:64]] * 4, axis=1))
    slots = blocks(one(own_slot == (lane & 31)))[0]
    total = dot2(one(own_rank == lane).astype(BF16), split(total))
    total = [jnp.concatenate([total[:, 32 * j : 32 * j + 32]] * 4, axis=1) for j in range(4)]
    odd = [
        dot2(slots, split(core[256:384]), NT),
        dot2(slots, split(second_rows), NT),
        dot3(first, split(core[0:128]), NT) + dot3(second, split(core[128:256]), NT),
    ]
    small_rows = split(small_rows)
    even = [dot3(first, small_rows, NT), dot3(second, small_rows, NT), jnp.concatenate(total, axis=0)]
    later, odd_x, even_x = odd_even(row_ref, i_ref, j_ref, p)
    rows = [None] * 8
    for j in range(4):
        kinds = []
        for parts, x in ((odd, odd_x[j]), (even, even_x[j])):
            goal = own_cls ^ x
            labels = (goal ^ l_ref[0], goal ^ l_ref[1], goal)
            kinds.append(
                jnp.concatenate(
                    [jnp.where(label == labels[k], parts[k][64 * j : 64 * j + 64], 0.0) for k in range(3)], axis=1
                )
            )
        rows[j] = jnp.where(later[j], kinds[1], kinds[0])
        rows[4 + j] = jnp.where(later[j], kinds[0], kinds[1])
    finish(jnp.concatenate(rows, axis=0), full, out_ref, left_ref)


VMEM = pl.BlockSpec(memory_space=pltpu.VMEM)
SMEM = pl.BlockSpec(memory_space=pltpu.SMEM)
PARAMS = pltpu.CompilerParams(vmem_limit_bytes=48 * 1024 * 1024)


def shape(*dims, dtype=F32):
    return jax.ShapeDtypeStruct(dims, dtype)


def compact(kernels, same, late, count, row, col, order, turn, panel, amplitudes, irrep_i, irrep_j, irrep_l, pos):
    panel = lax.all_to_all(panel, "ja", split_axis=0, concat_axis=0, tiled=True)
    mid = pl.pallas_call(
        functools.partial(kernels[0], count),
        out_shape=shape(16, sent_rows(same, late, count), 128),
        in_specs=[VMEM] * 5 + [SMEM] * 4,
        out_specs=VMEM,
        scratch_shapes=[pltpu.VMEM((512, 128), F32)],
        compiler_params=PARAMS,
        name="half_slots",
    )(row, col, order, amplitudes, panel, irrep_i, irrep_j, irrep_l, pos)
    mid = lax.all_to_all(mid, "aa", split_axis=0, concat_axis=0, tiled=True)
    return pl.pallas_call(
        functools.partial(kernels[1], count),
        out_shape=shape(*amplitudes.shape),
        in_specs=[VMEM] * 5 + [SMEM] * 4,
        out_specs=VMEM,
        scratch_shapes=[pltpu.VMEM((512, 12 * SLOTS), F32)],
        compiler_params=PARAMS,
        name="ladder_slots",
    )(row, col, turn, panel, mid, irrep_i, irrep_j, irrep_l, pos)


def panel_rows(half_ref, other_ref, core, high_ref, low_ref):
    @pl.loop(0, half_ref.shape[0])
    def _(k):
        for part, ref in ((core, half_ref), (1 - core, other_ref)):
            rows = pl.ds(pl.multiple_of((2 * k + part) * 64, 64), 64)
            high_ref[rows, :], low_ref[rows, :] = split(ref[k])


def dense_half_kernel(
    row_ref, col_ref, amp_ref, half_ref, other_ref, i_ref, j_ref, pos_ref, out_ref, ph_ref, pl_ref, high_ref, low_ref
):
    p, q = pos_ref[0], pos_ref[1]
    panel_rows(half_ref, other_ref, p & 1, ph_ref, pl_ref)
    pair_cls = own(col_ref, q, CLS) ^ row_ref[CLS : CLS + 1, :]

    @pl.loop(0, 8)
    def _(n):
        i, j = n >> 2, n & 3
        kept = jnp.where(pair_cls == (i_ref[i] ^ j_ref[p * 4 + j]), amp_ref[i, j], 0.0)
        rows = pl.ds(pl.multiple_of(64 * n, 64), 64)
        high_ref[rows, :], low_ref[rows, :] = split(kept)

    @pl.loop(0, 2, unroll=True)
    def _(k):
        rows = pl.ds(pl.multiple_of(512 * k, 512), 512)
        result = dot3((ph_ref[rows, :], pl_ref[rows, :]), (high_ref[...], low_ref[...]), NT)
        out_ref[pl.ds(8 * k, 8)] = result.reshape(8, 64, 512)


def dense_ladder_kernel(row_ref, col_ref, mid_ref, half_ref, other_ref, i_ref, j_ref, pos_ref, *refs):
    p, q = pos_ref[0], pos_ref[1]
    acc_ref = refs[0] if len(refs) == 6 else None
    out_ref, ph_ref, pl_ref, high_ref, low_ref = refs[-5:]
    panel_rows(half_ref, other_ref, p & 1, ph_ref, pl_ref)
    first = iota((64, 128), 1) < 64

    @pl.loop(0, 4)
    def _(k):
        lanes = pl.ds(pl.multiple_of(128 * k, 128), 128)
        pairs = [(mid_ref[s, :, lanes], mid_ref[s + 1, :, lanes]) for s in range(0, 16, 2)]
        left = [jnp.where(first, a, jnp.roll(b, 64, axis=1)) for a, b in pairs]
        right = [jnp.where(first, jnp.roll(a, 64, axis=1), b) for a, b in pairs]
        rows = pl.ds(pl.multiple_of(128 * k, 128), 128)
        whole = jnp.concatenate([jnp.concatenate(left, axis=1), jnp.concatenate(right, axis=1)], axis=0)
        high_ref[rows, :], low_ref[rows, :] = split(whole)

    pair_cls = own(col_ref, q, CLS) ^ row_ref[CLS : CLS + 1, :]

    @pl.loop(0, 2)
    def _(i):
        rows = pl.ds(pl.multiple_of(256 * i, 256), 256)
        result = dot3((high_ref[rows, :], low_ref[rows, :]), (ph_ref[...], pl_ref[...]))
        for j in range(4):
            x = i_ref[i] ^ j_ref[p * 4 + j]
            kept = jnp.where(pair_cls == x, result[64 * j : 64 * j + 64], 0.0)
            out_ref[i, j] = kept if acc_ref is None else acc_ref[i, j] + kept


CORES = [[2 * k + core for k in range(8)] for core in (0, 1)]


def dense(row, col, acc, amplitudes, panel, irrep_i, irrep_j, pos):
    half = jnp.broadcast_to(panel[None], (8, *panel.shape))
    half = lax.all_to_all(half, "ja", split_axis=0, concat_axis=0, tiled=True, axis_index_groups=CORES)
    other = lax.ppermute(half, "ja", [(n, n ^ 1) for n in range(16)])
    halves = [pltpu.VMEM((1024, 1024), BF16)] * 2 + [pltpu.VMEM((512, 1024), BF16)] * 2
    mid = pl.pallas_call(
        dense_half_kernel,
        out_shape=shape(16, 64, 512),
        in_specs=[VMEM] * 5 + [SMEM] * 3,
        out_specs=VMEM,
        scratch_shapes=halves,
        compiler_params=PARAMS,
        name="half_dense",
    )(row, col, amplitudes, half, other, irrep_i, irrep_j, pos)
    mid = lax.all_to_all(mid, "aa", split_axis=0, concat_axis=0, tiled=True)
    so_far = [] if acc is None else [acc]
    return pl.pallas_call(
        dense_ladder_kernel,
        out_shape=shape(*amplitudes.shape),
        in_specs=[VMEM] * 5 + [SMEM] * 3 + [VMEM] * len(so_far),
        out_specs=VMEM,
        scratch_shapes=halves,
        input_output_aliases={8: 0} if so_far else {},
        compiler_params=PARAMS,
        name="ladder_dense",
    )(row, col, mid, half, other, irrep_i, irrep_j, pos, *so_far)


def local(amplitudes, chol, irrep_i, irrep_j, irrep_v, irrep_l):
    pos = jnp.stack([lax.axis_index("ja"), lax.axis_index("aa")]).astype(I32)
    width = irrep_v.shape[0]
    row, col, order, turn, slots, rows, branch = pl.pallas_call(
        table_kernel,
        out_shape=(
            shape(8, width, dtype=I32),
            shape(width, 128, dtype=I32),
            shape(16 * RANKS, 4 * SLOTS, dtype=BF16),
            shape(4 * SLOTS, 16 * RANKS, dtype=BF16),
            shape(16, 32, 128),
            shape(chol.shape[1], width),
            shape(1, dtype=I32),
        ),
        in_specs=[VMEM, VMEM, SMEM, SMEM, SMEM],
        out_specs=(VMEM,) * 6 + (SMEM,),
        compiler_params=PARAMS,
        name="orbital_table",
    )(irrep_v.reshape(1, width), chol, irrep_i, irrep_l, pos)
    height = chol.shape[1]

    def together():
        return dense(row, col, None, amplitudes, rows, irrep_i, irrep_j, pos)

    def apart():
        own_rows = lax.dynamic_slice_in_dim(irrep_v, pos[0] * height, height)
        keep = (own_rows[:, None] ^ irrep_v[None, :]) == irrep_l[0]

        def step(n, acc):
            panel = jnp.where(keep, jnp.where(n == 0, chol[0], chol[1]), 0.0)
            return dense(row, col, acc, amplitudes, panel, irrep_i, irrep_j, pos)

        return lax.fori_loop(0, 2, step, jnp.zeros_like(amplitudes))

    few = (row, col, order, turn, slots, amplitudes, irrep_i, irrep_j, irrep_l, pos)
    paired = ((half_paired_kernel, ladder_paired_kernel), 64 + 2 * RANKS, RANKS)
    general = ((half_kernel, ladder_kernel), 128, 2 * RANKS)
    return lax.switch(
        branch[0],
        [
            lambda: compact(*paired, TIGHT, *few),
            lambda: compact(*general, TIGHT, *few),
            lambda: compact(*general, SLOTS, *few),
            together,
            apart,
        ],
    )


def solution(mesh):
    in_specs = (P(None, "ja", "aa", None), P(None, "ja", None), P(), P(), P(), P())
    out_specs = P(None, "ja", "aa", None)
    return jax.shard_map(local, mesh=mesh, in_specs=in_specs, out_specs=out_specs, check_vma=False)
```

```python
import functools

import jax
import jax.numpy as jnp
from jax import lax
from jax.experimental import pallas as pl
from jax.experimental.pallas import tpu as pltpu
from jax.sharding import PartitionSpec as P

F32, BF16, I32 = jnp.float32, jnp.bfloat16, jnp.int32
NN = (((1,), (0,)), ((), ()))
NT = (((1,), (1,)), ((), ()))
SLOTS = 32
TIGHT = 24
RANKS = 16
CLS, NUM, SLOT, SPOT, LAB, RANK, BRANCH, BITS = range(8)


def iota(shape, dim):
    return lax.broadcasted_iota(I32, shape, dim)


def parity(x):
    return (x ^ (x >> 1) ^ (x >> 2)) & 1


def one(cond):
    return jnp.where(cond, 1.0, 0.0).astype(F32)


def dot(a, b, dims=NN):
    return lax.dot_general(a, b, dims, preferred_element_type=F32)


def split(x):
    high = x.astype(BF16)
    return high, (x - high.astype(F32)).astype(BF16)


def dot3(a, b, dims=NN):
    (ah, al), (bh, bl) = a, b
    return dot(ah, bh, dims) + dot(ah, bl, dims) + dot(al, bh, dims)


def dot2(a, b, dims=NN):
    return dot(a, b[0], dims) + dot(a, b[1], dims)


def table_kernel(irrep_ref, chol_ref, i_ref, l_ref, pos_ref, row_ref, col_ref, order_ref, turn_ref, out_ref, rows_ref, branch_ref):
    cls = irrep_ref[...]
    width = cls.shape[1]
    chunks = width // 128
    onehot = one(cls == iota((16, width), 0))
    before = one(iota((128, 128), 0) < iota((128, 128), 1))
    count = jnp.zeros((16, 1), F32)
    blocks = jnp.zeros((16, 128), F32)
    slots = []
    for k in range(chunks):
        part = onehot[:, 128 * k : 128 * k + 128]
        ahead = dot(part.astype(BF16), before.astype(BF16)) + count
        slots.append(jnp.sum(part * ahead, axis=0, keepdims=True))
        count = count + jnp.sum(part, axis=1, keepdims=True)
        place = one(iota((128, 128), 1) == 2 * k + (iota((128, 128), 0) >> 6))
        blocks = blocks + dot(part.astype(BF16), place.astype(BF16))
    slot = jnp.concatenate(slots, axis=1).astype(I32)
    lane = iota((16, 128), 1)
    cand = iota((16, 128), 0)
    count_lane = jnp.sum(jnp.where(lane == cand, count, 0.0), axis=0, keepdims=True)
    member = (parity((cand >> 1) & lane) == (cand & 1)) & (lane < 8)
    largest = jnp.max(jnp.where(member, count_lane, 0.0), axis=1, keepdims=True)
    in_block = jnp.zeros((16, 128), F32)
    for g in range(8):
        in_block = in_block + jnp.where(parity((cand >> 1) & g) == (cand & 1), blocks[g : g + 1, :], 0.0)
    fullest = jnp.max(in_block, axis=1, keepdims=True)
    bits_col = cand[:, 0:1] >> 1
    good = (largest <= SLOTS) & (fullest <= RANKS)
    for n in range(l_ref.shape[0]):
        good = good & (parity(bits_col & l_ref[n]) == 1)
    paired = parity(bits_col & (i_ref[0] ^ i_ref[1])) == 1
    rank = cand[:, 0:1] + jnp.where(largest <= TIGHT, jnp.where(paired, 0, 16), 32)
    pick = jnp.min(jnp.where(good, rank.astype(F32), 99.0), axis=0, keepdims=True).astype(I32)
    branch = jnp.where(pick < 48, pick >> 4, jnp.where(l_ref[0] != l_ref[1], 3, 4))
    bits, side = (pick & 15) >> 1, pick & 1
    small = parity(bits & cls) == side
    group = jnp.zeros_like(cls)
    label = jnp.zeros_like(cls)
    lane_group = iota((1, width), 1) >> 5
    number = jnp.zeros((1, 1), I32)
    for g in range(8):
        is_small = parity(bits & g) == side
        group = group + jnp.where(is_small & (cls > g), 1, 0)
        label = label + jnp.where(is_small & (number == lane_group), g, 0)
        number = number + jnp.where(is_small, 1, 0)
    inner = one((iota((128, 128), 0) < iota((128, 128), 1)) & ((iota((128, 128), 0) >> 6) == (iota((128, 128), 1) >> 6)))
    small16 = jnp.broadcast_to(one(small), (16, width))
    ranks = [
        dot(small16[:, 128 * k : 128 * k + 128].astype(BF16), inner.astype(BF16))[0:1, :] for k in range(chunks)
    ]
    rank = jnp.concatenate(ranks, axis=1).astype(I32)
    none = jnp.full_like(cls, -1)
    table = jnp.concatenate(
        [
            cls,
            jnp.where(small, group * SLOTS + slot, none),
            jnp.where(small, slot, none),
            jnp.where(small, (iota((1, width), 1) >> 6) * RANKS + rank, none),
            label,
            jnp.where(small, rank, none),
            jnp.broadcast_to(branch, cls.shape),
            jnp.broadcast_to(bits, cls.shape),
        ],
        axis=0,
    )
    row_ref[...] = table
    branch_ref[0] = jnp.max(branch.astype(F32)).astype(I32)
    table = table.astype(F32)
    for k in range(chunks):
        tile = jnp.concatenate([table[:, 128 * k : 128 * k + 128], jnp.zeros((120, 128), F32)], axis=0)
        col_ref[128 * k : 128 * k + 128, :] = jnp.transpose(tile).astype(I32)
    spots, numbers = places(row_ref)
    order_ref[...] = dot(spots, numbers, NT).astype(BF16)
    turn_ref[...] = dot(numbers, spots, NT).astype(BF16)
    panel_slots(row_ref, col_ref, chol_ref, l_ref, pos_ref, out_ref, rows_ref)


def own(col_ref, block, field):
    return col_ref[pl.ds(pl.multiple_of(block * 64, 64), 64), field : field + 1]


def panel_slots(row_ref, col_ref, chol_ref, l_ref, pos_ref, out_ref, rows_ref):
    cls = row_ref[CLS : CLS + 1, :]
    slot = row_ref[SLOT : SLOT + 1, :]
    own_cls = own(col_ref, pos_ref[0], CLS)
    pick = one(slot == iota((SLOTS, slot.shape[1]), 0)).astype(BF16)
    parts = []
    kept_all = [jnp.where((own_cls ^ cls) == l_ref[n], chol_ref[n], 0.0) for n in range(2)]
    rows_ref[...] = kept_all[0] + kept_all[1]
    for kept in kept_all:
        high, low = split(kept)
        parts.append(dot(high, pick, NT) + dot(low, pick, NT))
    both = jnp.concatenate(parts, axis=1)
    packed = jnp.concatenate([both[0:32], both[32:64]], axis=1)
    out_ref[...] = jnp.broadcast_to(packed[None], out_ref.shape)


def unpack(gathered):
    n = gathered.shape[0]
    return jnp.concatenate([gathered, jnp.roll(gathered, 64, axis=2)], axis=1).reshape(n * 64, 128)


def places(row_ref):
    spot = row_ref[SPOT : SPOT + 1, :]
    number = row_ref[NUM : NUM + 1, :]
    width = spot.shape[1]
    spots = one(spot == iota((16 * RANKS, width), 0)).astype(BF16)
    numbers = one(number == iota((4 * SLOTS, width), 0)).astype(BF16)
    return spots, numbers


def finish(left, full, out_ref, left_ref):
    left_ref[...] = left

    @pl.loop(0, 2)
    def _(i):
        rows = pl.ds(pl.multiple_of(256 * i, 256), 256)
        picks = 8 * SLOTS
        high, low = split(left_ref[rows, :])
        result = dot(high, full[0]) + dot(high[:, 0:picks], full[1][0:picks]) + dot(low, full[0])
        out_ref[i] = result.reshape(4, 64, full[0].shape[1])


def ladder_kernel(
    count, row_ref, col_ref, order_ref, got_ref, mid_ref, i_ref, j_ref, l_ref, pos_ref, out_ref, left_ref
):
    p, q = pos_ref[0], pos_ref[1]
    cls = row_ref[CLS : CLS + 1, :]
    number = row_ref[NUM : NUM + 1, :]
    label = row_ref[LAB : LAB + 1, 0:128]
    bits = row_ref[BITS : BITS + 1, 0:1]
    label_col = col_ref[0:128, LAB : LAB + 1]
    width = cls.shape[1]
    turned = jnp.transpose(unpack(got_ref[...]))
    full = [
        jnp.where(label_col == (cls ^ l_ref[n]), jnp.concatenate([turned[32 * n : 32 * n + 32]] * 4, axis=0), 0.0)
        for n in range(2)
    ]
    full = split(jnp.concatenate(full + [one(number == iota((128, width), 0))], axis=0))
    rows, lates = receive(mid_ref, 128, 2 * RANKS, count)
    mids = [rows[:, 64 * i : 64 * i + 64].reshape(width, 128) for i in range(2)]
    core = dot3(full, split(jnp.concatenate(mids, axis=1)))
    order = order_ref[...]
    own_panel = unpack(got_ref[pl.ds(q, 1)])
    own_slot = own(col_ref, q, SLOT)
    own_rank = own(col_ref, q, RANK)
    own_cls = jnp.concatenate([own(col_ref, q, CLS)] * 4, axis=0)
    lane = iota((64, 128), 1)
    first_tile = jnp.concatenate([own_panel[:, 0:32]] * 4, axis=1)
    second_tile = jnp.concatenate([own_panel[:, 32:64]] * 4, axis=1)
    slot_tile = one(own_slot == (lane & 31))
    rank_pick = one(own_rank == lane).astype(BF16)
    lane_row = iota((1, 128), 1) >> 5
    results = []
    for i in range(2):
        xs = [i_ref[i] ^ j_ref[p * 4 + j] for j in range(4)]
        x_lane = jnp.zeros((1, 128), I32)
        x_row = jnp.zeros((256, 1), I32)
        for j in range(4):
            x_lane = jnp.where(lane_row == j, xs[j], x_lane)
            x_row = jnp.where((iota((256, 1), 0) >> 6) == j, xs[j], x_row)
        odd_lane = parity(x_lane & bits) == 1
        odd = [parity(bits & xs[j]) == 1 for j in range(4)]

        def blocks(tiles):
            return split(
                jnp.concatenate([jnp.where((lane >> 5) == j, tiles[j], 0.0) for j in range(4)], axis=0)
            )

        late = lates[:, RANKS * i : RANKS * (i + 1)]
        total = jnp.where(odd_lane, 0.0, jnp.sum(late, axis=0))
        late = jnp.where(odd_lane, late.reshape(16 * RANKS, 128), 0.0)
        lanes = slice(128 * i, 128 * i + 128)
        pick = core[256:384, lanes]
        pick2 = jnp.where(odd_lane, dot2(order, split(late)), pick)
        t1 = dot3(blocks([jnp.where(odd[j], slot_tile, first_tile) for j in range(4)]), split(pick), NT)
        t2 = dot3(blocks([jnp.where(odd[j], slot_tile, second_tile) for j in range(4)]), split(pick2), NT)
        t3 = dot3(blocks([first_tile] * 4), split(core[0:128, lanes]), NT)
        t3 = t3 + dot3(blocks([second_tile] * 4), split(core[128:256, lanes]), NT)
        total = jnp.concatenate([total, jnp.zeros((128 - RANKS, 128), F32)], axis=0)
        total = dot2(rank_pick, split(total))
        spread = [jnp.concatenate([total[:, 32 * j : 32 * j + 32]] * 4, axis=1) for j in range(4)]
        t3 = t3 + jnp.concatenate(spread, axis=0)
        goal = own_cls ^ x_row
        t1 = jnp.where(label == (goal ^ l_ref[0]), t1, 0.0)
        t2 = jnp.where(label == (goal ^ l_ref[1]), t2, 0.0)
        t3 = jnp.where(label == goal, t3, 0.0)
        results.append(jnp.concatenate([t1, t2, t3], axis=1))
    finish(jnp.concatenate(results, axis=0), full, out_ref, left_ref)


def sent_rows(same, own_rows, count):
    return same + own_rows if count == SLOTS else -(-(same + own_rows) * count // SLOTS // 8) * 8


def send(out_ref, same, different, count):
    rows, late = same.shape[0], different.shape[1]
    if count == SLOTS:
        out_ref[:, 0:rows, :] = jnp.broadcast_to(same[None], (16, rows, 128))
        out_ref[:, rows : rows + late, :] = different
        return
    total = out_ref.shape[1]
    same = jnp.concatenate([same[:, 32 * j : 32 * j + count] for j in range(4)], axis=1)
    different = jnp.concatenate([different[:, :, 32 * j : 32 * j + count] for j in range(4)], axis=2)
    rest = rows - total
    side = [same[total:, 32 * k : 32 * k + 32] for k in range(3)] + [jnp.zeros((total - 3 * rest, 32), F32)]
    main = jnp.concatenate([same[0:total], jnp.concatenate(side, axis=0)], axis=1)
    out_ref[...] = jnp.broadcast_to(main[None], out_ref.shape)
    for k in range(3):
        start = 3 * rest + late * k
        out_ref[:, start : start + late, 96:128] = different[:, :, 32 * k : 32 * k + 32]


def receive(mid_ref, rows, late, count):
    if count == SLOTS:
        return mid_ref[:, 0:rows, :], mid_ref[:, rows : rows + late, :]
    total = mid_ref.shape[1]
    rest = rows - total

    def side(start, size):
        parts = [mid_ref[:, start + size * k : start + size * (k + 1), 96:128] for k in range(3)]
        return jnp.concatenate(parts, axis=2)

    def widen(x):
        gap = jnp.zeros((*x.shape[:2], 32 - count), F32)
        parts = []
        for j in range(4):
            parts += [x[:, :, count * j : count * j + count], gap]
        return jnp.concatenate(parts, axis=2)

    same = jnp.concatenate([mid_ref[:, :, 0:96], side(0, rest)], axis=1)
    return widen(same), widen(side(3 * rest, late))


def half_products(row_ref, col_ref, amp_ref, got_ref, i_ref, j_ref, pos_ref, half_ref):
    p, q = pos_ref[0], pos_ref[1]
    cls = row_ref[CLS : CLS + 1, :]
    own_cls = own(col_ref, q, CLS)
    panel = unpack(got_ref[...])
    lane = iota(panel.shape, 1)
    slot = col_ref[:, SLOT : SLOT + 1]
    wh, wl = split(jnp.where(lane < 64, panel, one(slot == lane - 64)))
    both = jnp.concatenate([wh, wl], axis=1)
    pair_cls = own_cls ^ cls

    @pl.loop(0, 2, unroll=True)
    def _(i):
        kept = [jnp.where(pair_cls == (i_ref[i] ^ j_ref[p * 4 + j]), amp_ref[i, j], 0.0) for j in range(4)]
        high, low = split(jnp.concatenate(kept, axis=0))
        first = dot(high, both)
        rows = pl.ds(pl.multiple_of(256 * i, 256), 256)
        half_ref[rows, :] = first[:, 0:128] + first[:, 128:256] + dot(low, wh)

    return [half_ref[64 * n : 64 * n + 64, :] for n in range(8)]


def left_factor(col_ref, got_ref, q):
    own_rank = own(col_ref, q, RANK)
    own_panel = unpack(got_ref[pl.ds(q, 1)])
    stacked = jnp.concatenate([own_panel[:, 0:32], own_panel[:, 32:64]], axis=0)
    ranks = jnp.concatenate([jnp.full_like(own_rank, -1), own_rank], axis=0)
    lane = iota((128, 128), 1)
    left = jnp.where(lane < 32, jnp.concatenate([stacked] * 4, axis=1), one(ranks == lane - 32))
    return jnp.transpose(jnp.where(lane < 48, left, 0.0))


def odd_even(row_ref, i_ref, j_ref, p):
    bits = row_ref[BITS : BITS + 1, 0:1]
    later = [parity(bits & (i_ref[1] ^ j_ref[p * 4 + j])) == 1 for j in range(4)]
    xs = [[jnp.where(later[j], i_ref[i] ^ j_ref[p * 4 + j], i_ref[1 - i] ^ j_ref[p * 4 + j]) for j in range(4)] for i in (1, 0)]
    return later, xs[0], xs[1]


def half_kernel(
    count, row_ref, col_ref, order_ref, amp_ref, got_ref, i_ref, j_ref, l_ref, pos_ref, out_ref, half_ref
):
    p, q = pos_ref[0], pos_ref[1]
    label = row_ref[LAB : LAB + 1, 0:128]
    own_cls = own(col_ref, q, CLS)
    own_small = own(col_ref, q, NUM) >= 0
    xs = [i_ref[n // 4] ^ j_ref[p * 4 + n % 4] for n in range(8)]
    parts = half_products(row_ref, col_ref, amp_ref, got_ref, i_ref, j_ref, pos_ref, half_ref)
    firsts = [part[:, 64:96] + jnp.where(own_small, part[:, 0:32], 0.0) for part in parts]
    left = left_factor(col_ref, got_ref, q)
    pair_cls = jnp.concatenate([own_cls ^ l_ref[0], own_cls ^ l_ref[1]], axis=0)
    both = [jnp.concatenate([part[:, 0:32], part[:, 32:64]], axis=0) for part in parts]
    spread = [
        jnp.where(label == (pair_cls ^ xs[n]), jnp.concatenate([both[n]] * 4, axis=1), 0.0) for n in range(8)
    ]
    sums = dot3(split(left[0:32]), split(jnp.concatenate(spread, axis=1)))
    seconds = dot2(left[32:48].astype(BF16), split(jnp.concatenate(both, axis=1)))
    order = order_ref[...]
    mains, lates = [], []
    for i in range(2):
        rows = jnp.concatenate([sums[:, 128 * n : 128 * n + 128] for n in range(4 * i, 4 * i + 4)], axis=0)
        by_spot = dot2(order, split(rows), NT).reshape(16, RANKS, 128)
        lates.append(by_spot + seconds[None, :, 128 * i : 128 * i + 128])
        mains.append(jnp.concatenate(firsts[4 * i : 4 * i + 4], axis=1))
    send(out_ref, jnp.concatenate(mains, axis=0), jnp.concatenate(lates, axis=1), count)


def half_paired_kernel(
    count, row_ref, col_ref, order_ref, amp_ref, got_ref, i_ref, j_ref, l_ref, pos_ref, out_ref, half_ref
):
    p, q = pos_ref[0], pos_ref[1]
    label = row_ref[LAB : LAB + 1, 0:128]
    own_cls = own(col_ref, q, CLS)
    own_small = own(col_ref, q, NUM) >= 0
    parts = half_products(row_ref, col_ref, amp_ref, got_ref, i_ref, j_ref, pos_ref, half_ref)
    later, _, even_x = odd_even(row_ref, i_ref, j_ref, p)
    odd = [jnp.where(later[j], parts[4 + j], parts[j]) for j in range(4)]
    even = [jnp.where(later[j], parts[j], parts[4 + j]) for j in range(4)]
    rows = jnp.concatenate([part[:, 64:96] + jnp.where(own_small, part[:, 0:32], 0.0) for part in odd], axis=1)
    left = left_factor(col_ref, got_ref, q)
    firsts = jnp.concatenate([part[:, 64:96] for part in even], axis=1)
    seconds = jnp.concatenate([part[:, 32:64] for part in odd], axis=1)
    few = jnp.concatenate([firsts, seconds], axis=1)
    few = dot2(left[32:48].astype(BF16), split(jnp.concatenate([few, few], axis=0)))
    pair_cls = jnp.concatenate([own_cls ^ l_ref[0], own_cls ^ l_ref[1]], axis=0)
    spread = []
    for j in range(4):
        both = jnp.concatenate([even[j][:, 0:32], even[j][:, 32:64]], axis=0)
        spread.append(jnp.where(label == (pair_cls ^ even_x[j]), jnp.concatenate([both] * 4, axis=1), 0.0))
    sums = dot3(split(left[0:32]), split(jnp.concatenate(spread, axis=1)))
    sums = jnp.concatenate([sums[:, 128 * j : 128 * j + 128] for j in range(4)], axis=0)
    order = order_ref[...]
    rows = jnp.concatenate([rows, few[:, 0:128], few[:, 128:256]], axis=0)
    send(out_ref, rows, dot2(order, split(sums), NT).reshape(16, RANKS, 128), count)


def ladder_paired_kernel(
    count, row_ref, col_ref, order_ref, got_ref, mid_ref, i_ref, j_ref, l_ref, pos_ref, out_ref, left_ref
):
    p, q = pos_ref[0], pos_ref[1]
    cls = row_ref[CLS : CLS + 1, :]
    number = row_ref[NUM : NUM + 1, :]
    label = row_ref[LAB : LAB + 1, 0:128]
    label_col = col_ref[0:128, LAB : LAB + 1]
    width = cls.shape[1]
    turned = jnp.transpose(unpack(got_ref[...]))
    full = [
        jnp.where(label_col == (cls ^ l_ref[n]), jnp.concatenate([turned[32 * n : 32 * n + 32]] * 4, axis=0), 0.0)
        for n in range(2)
    ]
    full = split(jnp.concatenate(full + [one(number == iota((128, width), 0))], axis=0))
    rows, sums = receive(mid_ref, 64 + 2 * RANKS, RANKS, count)
    core = dot3(full, split(rows[:, 0:64].reshape(width, 128)))
    order = order_ref[...]
    few = [rows[:, 64 + RANKS * k : 64 + RANKS * (k + 1)].reshape(16 * RANKS, 128) for k in range(2)]
    small_rows, second_rows = [dot2(order, split(few[k])) for k in range(2)]
    total = jnp.concatenate([jnp.sum(sums, axis=0), jnp.zeros((128 - RANKS, 128), F32)], axis=0)
    own_panel = unpack(got_ref[pl.ds(q, 1)])
    own_slot = own(col_ref, q, SLOT)
    own_rank = own(col_ref, q, RANK)
    own_cls = own(col_ref, q, CLS)
    lane = iota((64, 128), 1)

    def blocks(tile):
        return split(jnp.concatenate([jnp.where((lane >> 5) == j, tile, 0.0) for j in range(4)], axis=0))

    first = blocks(jnp.concatenate([own_panel[:, 0:32]] * 4, axis=1))
    second = blocks(jnp.concatenate([own_panel[:, 32:64]] * 4, axis=1))
    slots = blocks(one(own_slot == (lane & 31)))[0]
    total = dot2(one(own_rank == lane).astype(BF16), split(total))
    total = [jnp.concatenate([total[:, 32 * j : 32 * j + 32]] * 4, axis=1) for j in range(4)]
    odd = [
        dot2(slots, split(core[256:384]), NT),
        dot2(slots, split(second_rows), NT),
        dot3(first, split(core[0:128]), NT) + dot3(second, split(core[128:256]), NT),
    ]
    small_rows = split(small_rows)
    even = [dot3(first, small_rows, NT), dot3(second, small_rows, NT), jnp.concatenate(total, axis=0)]
    later, odd_x, even_x = odd_even(row_ref, i_ref, j_ref, p)
    rows = [None] * 8
    for j in range(4):
        kinds = []
        for parts, x in ((odd, odd_x[j]), (even, even_x[j])):
            goal = own_cls ^ x
            labels = (goal ^ l_ref[0], goal ^ l_ref[1], goal)
            kinds.append(
                jnp.concatenate(
                    [jnp.where(label == labels[k], parts[k][64 * j : 64 * j + 64], 0.0) for k in range(3)], axis=1
                )
            )
        rows[j] = jnp.where(later[j], kinds[1], kinds[0])
        rows[4 + j] = jnp.where(later[j], kinds[0], kinds[1])
    finish(jnp.concatenate(rows, axis=0), full, out_ref, left_ref)


VMEM = pl.BlockSpec(memory_space=pltpu.VMEM)
SMEM = pl.BlockSpec(memory_space=pltpu.SMEM)
PARAMS = pltpu.CompilerParams(vmem_limit_bytes=48 * 1024 * 1024)


def shape(*dims, dtype=F32):
    return jax.ShapeDtypeStruct(dims, dtype)


def compact(kernels, same, late, count, row, col, order, turn, panel, amplitudes, irrep_i, irrep_j, irrep_l, pos):
    panel = lax.all_to_all(panel, "ja", split_axis=0, concat_axis=0, tiled=True)
    mid = pl.pallas_call(
        functools.partial(kernels[0], count),
        out_shape=shape(16, sent_rows(same, late, count), 128),
        in_specs=[VMEM] * 5 + [SMEM] * 4,
        out_specs=VMEM,
        scratch_shapes=[pltpu.VMEM((512, 128), F32)],
        compiler_params=PARAMS,
        name="half_slots",
    )(row, col, order, amplitudes, panel, irrep_i, irrep_j, irrep_l, pos)
    mid = lax.all_to_all(mid, "aa", split_axis=0, concat_axis=0, tiled=True)
    return pl.pallas_call(
        functools.partial(kernels[1], count),
        out_shape=shape(*amplitudes.shape),
        in_specs=[VMEM] * 5 + [SMEM] * 4,
        out_specs=VMEM,
        scratch_shapes=[pltpu.VMEM((512, 12 * SLOTS), F32)],
        compiler_params=PARAMS,
        name="ladder_slots",
    )(row, col, turn, panel, mid, irrep_i, irrep_j, irrep_l, pos)


def panel_rows(half_ref, other_ref, core, high_ref, low_ref):
    @pl.loop(0, half_ref.shape[0])
    def _(k):
        for part, ref in ((core, half_ref), (1 - core, other_ref)):
            rows = pl.ds(pl.multiple_of((2 * k + part) * 64, 64), 64)
            high_ref[rows, :], low_ref[rows, :] = split(ref[k])


def dense_half_kernel(
    row_ref, col_ref, amp_ref, half_ref, other_ref, i_ref, j_ref, pos_ref, out_ref, ph_ref, pl_ref, high_ref, low_ref
):
    p, q = pos_ref[0], pos_ref[1]
    panel_rows(half_ref, other_ref, p & 1, ph_ref, pl_ref)
    pair_cls = own(col_ref, q, CLS) ^ row_ref[CLS : CLS + 1, :]

    @pl.loop(0, 8)
    def _(n):
        i, j = n >> 2, n & 3
        kept = jnp.where(pair_cls == (i_ref[i] ^ j_ref[p * 4 + j]), amp_ref[i, j], 0.0)
        rows = pl.ds(pl.multiple_of(64 * n, 64), 64)
        high_ref[rows, :], low_ref[rows, :] = split(kept)

    @pl.loop(0, 2)
    def _(k):
        rows = pl.ds(pl.multiple_of(512 * k, 512), 512)
        result = dot3((ph_ref[rows, :], pl_ref[rows, :]), (high_ref[...], low_ref[...]), NT)
        out_ref[pl.ds(8 * k, 8)] = result.reshape(8, 64, 512)


def dense_ladder_kernel(row_ref, col_ref, mid_ref, half_ref, other_ref, i_ref, j_ref, pos_ref, *refs):
    p, q = pos_ref[0], pos_ref[1]
    acc_ref = refs[0] if len(refs) == 6 else None
    out_ref, ph_ref, pl_ref, high_ref, low_ref = refs[-5:]
    panel_rows(half_ref, other_ref, p & 1, ph_ref, pl_ref)
    first = iota((64, 128), 1) < 64

    @pl.loop(0, 4)
    def _(k):
        lanes = pl.ds(pl.multiple_of(128 * k, 128), 128)
        pairs = [(mid_ref[s, :, lanes], mid_ref[s + 1, :, lanes]) for s in range(0, 16, 2)]
        left = [jnp.where(first, a, jnp.roll(b, 64, axis=1)) for a, b in pairs]
        right = [jnp.where(first, jnp.roll(a, 64, axis=1), b) for a, b in pairs]
        rows = pl.ds(pl.multiple_of(128 * k, 128), 128)
        whole = jnp.concatenate([jnp.concatenate(left, axis=1), jnp.concatenate(right, axis=1)], axis=0)
        high_ref[rows, :], low_ref[rows, :] = split(whole)

    pair_cls = own(col_ref, q, CLS) ^ row_ref[CLS : CLS + 1, :]

    @pl.loop(0, 2)
    def _(i):
        rows = pl.ds(pl.multiple_of(256 * i, 256), 256)
        result = dot3((high_ref[rows, :], low_ref[rows, :]), (ph_ref[...], pl_ref[...]))
        for j in range(4):
            x = i_ref[i] ^ j_ref[p * 4 + j]
            kept = jnp.where(pair_cls == x, result[64 * j : 64 * j + 64], 0.0)
            out_ref[i, j] = kept if acc_ref is None else acc_ref[i, j] + kept


CORES = [[2 * k + core for k in range(8)] for core in (0, 1)]


def dense(row, col, acc, amplitudes, panel, irrep_i, irrep_j, pos):
    half = jnp.broadcast_to(panel[None], (8, *panel.shape))
    half = lax.all_to_all(half, "ja", split_axis=0, concat_axis=0, tiled=True, axis_index_groups=CORES)
    other = lax.ppermute(half, "ja", [(n, n ^ 1) for n in range(16)])
    halves = [pltpu.VMEM((1024, 1024), BF16)] * 2 + [pltpu.VMEM((512, 1024), BF16)] * 2
    mid = pl.pallas_call(
        dense_half_kernel,
        out_shape=shape(16, 64, 512),
        in_specs=[VMEM] * 5 + [SMEM] * 3,
        out_specs=VMEM,
        scratch_shapes=halves,
        compiler_params=PARAMS,
        name="half_dense",
    )(row, col, amplitudes, half, other, irrep_i, irrep_j, pos)
    mid = lax.all_to_all(mid, "aa", split_axis=0, concat_axis=0, tiled=True)
    so_far = [] if acc is None else [acc]
    return pl.pallas_call(
        dense_ladder_kernel,
        out_shape=shape(*amplitudes.shape),
        in_specs=[VMEM] * 5 + [SMEM] * 3 + [VMEM] * len(so_far),
        out_specs=VMEM,
        scratch_shapes=halves,
        input_output_aliases={8: 0} if so_far else {},
        compiler_params=PARAMS,
        name="ladder_dense",
    )(row, col, mid, half, other, irrep_i, irrep_j, pos, *so_far)


def local(amplitudes, chol, irrep_i, irrep_j, irrep_v, irrep_l):
    pos = jnp.stack([lax.axis_index("ja"), lax.axis_index("aa")]).astype(I32)
    width = irrep_v.shape[0]
    row, col, order, turn, slots, rows, branch = pl.pallas_call(
        table_kernel,
        out_shape=(
            shape(8, width, dtype=I32),
            shape(width, 128, dtype=I32),
            shape(16 * RANKS, 4 * SLOTS, dtype=BF16),
            shape(4 * SLOTS, 16 * RANKS, dtype=BF16),
            shape(16, 32, 128),
            shape(chol.shape[1], width),
            shape(1, dtype=I32),
        ),
        in_specs=[VMEM, VMEM, SMEM, SMEM, SMEM],
        out_specs=(VMEM,) * 6 + (SMEM,),
        compiler_params=PARAMS,
        name="orbital_table",
    )(irrep_v.reshape(1, width), chol, irrep_i, irrep_l, pos)
    height = chol.shape[1]

    def together():
        return dense(row, col, None, amplitudes, rows, irrep_i, irrep_j, pos)

    def apart():
        own_rows = lax.dynamic_slice_in_dim(irrep_v, pos[0] * height, height)
        keep = (own_rows[:, None] ^ irrep_v[None, :]) == irrep_l[0]

        def step(n, acc):
            panel = jnp.where(keep, jnp.where(n == 0, chol[0], chol[1]), 0.0)
            return dense(row, col, acc, amplitudes, panel, irrep_i, irrep_j, pos)

        return lax.fori_loop(0, 2, step, jnp.zeros_like(amplitudes))

    few = (row, col, order, turn, slots, amplitudes, irrep_i, irrep_j, irrep_l, pos)
    paired = ((half_paired_kernel, ladder_paired_kernel), 64 + 2 * RANKS, RANKS)
    general = ((half_kernel, ladder_kernel), 128, 2 * RANKS)
    return lax.switch(
        branch[0],
        [
            lambda: compact(*paired, TIGHT, *few),
            lambda: compact(*general, TIGHT, *few),
            lambda: compact(*general, SLOTS, *few),
            together,
            apart,
        ],
    )


def solution(mesh):
    in_specs = (P(None, "ja", "aa", None), P(None, "ja", None), P(), P(), P(), P())
    out_specs = P(None, "ja", "aa", None)
    return jax.shard_map(local, mesh=mesh, in_specs=in_specs, out_specs=out_specs, check_vma=False)
```
